32 devices in a mesh: dp: 16 (over z, y, core), mp: 2 (over x).
Axes of the slice: x: 2, y: 2, z: 4, core: 2. Of those that a mesh axis runs over, the one named last changes fastest.
Arguments:
- tokens_in: bfloat16 [32768, 768], P(('dp', 'mp')), may hold values from -6 to 6
- seg_lengths: int32 [64, 4], P('dp'), may hold values from 1 to 256, 512 in all within a row
- pad_counts: int32 [64], P('dp'), may hold values from 0 to 64
- w_qkv: bfloat16 [3, 768, 768], P(None, None, 'mp'), may hold values from -0.21875 to 0.21875
- qv_bias: bfloat16 [2, 768], P(None, 'mp'), may hold values from -3 to 3
- w_out: bfloat16 [768, 768], P('mp'), may hold values from -1.5 to 1.5
- out_bias: bfloat16 [768], replicated, may hold values from -3 to 3
- norm1_gain: bfloat16 [768], replicated, may hold values from 0.5 to 1.5
- norm1_bias: bfloat16 [768], replicated, may hold values from -3 to 3
- w_up: bfloat16 [768, 3072], P(None, 'mp'), may hold values from -0.21875 to 0.21875
- up_bias: bfloat16 [3072], P('mp'), may hold values from -3 to 3
- w_down: bfloat16 [3072, 768], P('mp'), may hold values from -0.109375 to 0.109375
- down_bias: bfloat16 [768], replicated, may hold values from -3 to 3
- norm2_gain: bfloat16 [768], replicated, may hold values from 0.5 to 1.5
- norm2_bias: bfloat16 [768], replicated, may hold values from -3 to 3
- cotangent: bfloat16 [32768, 768], P(('dp', 'mp')), may hold values from -6 to 6
Outputs:
- tokens_out: bfloat16 [32768, 768], P(('dp', 'mp'))
- pooled: float32 [64, 768], P(('dp', 'mp'))
- grad_input: bfloat16 [32768, 768], P(('dp', 'mp'))
- grad_qkv: float32 [3, 768, 768], P(None, None, 'mp')
- grad_qv_bias: float32 [2, 768], P(None, 'mp')
- grad_out: float32 [768, 768], P('mp')
- grad_out_bias: float32 [768], replicated
- grad_norm1_gain: float32 [768], replicated
- grad_norm1_bias: float32 [768], replicated
- grad_up: float32 [768, 3072], P(None, 'mp')
- grad_up_bias: float32 [3072], P('mp')
- grad_down: float32 [3072, 768], P('mp')
- grad_down_bias: float32 [768], replicated
- grad_norm2_gain: float32 [768], replicated
- grad_norm2_bias: float32 [768], replicated
The draws below stay inside these ranges and needn't reach their ends.
All inputs are finite; a program needn't handle non-finite values.
Results may differ from the reference program's by a relative error of at most 0.019.
Values may be sent and summed in bfloat16 or wider, within the bound.
No kernel may reach another device: no remote copies, remote signals or barrier semaphores. Data moves between devices by JAX's collectives and lax.ppermute only.
A program may use at most 192 MiB of HBM per device.

```python
import math
import jax
import jax.numpy as jnp
import numpy as np
from jax import lax

D = 768
HEADS = 12
HD = 64
FF = 3072
SEQ = 512
SEGS = 4
ROWS = 64
TOKENS = 32768


def plant(array, rng, low, top_value):
    spot = [jax.random.randint(jax.random.fold_in(rng, axis), (), 0, length) for axis, length in enumerate(array.shape)]
    widest = array.shape.index(max(array.shape))
    neighbour = spot[:widest] + [(spot[widest] + 1) % array.shape[widest]] + spot[widest + 1:]
    return array.at[tuple(spot)].set(low).at[tuple(neighbour)].set(top_value)


def level_of(own_key, dims, cuts, low, top_value):
    level = 1.0
    for axis_at, shards_of in cuts:
        draws = jax.random.uniform(jax.random.fold_in(jax.random.fold_in(own_key, 6), axis_at), (shards_of,), jnp.float32, low / len(cuts), top_value / len(cuts))
        level = level * jnp.repeat(jnp.exp(draws), dims[axis_at] // shards_of).reshape((-1,) + (1,) * (len(dims) - 1 - axis_at))
    return level


def length_profile(count, total, reach, skew):
    loads = [(1 << 20) // math.isqrt(standing ** skew) + 1 for standing in range(2, count + 1)]
    spare, counts = total - reach - (count - 1), [1] * (count - 1)
    while spare > 0:
        free = [i for i in range(count - 1) if counts[i] < reach]
        pool, remaining = sum([loads[i] for i in free]), spare
        for i in free:
            more = min(reach - counts[i], max(1, remaining * loads[i] // pool), spare)
            counts[i] = counts[i] + more
            spare = spare - more
    return np.array([reach] + counts)


def uneven(key, amount, total, reach, lean):
    if amount == 2:
        one = jax.random.randint(key, (), max(1, total - reach), min(reach, total - 1) + 1)
        return jnp.stack([one, total - one])
    sizes = jnp.asarray(length_profile(amount, total, reach, lean), jnp.int32)
    pairs = (amount - 1) // 2
    giver, taker = sizes[1:1 + 2 * pairs:2], sizes[2:2 + 2 * pairs:2]
    room = jnp.minimum(giver - 1, reach - taker)
    moved = jax.random.randint(jax.random.fold_in(key, 1), (pairs,), 0, 1 << 20) % (room + 1)
    sizes = sizes.at[1:1 + 2 * pairs:2].set(giver - moved).at[2:2 + 2 * pairs:2].set(taker + moved)
    return sizes[jax.random.permutation(jax.random.fold_in(key, 2), amount)]


def bell_draw(key, dims, scale, most, cuts=(), kind=jnp.bfloat16):
    values = jax.random.normal(key, dims, jnp.float32) * scale
    if len(cuts) > 0:
        values = level_of(key, dims, cuts, -0.22, 0.18) * values
    return jnp.clip(values, min=-most, max=most).astype(kind)


def setup_inputs(seed: int = 0) -> dict:
    seeds = jax.random.split(jax.random.key(seed), 17)
    tokens_in = bell_draw(seeds[0], (TOKENS, D), 1.0, 6.0, ((0, 32),))
    seg_lengths = jax.vmap(lambda own: uneven(own, SEGS, SEQ, SEQ // 2, 1))(jax.random.split(seeds[1], ROWS)).reshape((ROWS, SEGS)).astype(jnp.int32)
    pad_counts = plant(jax.random.randint(seeds[2], (ROWS,), 0, SEQ // 8 + 1), jax.random.fold_in(seeds[2], 1), 0, (SEQ // 8 + 1) - 1).astype(jnp.int32)
    w_qkv = bell_draw(seeds[3], (3, D, D), D ** -0.5, 0.21875, ((2, 2),))
    qv_bias = bell_draw(seeds[4], (2, D), 0.5, 3.0, ((1, 2),))
    w_out = bell_draw(seeds[5], (D, D), (D // 48) ** -0.5, 1.5, ((0, 2),))
    out_bias = bell_draw(seeds[6], (D,), 0.5, 3.0)
    norm1_gain = jnp.clip(1.0 + 0.1 * jax.random.normal(seeds[7], (D,), jnp.float32), 0.5, 1.5).astype(jnp.bfloat16)
    norm1_bias = bell_draw(seeds[8], (D,), 0.5, 3.0)
    w_up = bell_draw(seeds[9], (D, FF), D ** -0.5, 0.21875, ((1, 2),))
    up_bias = bell_draw(seeds[10], (FF,), 0.5, 3.0, ((0, 2),))
    w_down = bell_draw(seeds[11], (FF, D), FF ** -0.5, 0.109375, ((0, 2),))
    down_bias = bell_draw(seeds[12], (D,), 0.5, 3.0)
    norm2_gain = jnp.clip(1.0 + 0.1 * jax.random.normal(seeds[13], (D,), jnp.float32), 0.5, 1.5).astype(jnp.bfloat16)
    norm2_bias = bell_draw(seeds[14], (D,), 0.5, 3.0)
    cotangent = bell_draw(seeds[15], (TOKENS, D), 1.0, 6.0, ((0, 32),))
    return dict(tokens_in=tokens_in, seg_lengths=seg_lengths, pad_counts=pad_counts, w_qkv=w_qkv, qv_bias=qv_bias, w_out=w_out, out_bias=out_bias, norm1_gain=norm1_gain, norm1_bias=norm1_bias, w_up=w_up, up_bias=up_bias, w_down=w_down, down_bias=down_bias, norm2_gain=norm2_gain, norm2_bias=norm2_bias, cotangent=cotangent)


PRECISE = lax.Precision.HIGHEST
EPSILON = 1e-12
SCORE_SCALE = 0.125
GELU_COEF = 0.7978845608028654

@jax.custom_vjp
def low(v):
    return lax.optimization_barrier(v.astype(jnp.bfloat16)).astype(jnp.float32)

@jax.custom_vjp
def low_back(v):
    return v

def low_keep(v):
    return (low(v), None)

def low_pass(kept, grad):
    return (grad,)

def back_keep(v):
    return (v, None)

def back_low(kept, grad):
    return (low(grad),)
low.defvjp(low_keep, low_pass)
low_back.defvjp(back_keep, back_low)

def layer_norm(hidden, gain_vec, shift_vec):
    centered = hidden - lax.optimization_barrier(jnp.mean(hidden, axis=-1, keepdims=True))
    spread = lax.optimization_barrier(jnp.mean(centered * centered, axis=-1, keepdims=True))
    return centered * lax.rsqrt(spread + EPSILON) * gain_vec + shift_vec

def gelu_tanh(inputs):
    return 0.5 * inputs * (1.0 + jnp.tanh(GELU_COEF * (inputs + 0.044715 * inputs * inputs * inputs)))

def allowed_mask(seg_row, pad_row, seq_len):
    positions = jnp.arange(seq_len, dtype=jnp.int32)
    seg_ends = jnp.cumsum(seg_row).astype(jnp.int32)
    segment = lax.optimization_barrier(jnp.sum((positions[:, None] >= seg_ends[None, :]).astype(jnp.int32), axis=1))
    usable = positions < seq_len - pad_row
    same_doc = segment[:, None] == segment[None, :]
    return same_doc & (usable[None, :] | (positions[:, None] == positions[None, :]))

def row_layer(params, row_in, seg_row, pad_row):
    w_qkv, qv_bias, w_out, out_bias, gain_one, shift_one, w_up, up_bias, w_down, down_bias, gain_two, shift_two = params
    allowed = allowed_mask(seg_row, pad_row, SEQ)
    bias_stack = jnp.stack([qv_bias[0], jnp.zeros_like(qv_bias[0]), qv_bias[1]])
    projected = jnp.einsum('td,cde->cte', row_in, w_qkv, precision=PRECISE) + bias_stack[:, None, :]
    qkv = low(low_back(projected)).reshape(3, SEQ, HEADS, HD)
    scores = low_back(jnp.einsum('qhd,khd->hqk', qkv[0], qkv[1], precision=PRECISE))
    scaled = jnp.where(allowed[None], scores * SCORE_SCALE, -1e+30)
    row_peak = lax.optimization_barrier(jnp.max(scaled, axis=-1, keepdims=True))
    row_exp = jnp.exp(scaled - row_peak)
    row_total = lax.optimization_barrier(jnp.sum(row_exp, axis=-1, keepdims=True))
    probs = low(row_exp / row_total)
    context = low(low_back(jnp.einsum('hqk,khd->qhd', probs, qkv[2], precision=PRECISE))).reshape(SEQ, D)
    attended = low_back(jnp.dot(context, w_out, precision=PRECISE) + out_bias)
    normed = layer_norm(row_in + attended, gain_one, shift_one)
    pre_act = low_back(jnp.dot(low(normed), w_up, precision=PRECISE) + up_bias)
    activated = low(gelu_tanh(pre_act))
    branch = low_back(jnp.dot(activated, w_down, precision=PRECISE) + down_bias)
    final_rows = layer_norm(normed + branch, gain_two, shift_two)
    usable = jnp.arange(SEQ, dtype=jnp.int32) < SEQ - pad_row
    pooled = lax.optimization_barrier(jnp.sum(jnp.where(usable[:, None], final_rows, 0.0), axis=0)) / (SEQ - pad_row).astype(jnp.float32)
    return (final_rows, pooled)

def reference(tokens_in, seg_lengths, pad_counts, w_qkv, qv_bias, w_out, out_bias, norm1_gain, norm1_bias, w_up, up_bias, w_down, down_bias, norm2_gain, norm2_bias, cotangent):
    params = tuple((weight.astype(jnp.float32) for weight in (w_qkv, qv_bias, w_out, out_bias, norm1_gain, norm1_bias, w_up, up_bias, w_down, down_bias, norm2_gain, norm2_bias)))
    inputs = tokens_in.astype(jnp.float32).reshape(ROWS, SEQ, D)

    def forward(inputs, params):

        def one_row(row_items):
            return row_layer(params, row_items[0], row_items[1], row_items[2])
        return lax.map(jax.checkpoint(one_row), (inputs, seg_lengths, pad_counts))
    (final_rows, pooled), pull = jax.vjp(forward, inputs, params)
    grad_in, grads = pull((cotangent.astype(jnp.float32).reshape(ROWS, SEQ, D), jnp.zeros_like(pooled)))
    tokens_out = final_rows.reshape(TOKENS, D).astype(jnp.bfloat16)
    grad_input = grad_in.reshape(TOKENS, D).astype(jnp.bfloat16)
    return (tokens_out, pooled, grad_input, grads[0], grads[1], grads[2], grads[3], grads[4], grads[5], grads[6], grads[7], grads[8], grads[9], grads[10], grads[11])
```

```python
import functools

import jax
import jax.numpy as jnp
from jax import lax
from jax.experimental import pallas as pl
from jax.experimental.pallas import tpu as pltpu
from jax.sharding import PartitionSpec as P

HD = 64
SEQ = 512
PAIR = 128
EPSILON = 1e-12
SCORE_SCALE = 0.125
GELU_COEF = 0.7978845608028654
MASKED = -1e30
F32 = jnp.float32
BF16 = jnp.bfloat16

NT = (((1,), (1,)), ((), ()))
NN = (((1,), (0,)), ((), ()))
TN = (((0,), (0,)), ((), ()))


def dot(a, b, dims=NN):
    return lax.dot_general(a, b, dims, preferred_element_type=F32)


def attn_fwd_kernel(pad_ref, q_ref, k_ref, v_ref, qa_ref, ka_ref, ctx_ref, e_ref, rinv_ref):
    limit = SEQ - pad_ref[pl.program_id(0)]
    q, k = q_ref[0], k_ref[0]
    v_t = v_ref[0].astype(F32).T.astype(BF16)
    low = lax.broadcasted_iota(jnp.int32, (SEQ, PAIR), 1) < HD
    parts = []
    for h in range(2):
        own = low if h == 0 else ~low
        q_h = jnp.where(own, q, qa_ref[0])
        k_h = jnp.where(own, k, ka_ref[0])
        s = dot(k_h, q_h, NT)
        j = lax.broadcasted_iota(jnp.int32, (64, SEQ), 0) + (SEQ - 64)
        i = lax.broadcasted_iota(jnp.int32, (64, SEQ), 1)
        tail = jnp.where((j < limit) | (j == i), s[SEQ - 64 :], MASKED)
        s = jnp.concatenate([s[: SEQ - 64], tail], axis=0)
        peak = jnp.max(s, axis=0, keepdims=True)
        e = jnp.exp((s - peak) * SCORE_SCALE)
        rinv = 1.0 / jnp.sum(e, axis=0, keepdims=True)
        eb = e.astype(BF16)
        e_ref[h] = eb
        rinv_ref[0, 0, h : h + 1, :] = rinv
        parts.append(dot(v_t[h * HD : (h + 1) * HD], eb) * rinv)
    ctx_ref[...] = jnp.concatenate(parts, axis=0).T.astype(BF16)


def attn_fwd(qkv, pads, q_aug, k_aug):
    rows, pairs = pads.shape[0], qkv.shape[2] // PAIR
    width = qkv.shape[2]
    take = lambda c: pl.BlockSpec((1, SEQ, PAIR), lambda r, p, *_: (c, r, p))
    aug = pl.BlockSpec((1, SEQ, PAIR), lambda r, p, *_: (r, 0, 0))
    return pl.pallas_call(
        attn_fwd_kernel,
        grid_spec=pltpu.PrefetchScalarGridSpec(
            num_scalar_prefetch=1,
            grid=(rows, pairs),
            in_specs=[take(0), take(1), take(2), aug, aug],
            out_specs=[
                pl.BlockSpec((SEQ, PAIR), lambda r, p, *_: (r, p)),
                pl.BlockSpec((2, SEQ, SEQ), lambda r, p, *_: (r * pairs + p, 0, 0)),
                pl.BlockSpec((1, 1, 2, SEQ), lambda r, p, *_: (r, p, 0, 0)),
            ],
        ),
        out_shape=[
            jax.ShapeDtypeStruct((rows * SEQ, width), BF16),
            jax.ShapeDtypeStruct((rows * pairs * 2, SEQ, SEQ), BF16),
            jax.ShapeDtypeStruct((rows, pairs, 2, SEQ), F32),
        ],
        cost_estimate=pl.CostEstimate(
            flops=rows * pairs * 2 * 4 * SEQ * SEQ * PAIR * 2,
            bytes_accessed=rows * pairs * 2 * SEQ * SEQ * 2,
            transcendentals=rows * pairs * 2 * SEQ * SEQ,
        ),
        name="attn_fwd",
    )(pads, qkv, qkv, qkv, q_aug, k_aug)


def attn_bwd_kernel(q_ref, k_ref, v_ref, ctx_ref, dctx_ref, e_ref, rinv_ref, out_ref):
    q, k = q_ref[0], k_ref[0]
    v = v_ref[0]
    k_t = k.astype(F32).T.astype(BF16)
    d_t = dctx_ref[...].astype(F32).T
    c_t = ctx_ref[...].astype(F32).T
    lane = lax.broadcasted_iota(jnp.int32, (SEQ, PAIR), 1)
    row8 = lax.broadcasted_iota(jnp.int32, (8, SEQ), 0)
    low = lane < HD
    ones = jnp.where((lane & (HD - 1)) < 2, 1.0, 0.0).astype(BF16)
    dv, dk, dq = [], [], []
    for h in range(2):
        own = low if h == 0 else ~low
        rinv = rinv_ref[0, 0, h : h + 1, :]
        mine = d_t[h * HD : (h + 1) * HD] * rinv
        minus = -jnp.sum(mine * c_t[h * HD : (h + 1) * HD], axis=0, keepdims=True)
        high = minus.astype(BF16).astype(F32)
        extra = jnp.where(row8 == 0, high, jnp.where(row8 == 1, minus - high, 0.0))
        blank = jnp.zeros((HD - 8, SEQ), F32)
        stack = [mine, extra, blank] if h == 0 else [extra, blank, mine]
        g_t = jnp.concatenate(stack, axis=0).astype(BF16)
        v_h = jnp.where(own, v, ones)
        e = e_ref[h]
        d = e * dot(v_h, g_t).astype(BF16)
        dv.append(dot(e, g_t, NT))
        dk.append(dot(d, q))
        dq.append(dot(k_t[h * HD : (h + 1) * HD], d))
    out_ref[0] = (jnp.concatenate(dq, axis=0).T * SCORE_SCALE).astype(BF16)
    out_ref[1] = (jnp.where(low, dk[0], dk[1]) * SCORE_SCALE).astype(BF16)
    out_ref[2] = jnp.where(low, dv[0], dv[1]).astype(BF16)


def attn_bwd(qkv, ctx, dctx, e, rinv):
    rows, pairs = rinv.shape[0], rinv.shape[1]
    width = qkv.shape[2]
    take = lambda c: pl.BlockSpec((1, SEQ, PAIR), lambda r, p: (c, r, p))
    flat = pl.BlockSpec((SEQ, PAIR), lambda r, p: (r, p))
    return pl.pallas_call(
        attn_bwd_kernel,
        grid=(rows, pairs),
        in_specs=[
            take(0),
            take(1),
            take(2),
            flat,
            flat,
            pl.BlockSpec((2, SEQ, SEQ), lambda r, p: (r * pairs + p, 0, 0)),
            pl.BlockSpec((1, 1, 2, SEQ), lambda r, p: (r, p, 0, 0)),
        ],
        out_specs=pl.BlockSpec((3, SEQ, PAIR), lambda r, p: (0, r, p)),
        out_shape=jax.ShapeDtypeStruct((3, rows * SEQ, width), BF16),
        cost_estimate=pl.CostEstimate(
            flops=rows * pairs * 2 * 8 * SEQ * SEQ * PAIR * 2,
            bytes_accessed=rows * pairs * 2 * SEQ * SEQ * 2,
            transcendentals=0,
        ),
        name="attn_bwd",
    )(qkv, qkv, qkv, ctx, dctx, e, rinv)


def mask_lanes(seg_rows):
    ends = [seg_rows[:, 0]]
    for s in range(1, seg_rows.shape[1]):
        ends.append(ends[-1] + seg_rows[:, s])
    slot = jnp.arange(SEQ, dtype=jnp.int32)[None, :]
    segment = sum((slot >= end[:, None]).astype(jnp.int32) for end in ends)[..., None]
    lane = jnp.arange(PAIR, dtype=jnp.int32)[None, None, :] & (HD - 1)
    used = lane < seg_rows.shape[1]
    k_aug = jnp.where(used & (lane == segment), 1.0, 0.0).astype(BF16)
    q_aug = jnp.where(used & (lane != segment), MASKED, 0.0).astype(BF16)
    return q_aug, k_aug


def over_mp(x):
    n = lax.axis_size("mp")
    return lax.ppermute(x, "mp", [(i, i ^ 1) for i in range(n)])


def over_dp(x, bit):
    n = lax.axis_size("dp")
    return lax.ppermute(x, "dp", [(i, i ^ bit) for i in range(n)])


def place_kernel(n, rows, at_ref, *refs):
    out_ref = refs[-1]
    k = 0
    for ref in refs[:-1]:
        for i in range(ref.shape[-2] // rows):
            spot = pl.ds(pl.multiple_of(at_ref[k], 16), rows)
            take = pl.ds(i * rows, rows)
            if len(out_ref.shape) == 2:
                out_ref[spot, :] = ref[take, :].astype(out_ref.dtype)
            else:
                out_ref[:, spot, :] = ref[:, take, :].astype(out_ref.dtype)
            k += 1


def place(pieces, at, rows, dtype):
    total = sum(piece.shape[-2] for piece in pieces)
    n = total // rows
    lead, cols = pieces[0].shape[:-2], pieces[0].shape[-1]
    size = total * cols * (lead[0] if lead else 1)
    whole = pl.BlockSpec(memory_space=pltpu.VMEM)
    return pl.pallas_call(
        functools.partial(place_kernel, n, rows),
        in_specs=[pl.BlockSpec(memory_space=pltpu.SMEM)] + [whole] * len(pieces),
        out_specs=whole,
        out_shape=jax.ShapeDtypeStruct(lead + (total, cols), dtype),
        compiler_params=pltpu.CompilerParams(vmem_limit_bytes=32 * 2**20),
        cost_estimate=pl.CostEstimate(flops=0, bytes_accessed=6 * size, transcendentals=0),
        name="place",
    )(at, *pieces)


def fetch_other(w, quarter):
    rows = w.shape[-2] // 4
    own = lax.dynamic_slice_in_dim(w, quarter * rows, rows, w.ndim - 2)
    first = over_mp(own)
    second = over_dp(first, 2)
    third, fourth = over_dp(first, 1), over_dp(second, 1)
    at = jnp.stack([quarter, quarter ^ 2, quarter ^ 1, quarter ^ 3]).astype(jnp.int32) * rows
    return place([first, second, third, fourth], at, rows, w.dtype)


SPLIT_BITS = (1, 2, 4, 8)


def reduce_all(mine, other, me):
    rows = mine.shape[0]

    def halves(x, bit):
        half = x.shape[0] // 2
        up = (me & bit) // bit
        keep = lax.dynamic_slice_in_dim(x, up * half, half, 0)
        send = lax.dynamic_slice_in_dim(x, (1 - up) * half, half, 0)
        return keep, send

    add = lambda a, b: (a.astype(F32) + b.astype(F32)).astype(BF16)
    keep_o, send_o = halves(other, 1)
    keep_m, send_m = halves(mine, 1)
    other = add(keep_o, over_dp(send_o, 1))
    mine = add(keep_m, over_dp(send_m, 1))
    mine = add(mine, over_mp(other))
    for bit in SPLIT_BITS[1:]:
        keep, send = halves(mine, bit)
        mine = add(keep, over_dp(send, bit))
    bit = 2 * SPLIT_BITS[-1]
    while bit < lax.axis_size("dp"):
        mine = add(mine, over_dp(mine, bit))
        bit *= 2
    held, order = [mine], [0]
    for bit in reversed(SPLIT_BITS):
        full = jnp.concatenate(held, axis=0) if len(held) > 1 else held[0]
        held.append(over_dp(full, bit))
        order += [o ^ bit for o in order]
    size = len(SPLIT_BITS)
    at = []
    for o in order:
        who = me ^ o
        spot = sum(((who >> b) & 1) << (size - 1 - b) for b in range(size))
        at.append(spot * (rows // 16))
    return place(held, jnp.stack(at).astype(jnp.int32), rows // 16, F32)


def layer_norm(v):
    centered = v - jnp.mean(v, axis=-1, keepdims=True)
    rstd = lax.rsqrt(jnp.mean(centered * centered, axis=-1, keepdims=True) + EPSILON)
    return centered * rstd, rstd


def layer_norm_back(dy, xhat, rstd, gain):
    dg = dy * gain
    return rstd * (
        dg
        - jnp.mean(dg, axis=-1, keepdims=True)
        - xhat * jnp.mean(dg * xhat, axis=-1, keepdims=True)
    )


def gelu_and_slope(u):
    inner = GELU_COEF * (u + 0.044715 * u * u * u)
    t = jnp.tanh(inner)
    act = 0.5 * u * (1.0 + t)
    slope = 0.5 * (1.0 + t) + 0.5 * u * (1.0 - t * t) * GELU_COEF * (1.0 + 3 * 0.044715 * u * u)
    return act, slope


def shards(
    tokens_in,
    seg_lengths,
    pad_counts,
    w_qkv,
    qv_bias,
    w_out,
    out_bias,
    norm1_gain,
    norm1_bias,
    w_up,
    up_bias,
    w_down,
    down_bias,
    norm2_gain,
    norm2_bias,
    cotangent,
):
    tokens, width = tokens_in.shape
    rows_here = tokens // SEQ
    local = w_qkv.shape[2]
    units = w_up.shape[1]
    me = lax.axis_index("dp")
    quarter = me & 3
    start = lax.axis_index("mp") * rows_here
    seg_rows = lax.dynamic_slice_in_dim(seg_lengths, start, rows_here, 0)
    pads = lax.dynamic_slice_in_dim(pad_counts, start, rows_here, 0)

    small_w = jnp.concatenate([qv_bias.reshape(-1), up_bias])
    small_o = over_mp(small_w)
    qv_biases = (qv_bias, small_o[: 2 * local].reshape(2, local))
    up_biases = (up_bias, small_o[2 * local :])
    w_qkvs = (w_qkv, fetch_other(w_qkv, quarter))
    w_outs = (w_out, fetch_other(w_out, quarter))
    w_ups = (w_up, fetch_other(w_up, quarter))
    w_downs = (w_down, fetch_other(w_down, quarter))

    q_aug, k_aug = mask_lanes(seg_rows)
    qkv, ctx, probs, rinv = [], [], [], []
    for h in range(2):
        b = qv_biases[h].astype(F32)
        bias = jnp.stack([b[0], jnp.zeros_like(b[0]), b[1]])
        projected = jnp.einsum("td,cde->cte", tokens_in, w_qkvs[h], preferred_element_type=F32)
        qkv.append((projected + bias[:, None, :]).astype(BF16))
        c, e, r = attn_fwd(qkv[h], pads, q_aug, k_aug)
        ctx.append(c)
        probs.append(e)
        rinv.append(r)

    gain_one, shift_one = norm1_gain.astype(F32), norm1_bias.astype(F32)
    gain_two, shift_two = norm2_gain.astype(F32), norm2_bias.astype(F32)
    attended = dot(ctx[0], w_outs[0]) + dot(ctx[1], w_outs[1]) + out_bias.astype(F32)
    xhat_one, rstd_one = layer_norm(tokens_in.astype(F32) + attended)
    normed = xhat_one * gain_one + shift_one
    mid = normed.astype(BF16)
    act, slope = [], []
    for h in range(2):
        a, s = gelu_and_slope(dot(mid, w_ups[h]) + up_biases[h].astype(F32))
        act.append(a.astype(BF16))
        slope.append(s.astype(BF16))
    second = (
        normed + dot(act[0], w_downs[0]) + dot(act[1], w_downs[1]) + down_bias.astype(F32)
    )
    xhat_two, rstd_two = layer_norm(second)
    final_rows = xhat_two * gain_two + shift_two
    tokens_out = final_rows.astype(BF16)
    count = SEQ - pads
    usable = (jnp.arange(SEQ, dtype=jnp.int32)[None, :] < count[:, None]).astype(F32)
    pooled = (
        jnp.sum(final_rows.reshape(rows_here, SEQ, width) * usable[..., None], axis=1)
        / count.astype(F32)[:, None]
    )

    dy = cotangent.astype(F32)
    grad_gain_two, grad_shift_two = jnp.sum(dy * xhat_two, axis=0), jnp.sum(dy, axis=0)
    grad_second = layer_norm_back(dy, xhat_two, rstd_two, gain_two)
    grad_branch = grad_second.astype(BF16)
    grad_down_bias = jnp.sum(grad_branch.astype(F32), axis=0)
    grad_down = [dot(act[h], grad_branch, TN).astype(BF16) for h in range(2)]
    grad_down = reduce_all(*grad_down, me)
    upper = [
        (dot(grad_branch, w_downs[h], NT) * slope[h].astype(F32)).astype(BF16) for h in range(2)
    ]
    grad_up_bias = [jnp.sum(u.astype(F32), axis=0) for u in upper]
    grad_up = [dot(mid, upper[h], TN).astype(BF16) for h in range(2)]
    grad_up = reduce_all(*grad_up, me)
    grad_normed = grad_second + dot(upper[0], w_ups[0], NT) + dot(upper[1], w_ups[1], NT)
    grad_gain_one = jnp.sum(grad_normed * xhat_one, axis=0)
    grad_shift_one = jnp.sum(grad_normed, axis=0)
    grad_resid = layer_norm_back(grad_normed, xhat_one, rstd_one, gain_one)
    grad_attended = grad_resid.astype(BF16)
    grad_out_bias = jnp.sum(grad_attended.astype(F32), axis=0)

    total, grad_qv_bias, grad_attn = grad_resid, [], []
    for h in range(2):
        grad_ctx = dot(grad_attended, w_outs[h], NT).astype(BF16)
        grad_act = attn_bwd(qkv[h], ctx[h], grad_ctx, probs[h], rinv[h])
        grad_qv_bias.append(jnp.sum(grad_act[::2].astype(F32), axis=1))
        g = jnp.einsum("td,cte->cde", tokens_in, grad_act, preferred_element_type=F32)
        g = g.astype(BF16).reshape(3 * width, local)
        g_out = dot(grad_attended, ctx[h], TN).astype(BF16)
        grad_attn.append(jnp.concatenate([g, g_out], axis=0))
        total = total + jnp.einsum(
            "cte,cde->td", grad_act, w_qkvs[h], preferred_element_type=F32
        )
    grad_input = total.astype(BF16)
    grad_attn = reduce_all(*grad_attn, me)
    grad_qkv = grad_attn[: 3 * width].reshape(3, width, local)
    grad_out = grad_attn[3 * width :].T

    same = jnp.concatenate(
        [
            grad_out_bias,
            grad_gain_one,
            grad_shift_one,
            grad_down_bias,
            grad_gain_two,
            grad_shift_two,
        ]
    )
    own = [jnp.concatenate([grad_qv_bias[h].reshape(-1), grad_up_bias[h]]) for h in range(2)]
    small = jnp.concatenate([same, own[0]]) + over_mp(jnp.concatenate([same, own[1]]))
    bit = 1
    while bit < lax.axis_size("dp"):
        small = small + over_dp(small, bit)
        bit *= 2
    vectors = small[: 6 * width].reshape(6, width)
    grad_qv_bias = small[6 * width : 6 * width + 2 * local].reshape(2, local)
    grad_up_bias = small[6 * width + 2 * local :]
    return (
        tokens_out,
        pooled,
        grad_input,
        grad_qkv,
        grad_qv_bias,
        grad_out,
        vectors[0],
        vectors[1],
        vectors[2],
        grad_up,
        grad_up_bias,
        grad_down,
        vectors[3],
        vectors[4],
        vectors[5],
    )


def solution(mesh):
    token = P(("dp", "mp"), None)
    in_specs = (
        token,
        P("dp", None),
        P("dp"),
        P(None, None, "mp"),
        P(None, "mp"),
        P("mp", None),
        P(),
        P(),
        P(),
        P(None, "mp"),
        P("mp"),
        P("mp", None),
        P(),
        P(),
        P(),
        token,
    )
    out_specs = (
        token,
        token,
        token,
        P(None, None, "mp"),
        P(None, "mp"),
        P("mp", None),
        P(),
        P(),
        P(),
        P(None, "mp"),
        P("mp"),
        P("mp", None),
        P(),
        P(),
        P(),
    )
    return jax.shard_map(shards, mesh=mesh, in_specs=in_specs, out_specs=out_specs, check_vma=False)
```

```python
import functools

import jax
import jax.numpy as jnp
from jax import lax
from jax.experimental import pallas as pl
from jax.experimental.pallas import tpu as pltpu
from jax.sharding import PartitionSpec as P

HD = 64
SEQ = 512
PAIR = 128
EPSILON = 1e-12
SCORE_SCALE = 0.125
GELU_COEF = 0.7978845608028654
MASKED = -1e30
F32 = jnp.float32
BF16 = jnp.bfloat16

NT = (((1,), (1,)), ((), ()))
NN = (((1,), (0,)), ((), ()))
TN = (((0,), (0,)), ((), ()))


TILE = 256
CHUNK = 512
HINT = 8.0
VMEM_LIMIT = 56 * 2**20


def cost(gflop, size):
    return pl.CostEstimate(
        flops=int(gflop * HINT * 1e9), bytes_accessed=int(size * HINT), transcendentals=0
    )


def dot(a, b, dims=NN):
    return lax.dot_general(a, b, dims, preferred_element_type=F32)


def attn_fwd_kernel(
    info_ref, pad_ref, x_ref, w_ref, bias_ref, qa_ref, ka_ref, qkv_ref, ctx_ref, e_ref, rinv_ref
):
    limit = SEQ - pad_ref[info_ref[4] + pl.program_id(0)]
    w = jnp.concatenate([w_ref[0], w_ref[1], w_ref[2]], axis=1)
    qkv = dot(x_ref[...], w)
    bias = bias_ref[...].astype(F32)
    q = (qkv[:, :PAIR] + bias[0:1]).astype(BF16)
    k = qkv[:, PAIR : 2 * PAIR].astype(BF16)
    v = (qkv[:, 2 * PAIR :] + bias[1:2]).astype(BF16)
    qkv_ref[0], qkv_ref[1], qkv_ref[2] = q, k, v
    v_t = v.astype(F32).T.astype(BF16)
    low = lax.broadcasted_iota(jnp.int32, (SEQ, PAIR), 1) < HD
    parts = []
    for h in range(2):
        own = low if h == 0 else ~low
        q_h = jnp.where(own, q, qa_ref[0])
        k_h = jnp.where(own, k, ka_ref[0])
        s = dot(k_h, q_h, NT)
        j = lax.broadcasted_iota(jnp.int32, (64, SEQ), 0) + (SEQ - 64)
        i = lax.broadcasted_iota(jnp.int32, (64, SEQ), 1)
        tail = jnp.where((j < limit) | (j == i), s[SEQ - 64 :], MASKED)
        s = jnp.concatenate([s[: SEQ - 64], tail], axis=0)
        peak = jnp.max(s, axis=0, keepdims=True)
        e = jnp.exp((s - peak) * SCORE_SCALE)
        rinv = 1.0 / jnp.sum(e, axis=0, keepdims=True)
        eb = e.astype(BF16)
        e_ref[h] = eb
        rinv_ref[0, 0, h : h + 1, :] = rinv
        parts.append(dot(v_t[h * HD : (h + 1) * HD], eb) * rinv)
    ctx_ref[...] = jnp.concatenate(parts, axis=0).T.astype(BF16)


def attn_fwd(tokens, w_qkv, bias, info, pads, q_aug, k_aug, span=None, into=None):
    rows, width = tokens.shape[0] // SEQ, w_qkv.shape[2]
    pairs, model = width // PAIR, tokens.shape[1]
    first, end = span or (0, pairs)
    aug = pl.BlockSpec((1, SEQ, PAIR), lambda r, p, *_: (r, 0, 0))
    into = list(into or ())
    kernel = attn_fwd_kernel
    if into:
        kernel = lambda *refs: attn_fwd_kernel(*refs[:7], *refs[7 + len(into) :])
    return pl.pallas_call(
        kernel,
        grid_spec=pltpu.PrefetchScalarGridSpec(
            num_scalar_prefetch=2,
            grid=(rows, end - first),
            in_specs=[
                pl.BlockSpec((SEQ, model), lambda r, p, *_: (r, 0)),
                pl.BlockSpec((3, model, PAIR), lambda r, p, *_: (0, 0, first + p)),
                pl.BlockSpec((2, PAIR), lambda r, p, *_: (0, first + p)),
                aug,
                aug,
            ]
            + [pl.BlockSpec(memory_space=pl.ANY)] * len(into),
            out_specs=[
                pl.BlockSpec((3, SEQ, PAIR), lambda r, p, *_: (0, r, first + p)),
                pl.BlockSpec((SEQ, PAIR), lambda r, p, *_: (r, first + p)),
                pl.BlockSpec((2, SEQ, SEQ), lambda r, p, *_: (r * pairs + first + p, 0, 0)),
                pl.BlockSpec((1, 1, 2, SEQ), lambda r, p, *_: (r, first + p, 0, 0)),
            ],
        ),
        out_shape=[
            jax.ShapeDtypeStruct((3, rows * SEQ, width), BF16),
            jax.ShapeDtypeStruct((rows * SEQ, width), BF16),
            jax.ShapeDtypeStruct((rows * pairs * 2, SEQ, SEQ), BF16),
            jax.ShapeDtypeStruct((rows, pairs, 2, SEQ), F32),
        ],
        input_output_aliases={7 + i: i for i in range(len(into))},
        compiler_params=pltpu.CompilerParams(vmem_limit_bytes=VMEM_LIMIT),
        cost_estimate=cost(2.3 * rows * (end - first), rows * (end - first) * 2 * SEQ * SEQ * 2),
        name="attn_fwd",
    )(info, pads, tokens, w_qkv, bias, q_aug, k_aug, *into)


def attn_bwd_kernel(
    x_ref, ga_ref, wo_ref, qkv_ref, ctx_ref, e_ref, rinv_ref, out_ref, gw_ref, gb_ref, acc_ref
):
    row, last = pl.program_id(1), pl.num_programs(1) - 1
    q, k, v = qkv_ref[0], qkv_ref[1], qkv_ref[2]
    k_t = k.astype(F32).T.astype(BF16)
    d_t = dot(wo_ref[...], ga_ref[...], NT).astype(BF16).astype(F32)
    c_t = ctx_ref[...].astype(F32).T
    lane = lax.broadcasted_iota(jnp.int32, (SEQ, PAIR), 1)
    row8 = lax.broadcasted_iota(jnp.int32, (8, SEQ), 0)
    low = lane < HD
    ones = jnp.where((lane & (HD - 1)) < 2, 1.0, 0.0).astype(BF16)
    dv, dk, dq = [], [], []
    for h in range(2):
        own = low if h == 0 else ~low
        rinv = rinv_ref[0, 0, h : h + 1, :]
        mine = d_t[h * HD : (h + 1) * HD] * rinv
        minus = -jnp.sum(mine * c_t[h * HD : (h + 1) * HD], axis=0, keepdims=True)
        high = minus.astype(BF16).astype(F32)
        extra = jnp.where(row8 == 0, high, jnp.where(row8 == 1, minus - high, 0.0))
        blank = jnp.zeros((HD - 8, SEQ), F32)
        stack = [mine, extra, blank] if h == 0 else [extra, blank, mine]
        g_t = jnp.concatenate(stack, axis=0).astype(BF16)
        v_h = jnp.where(own, v, ones)
        e = e_ref[h]
        d = e * dot(v_h, g_t).astype(BF16)
        dv.append(dot(e, g_t, NT))
        dk.append(dot(d, q))
        dq.append(dot(k_t[h * HD : (h + 1) * HD], d))
    dq_t = jnp.concatenate(dq, axis=0) * SCORE_SCALE
    dk = jnp.where(low, dk[0], dk[1]) * SCORE_SCALE
    dv = jnp.where(low, dv[0], dv[1])
    dq_b = dq_t.T.astype(BF16)
    dk_b, dv_b = dk.astype(BF16), dv.astype(BF16)
    out_ref[0], out_ref[1], out_ref[2] = dq_b, dk_b, dv_b
    left = jnp.concatenate([dq_t, dk.T, dv.T], axis=0).astype(BF16)
    g_w = dot(left, x_ref[...]).reshape(3, PAIR, x_ref.shape[1])
    g_o = dot(c_t.astype(BF16), ga_ref[...])
    g_b = jnp.concatenate(
        [
            jnp.sum(dq_b.astype(F32), axis=0, keepdims=True),
            jnp.sum(dv_b.astype(F32), axis=0, keepdims=True),
        ],
        axis=0,
    )

    @pl.when(row == 0)
    def _():
        acc_ref[:3] = g_w
        acc_ref[3] = g_o
        gb_ref[...] = g_b

    @pl.when(row > 0)
    def _():
        acc_ref[:3] += g_w
        acc_ref[3] += g_o
        gb_ref[...] += g_b

    @pl.when(row == last)
    def _():
        gw_ref[...] = acc_ref[...].astype(BF16)


def attn_bwd(tokens, grad_att, w_out, qkv, ctx, e, rinv):
    rows, pairs = rinv.shape[0], rinv.shape[1]
    width, model = qkv.shape[2], tokens.shape[1]
    wide = pl.BlockSpec((SEQ, model), lambda p, r: (r, 0))
    triple = pl.BlockSpec((3, SEQ, PAIR), lambda p, r: (0, r, p))
    return pl.pallas_call(
        attn_bwd_kernel,
        grid=(pairs, rows),
        in_specs=[
            wide,
            wide,
            pl.BlockSpec((PAIR, model), lambda p, r: (p, 0)),
            triple,
            pl.BlockSpec((SEQ, PAIR), lambda p, r: (r, p)),
            pl.BlockSpec((2, SEQ, SEQ), lambda p, r: (r * pairs + p, 0, 0)),
            pl.BlockSpec((1, 1, 2, SEQ), lambda p, r: (r, p, 0, 0)),
        ],
        out_specs=[
            triple,
            pl.BlockSpec((4, PAIR, model), lambda p, r: (0, p, 0)),
            pl.BlockSpec((2, PAIR), lambda p, r: (0, p)),
        ],
        out_shape=[
            jax.ShapeDtypeStruct((3, rows * SEQ, width), BF16),
            jax.ShapeDtypeStruct((4, width, model), BF16),
            jax.ShapeDtypeStruct((2, width), F32),
        ],
        scratch_shapes=[pltpu.VMEM((4, PAIR, model), F32)],
        compiler_params=pltpu.CompilerParams(vmem_limit_bytes=VMEM_LIMIT),
        cost_estimate=cost(8 * rows, rows * pairs * 2 * SEQ * SEQ * 2),
        name="attn_bwd",
    )(tokens, grad_att, w_out, qkv, ctx, e, rinv)


def vector(x):
    return pl.BlockSpec(x.shape, lambda *_: (0,) * x.ndim)


def normalise(v):
    centered = v - jnp.mean(v, axis=-1, keepdims=True)
    rstd = lax.rsqrt(jnp.mean(centered * centered, axis=-1, keepdims=True) + EPSILON)
    return centered * rstd, rstd


def normalise_back(dy, xhat, rstd, gain):
    dg = dy * gain
    return rstd * (
        dg
        - jnp.mean(dg, axis=-1, keepdims=True)
        - xhat * jnp.mean(dg * xhat, axis=-1, keepdims=True)
    )


def gelu_and_slope(u):
    u2 = u * u
    t = jnp.tanh(u * (GELU_COEF + (GELU_COEF * 0.044715) * u2))
    half = 0.5 + 0.5 * t
    act = u * half
    slope = half * (1.0 + u * (1.0 - t) * (GELU_COEF + (3 * GELU_COEF * 0.044715) * u2))
    return act, slope


def flat_bias(ref):
    b = ref[...].astype(F32)
    return jnp.concatenate([b[i : i + 1] for i in range(b.shape[0])], axis=1)


def units(mid, acc, wu_ref, ub_ref, wd_ref, act_ref, slope_ref):
    bias = flat_bias(ub_ref)
    for j in range(0, wu_ref.shape[1], CHUNK):
        part = slice(j, j + CHUNK)
        act, slope = gelu_and_slope(dot(mid, wu_ref[:, part]) + bias[:, part])
        act = act.astype(BF16)
        act_ref[:, part] = act
        slope_ref[:, part] = slope.astype(BF16)
        acc = acc + dot(act, wd_ref[part, :])
    return acc


def ffn_front_kernel(
    cm_ref, co_ref, x_ref, wm_ref, wo_ref, vec_ref, wu_ref, ub_ref, wd_ref,
    mid_ref, xhat_ref, rstd_ref, part_ref, act_ref, slope_ref,
):
    vec = vec_ref[...].astype(F32)
    attended = dot(cm_ref[...], wm_ref[...]) + dot(co_ref[...], wo_ref[...])
    resid = x_ref[...].astype(F32) + (attended + vec[0:1])
    xhat, rstd = normalise(resid)
    normed = xhat * vec[1:2] + vec[2:3]
    mid = normed.astype(BF16)
    mid_ref[...] = mid
    xhat_ref[...] = xhat
    rstd_ref[...] = rstd
    part_ref[...] = units(mid, normed + vec[3:4], wu_ref, ub_ref, wd_ref, act_ref, slope_ref)


def ffn_front(ctx, tokens, w_outs, vectors, w_up, up_bias, w_down):
    n, model = tokens.shape
    width, hidden = ctx[0].shape[1], w_up.shape[1]
    row = lambda c: pl.BlockSpec((TILE, c), lambda t: (t, 0))
    shape = lambda c, d: jax.ShapeDtypeStruct((n, c), d)
    fixed = [vectors, w_up, up_bias, w_down]
    return pl.pallas_call(
        ffn_front_kernel,
        grid=(n // TILE,),
        in_specs=[row(width), row(width), row(model)] + [vector(a) for a in (*w_outs, *fixed)],
        out_specs=[row(model), row(model), row(1), row(model), row(hidden), row(hidden)],
        out_shape=[
            shape(model, BF16),
            shape(model, F32),
            shape(1, F32),
            shape(model, F32),
            shape(hidden, BF16),
            shape(hidden, BF16),
        ],
        compiler_params=pltpu.CompilerParams(vmem_limit_bytes=VMEM_LIMIT),
        cost_estimate=cost(10, n * model * 24),
        name="ffn_front",
    )(*ctx, tokens, *w_outs, *fixed)


def ffn_back_kernel(
    info_ref, pad_ref, mid_ref, xhat_ref, rstd_ref, part_ref, slope_m_ref, cot_ref,
    wu_m_ref, wd_m_ref, wu_o_ref, ub_o_ref, wd_o_ref, vec_ref,
    out_ref, pool_ref, act_ref, branch_ref, up_m_ref, up_o_ref, resid_ref, att_ref,
    sums_ref, ub_m_sum_ref, ub_o_sum_ref, slope_ref,
):
    t = pl.program_id(0)
    per_row = SEQ // TILE
    mid = mid_ref[...]
    second = units(mid, part_ref[...], wu_o_ref, ub_o_ref, wd_o_ref, act_ref, slope_ref)
    vec = vec_ref[...].astype(F32)
    gain_two = vec[4:5]
    xhat_two, rstd_two = normalise(second)
    final = xhat_two * gain_two + vec[5:6]
    out_ref[...] = final.astype(BF16)
    count = SEQ - pad_ref[info_ref[4] + t // per_row]
    slot = lax.broadcasted_iota(jnp.int32, (TILE, 1), 0) + (t % per_row) * TILE
    pooled = jnp.sum(jnp.where(slot < count, final, 0.0), axis=0, keepdims=True)
    pooled = pooled / count.astype(F32)
    which = lax.broadcasted_iota(jnp.int32, pool_ref.shape, 0) == t // per_row
    pooled = jnp.where(which, pooled, 0.0)

    dy = cot_ref[...].astype(F32)
    down = lambda v: jnp.sum(v, axis=0, keepdims=True)
    sums = [down(dy * xhat_two), down(dy)]
    second_grad = normalise_back(dy, xhat_two, rstd_two, gain_two)
    branch = second_grad.astype(BF16)
    branch_ref[...] = branch
    sums.append(down(branch.astype(F32)))
    normed_grad = second_grad
    bias_sums = []
    for wu_ref, wd_ref, s_ref, up_ref in (
        (wu_o_ref, wd_o_ref, slope_ref, up_o_ref),
        (wu_m_ref, wd_m_ref, slope_m_ref, up_m_ref),
    ):
        parts = []
        for j in range(0, wu_ref.shape[1], CHUNK):
            part = slice(j, j + CHUNK)
            upper = dot(branch, wd_ref[part, :], NT) * s_ref[:, part].astype(F32)
            upper = upper.astype(BF16)
            up_ref[:, part] = upper
            parts.append(down(upper.astype(F32)))
            normed_grad = normed_grad + dot(upper, wu_ref[:, part], NT)
        bias_sums.append(jnp.concatenate(parts, axis=1))
    xhat_one = xhat_ref[...]
    sums += [down(normed_grad * xhat_one), down(normed_grad)]
    resid = normalise_back(normed_grad, xhat_one, rstd_ref[...], vec[1:2])
    resid_ref[...] = resid
    att = resid.astype(BF16)
    att_ref[...] = att
    sums.append(down(att.astype(F32)))
    sums = jnp.concatenate(sums, axis=0)

    @pl.when(t == 0)
    def _():
        pool_ref[...] = pooled
        sums_ref[...] = sums
        ub_o_sum_ref[...] = bias_sums[0]
        ub_m_sum_ref[...] = bias_sums[1]

    @pl.when(t > 0)
    def _():
        pool_ref[...] += pooled
        sums_ref[...] += sums
        ub_o_sum_ref[...] += bias_sums[0]
        ub_m_sum_ref[...] += bias_sums[1]


def ffn_back(info, pads, mid, xhat, rstd, part, slope, cot, w_ups, w_downs, up_bias_o, vectors):
    n, model = mid.shape
    hidden, rows = slope.shape[1], n // SEQ
    row = lambda c: pl.BlockSpec((TILE, c), lambda t, *_: (t, 0))
    keep = lambda r, c: pl.BlockSpec((r, c), lambda t, *_: (0, 0))
    shape = lambda c, d: jax.ShapeDtypeStruct((n, c), d)
    fixed = [w_ups[0], w_downs[0], w_ups[1], up_bias_o, w_downs[1], vectors]
    return pl.pallas_call(
        ffn_back_kernel,
        grid_spec=pltpu.PrefetchScalarGridSpec(
            num_scalar_prefetch=2,
            grid=(n // TILE,),
            in_specs=[row(model), row(model), row(1), row(model), row(hidden), row(model)]
            + [vector(a) for a in fixed],
            out_specs=[
                row(model),
                keep(rows, model),
                row(hidden),
                row(model),
                row(hidden),
                row(hidden),
                row(model),
                row(model),
                keep(6, model),
                keep(1, hidden),
                keep(1, hidden),
            ],
            scratch_shapes=[pltpu.VMEM((TILE, hidden), BF16)],
        ),
        out_shape=[
            shape(model, BF16),
            jax.ShapeDtypeStruct((rows, model), F32),
            shape(hidden, BF16),
            shape(model, BF16),
            shape(hidden, BF16),
            shape(hidden, BF16),
            shape(model, F32),
            shape(model, BF16),
            jax.ShapeDtypeStruct((6, model), F32),
            jax.ShapeDtypeStruct((1, hidden), F32),
            jax.ShapeDtypeStruct((1, hidden), F32),
        ],
        compiler_params=pltpu.CompilerParams(vmem_limit_bytes=VMEM_LIMIT),
        cost_estimate=cost(25, n * model * 40),
        name="ffn_back",
    )(info, pads, mid, xhat, rstd, part, slope, cot, *fixed)


def pack_attn_kernel(info_ref, wq_ref, wo_ref, qb_ref, attn_ref):
    r, w = wq_ref.shape[1:]
    attn_ref[:r, :w] = wq_ref[0]
    attn_ref[:r, w:] = wq_ref[1]
    attn_ref[r : r + r // 2, :w] = wq_ref[2, : r // 2]
    attn_ref[r : r + r // 2, w:] = wq_ref[2, r // 2 :]
    at = r + r // 2
    attn_ref[at : at + wo_ref.shape[0], :] = wo_ref[...]
    at += wo_ref.shape[0]
    attn_ref[at:, :] = jnp.zeros((16, 2 * w), BF16)
    attn_ref[at : at + 2, :w] = qb_ref[...]


def pack_ffn_kernel(info_ref, seg_ref, wu_ref, wd_ref, ub_ref, up_ref, qa_ref, ka_ref):
    u, c = wu_ref.shape[0], up_ref.shape[1]
    up_ref[:u, :] = wu_ref[:, :c]
    up_ref[u : 2 * u, :] = wu_ref[:, c:]
    up_ref[2 * u : 2 * u + wd_ref.shape[0], :] = wd_ref[...]
    at = 2 * u + wd_ref.shape[0]
    up_ref[at:, :] = jnp.zeros((16, c), BF16)
    up_ref[at : at + 2, :] = ub_ref[...]
    segs = seg_ref.shape[1]
    slot = lax.broadcasted_iota(jnp.int32, (SEQ, PAIR), 0)
    lane = lax.broadcasted_iota(jnp.int32, (SEQ, PAIR), 1) & (HD - 1)
    for row in range(qa_ref.shape[0]):
        end, segment = 0, jnp.zeros((SEQ, PAIR), jnp.int32)
        for s in range(segs):
            end = end + seg_ref[info_ref[4] + row, s]
            segment = segment + jnp.where(slot >= end, 1, 0)
        same = lane == segment
        ka_ref[row] = jnp.where(same & (lane < segs), 1.0, 0.0).astype(BF16)
        qa_ref[row] = jnp.where((lane < segs) & ~same, MASKED, 0.0).astype(BF16)


def pack_attn(info, w_qkv, w_out, qv_bias):
    model, width = w_qkv.shape[1:]
    out_rows = w_out.shape[0] // 4
    shape = (3 * width // 4 + out_rows + 16, model)
    whole = lambda s: pl.BlockSpec(s, lambda i, *_: (0,) * len(s))
    return pl.pallas_call(
        pack_attn_kernel,
        grid_spec=pltpu.PrefetchScalarGridSpec(
            num_scalar_prefetch=1,
            grid=(1,),
            in_specs=[
                pl.BlockSpec((3, model // 4, width), lambda i, at: (0, at[0], 0)),
                pl.BlockSpec((out_rows, model), lambda i, at: (at[0], 0)),
                whole(qv_bias.shape),
            ],
            out_specs=whole(shape),
        ),
        out_shape=jax.ShapeDtypeStruct(shape, BF16),
        cost_estimate=cost(0, 2 * 2**20),
        name="pack_attn",
    )(info, w_qkv, w_out, qv_bias)


def pack_ffn(info, rows, seg_lengths, w_up, w_down, up_bias):
    model = w_up.shape[0]
    up_rows, down_rows = model // 4, w_down.shape[0] // 4
    whole = lambda s: pl.BlockSpec(s, lambda i, *_: (0,) * len(s))
    shapes = [(2 * up_rows + down_rows + 16, model)] + [(rows, SEQ, PAIR)] * 2
    return pl.pallas_call(
        pack_ffn_kernel,
        grid_spec=pltpu.PrefetchScalarGridSpec(
            num_scalar_prefetch=2,
            grid=(1,),
            in_specs=[
                pl.BlockSpec((up_rows, w_up.shape[1]), lambda i, at, _: (at[0], 0)),
                pl.BlockSpec((down_rows, model), lambda i, at, _: (at[0], 0)),
                whole(up_bias.shape),
            ],
            out_specs=[whole(s) for s in shapes],
        ),
        out_shape=[jax.ShapeDtypeStruct(s, BF16) for s in shapes],
        cost_estimate=cost(0, 4 * 2**20),
        name="pack_ffn",
    )(info, seg_lengths, w_up, w_down, up_bias)


def unpack_attn_kernel(at_ref, *refs):
    pieces, (wq_ref, wo_ref, qb_ref) = refs[:4], refs[4:]
    r, w, o = wq_ref.shape[1] // 4, wq_ref.shape[2], wo_ref.shape[0] // 4
    for i, piece in enumerate(pieces):
        q = at_ref[i]
        rows = pl.ds(pl.multiple_of(q * r, 16), r)
        wq_ref[0, rows, :] = piece[:r, :w]
        wq_ref[1, rows, :] = piece[:r, w:]
        wq_ref[2, pl.ds(pl.multiple_of(q * r, 16), r // 2), :] = piece[r : r + r // 2, :w]
        wq_ref[2, pl.ds(pl.multiple_of(q * r + r // 2, 16), r // 2), :] = piece[r : r + r // 2, w:]
        at = r + r // 2
        wo_ref[pl.ds(pl.multiple_of(q * o, 16), o), :] = piece[at : at + o, :]
    at += o
    qb_ref[...] = pieces[0][at : at + 2, :w]


def unpack_ffn_kernel(at_ref, *refs):
    pieces, (wu_ref, wd_ref, ub_ref) = refs[:4], refs[4:]
    r, c, d = wu_ref.shape[0] // 4, wu_ref.shape[1] // 2, wd_ref.shape[0] // 4
    for i, piece in enumerate(pieces):
        rows = pl.ds(pl.multiple_of(at_ref[i] * r, 16), r)
        wu_ref[rows, :c] = piece[:r, :]
        wu_ref[rows, c:] = piece[r : 2 * r, :]
        wd_ref[pl.ds(pl.multiple_of(at_ref[i] * d, 16), d), :] = piece[2 * r : 2 * r + d, :]
    ub_ref[...] = pieces[0][2 * r + d : 2 * r + d + 2, :]


def unpack(kernel, at, pieces, like):
    whole = pl.BlockSpec(memory_space=pltpu.VMEM)
    return pl.pallas_call(
        kernel,
        in_specs=[pl.BlockSpec(memory_space=pltpu.SMEM)] + [whole] * 4,
        out_specs=[whole] * len(like),
        out_shape=[jax.ShapeDtypeStruct(a.shape, BF16) for a in like],
        compiler_params=pltpu.CompilerParams(vmem_limit_bytes=32 * 2**20),
        cost_estimate=cost(0, 5 * 2**20),
        name=kernel.__name__,
    )(at, *pieces)


def over_mp(x):
    n = lax.axis_size("mp")
    return lax.ppermute(x, "mp", [(i, i ^ 1) for i in range(n)])


def over_dp(x, bit):
    n = lax.axis_size("dp")
    return lax.ppermute(x, "dp", [(i, i ^ bit) for i in range(n)])


def gather_pieces(rows, at_ref, refs, store):
    k = 0
    for ref in refs:
        for i in range(ref.shape[0] // rows):
            spot = pl.ds(pl.multiple_of(at_ref[k] * rows, 16), rows)
            store(spot, ref[i * rows : (i + 1) * rows, :].astype(F32))
            k += 1


def place_kernel(rows, at_ref, *refs):
    out_ref = refs[-1]

    def store(spot, value):
        out_ref[spot, :] = value

    gather_pieces(rows, at_ref, refs[:-1], store)


def place_attn_kernel(rows, at_ref, *refs):
    qkv_ref, out_ref, held_ref = refs[-3:]

    def store(spot, value):
        held_ref[spot, :] = value

    gather_pieces(rows, at_ref, refs[:-3], store)
    width = qkv_ref.shape[2]
    for c in range(3):
        for e in range(0, width, PAIR):
            qkv_ref[c, :, e : e + PAIR] = held_ref[c * width + e : c * width + e + PAIR, :].T
    out_ref[...] = held_ref[3 * width :, :]


def place(pieces, at, *shapes):
    total, cols = sum(piece.shape[0] for piece in pieces), pieces[0].shape[1]
    whole = pl.BlockSpec(memory_space=pltpu.VMEM)
    kernel = place_kernel if len(shapes) == 1 else place_attn_kernel
    return pl.pallas_call(
        functools.partial(kernel, total // at.shape[0]),
        in_specs=[pl.BlockSpec(memory_space=pltpu.SMEM)] + [whole] * len(pieces),
        out_specs=[whole] * len(shapes),
        out_shape=[jax.ShapeDtypeStruct(s, F32) for s in shapes],
        scratch_shapes=[] if len(shapes) == 1 else [pltpu.VMEM((total, cols), F32)],
        compiler_params=pltpu.CompilerParams(vmem_limit_bytes=32 * 2**20),
        cost_estimate=cost(0, 6 * total * cols),
        name=kernel.__name__,
    )(at, *pieces)


def tie(x, *after):
    return lax.optimization_barrier((x,) + after)[0]


def land(info, x, got, own=None, step=None):
    n = got.shape[0]
    if own is not None:
        x = lax.dynamic_slice_in_dim(x, info[own] * n, n, 0)
    total = (x.astype(F32) + got.astype(F32)).astype(BF16)
    if step is None:
        return total
    return total, lax.dynamic_slice_in_dim(total, (1 - info[step]) * (n // 2), n // 2, 0)


CORE, Y, Z1, Z2 = 1, 2, 4, 8
SLOT = {CORE: 5, Y: 6, Z1: 7, Z2: 8}


class Chain:
    def __init__(self, info, bits):
        self.info, self.bits = info, bits
        self.dp_bits = [b for b in bits if b != "x"]
        self.order = [0]
        for b in reversed(self.dp_bits):
            self.order += [o ^ b for o in self.order]
        self.x, self.got, self.own, self.at = {}, {}, {}, {}
        self.held, self.back = None, list(reversed(self.dp_bits))

    def send(self, part, x):
        bit = self.bits[0]
        half = x.shape[0] // 2
        away = (1 - self.info[SLOT[bit]]) * half
        self.got[part] = over_dp(lax.dynamic_slice_in_dim(x, away, half, 0), bit)
        self.x[part], self.own[part], self.at[part] = x, SLOT[bit], 0

    def hop(self, part="m", *after):
        if self.held is not None:
            return self.double(*after)
        x, at = tie(self.x[part], *after), self.at[part]
        got = self.crossed if self.bits[at] == "x" else self.got[part]
        bit = self.bits[at + 1] if at + 1 < len(self.bits) else None
        self.at[part] = at + 1
        if bit is None or bit == "x":
            x = land(self.info, x, got, self.own[part])
            self.x[part], self.own[part] = x, None
            if bit is None:
                bit = 2 * max(self.dp_bits)
                while bit < lax.axis_size("dp"):
                    x = land(self.info, x, over_dp(x, bit))
                    bit *= 2
                self.held = [x]
                self.double()
            elif part == "o":
                self.crossed = over_mp(x)
            return x
        x, away = land(self.info, x, got, self.own[part], SLOT[bit])
        self.x[part], self.own[part], self.got[part] = x, SLOT[bit], over_dp(away, bit)
        return x

    def merge(self, *after):
        x, bit = self.x["m"], self.bits[2]
        half = self.crossed.shape[0]
        x = lax.dynamic_slice_in_dim(tie(x, *after), self.info[self.own["m"]] * half, half, 0)
        x = lax.optimization_barrier(x.astype(F32) + self.crossed.astype(F32))
        x, away = land(self.info, x, self.got["m"], None, SLOT[bit])
        self.at["m"] = 2
        self.x["m"], self.own["m"], self.got["m"] = x, SLOT[bit], over_dp(away, bit)
        return x

    def double(self, *after):
        full = jnp.concatenate(self.held, axis=0) if len(self.held) > 1 else self.held[0]
        full = tie(full, *after)
        self.held.append(over_dp(full, self.back.pop(0)))
        return full

    def spots(self, me):
        who = me ^ jnp.array(self.order, jnp.int32)
        spot = jnp.zeros_like(who)
        for b in self.dp_bits:
            spot = 2 * spot + (who & b) // b
        return spot


def pack_small_kernel(sums_ref, um_ref, uo_ref, qm_ref, qo_ref, keep_ref, send_ref):
    n, c, w = sums_ref.shape[0], sums_ref.shape[1], qm_ref.shape[1]
    for out_ref, u_ref, q_ref in ((keep_ref, um_ref, qm_ref), (send_ref, uo_ref, qo_ref)):
        out_ref[...] = jnp.zeros(out_ref.shape, F32)
        out_ref[:n, :] = sums_ref[...]
        for i in range(u_ref.shape[1] // c):
            out_ref[n + i : n + i + 1, :] = u_ref[:, i * c : (i + 1) * c]
        at = n + u_ref.shape[1] // c
        for i in range(2):
            out_ref[at : at + 1, i * w : (i + 1) * w] = q_ref[i : i + 1, :]


def pack_small(sums, up_sums, qv_sums):
    shape = jax.ShapeDtypeStruct((16, sums.shape[1]), F32)
    return pl.pallas_call(
        pack_small_kernel, out_shape=[shape, shape], cost_estimate=cost(0, 2**18), name="pack_small"
    )(sums, *up_sums, *qv_sums)


def shards(
    tokens_in,
    seg_lengths,
    pad_counts,
    w_qkv,
    qv_bias,
    w_out,
    out_bias,
    norm1_gain,
    norm1_bias,
    w_up,
    up_bias,
    w_down,
    down_bias,
    norm2_gain,
    norm2_bias,
    cotangent,
):
    tokens, width = tokens_in.shape
    local = w_qkv.shape[2]
    me = lax.axis_index("dp")
    rows_here = tokens // SEQ
    slot = jnp.arange(9, dtype=jnp.int32)
    start = lax.axis_index("mp") * rows_here
    first = jnp.array([0, 2, 1, 3, 0, 0, 0, 0, 0], jnp.int32) ^ (me & 3)
    info = jnp.where(slot < 4, first, jnp.where(slot == 4, start, (me >> jnp.maximum(slot - 5, 0)) & 1))
    vectors = jnp.stack([out_bias, norm1_gain, norm1_bias, down_bias, norm2_gain, norm2_bias])
    up_bias = up_bias.reshape(-1, width)

    attn_w = pack_attn(info, w_qkv, w_out, qv_bias)
    up_w, q_aug, k_aug = pack_ffn(
        info, rows_here, seg_lengths, w_up, w_down, tie(up_bias, attn_w)
    )
    attn_w, up_w = over_mp(attn_w), over_mp(up_w)
    early = local // PAIR - 1
    attn_args = (info, pad_counts, q_aug, k_aug)
    fwd_m = attn_fwd(tokens_in, w_qkv, qv_bias, *attn_args, span=(0, early))
    attn_w = tie(attn_w, fwd_m[1])
    attn_y, attn_core = over_dp(attn_w, Y), over_dp(attn_w, CORE)
    bias_m = tie(qv_bias, attn_w)
    fwd_m = attn_fwd(
        tokens_in, w_qkv, bias_m, *attn_args, span=(early, local // PAIR), into=fwd_m
    )
    attn_core = tie(attn_core, fwd_m[1])
    attn_y = tie(attn_y, attn_core)
    w_qkv_o, w_out_o, qv_bias_o = unpack(
        unpack_attn_kernel,
        info,
        (attn_w, attn_y, attn_core, over_dp(attn_y, CORE)),
        (w_qkv, w_out, qv_bias),
    )
    w_qkvs, w_outs = (w_qkv, w_qkv_o), (w_out, w_out_o)
    up_w = tie(up_w, w_qkv_o)
    up_y = over_dp(up_w, Y)
    bias_o = tie(qv_bias_o, up_w)
    fwd_o = attn_fwd(tokens_in, w_qkv_o, bias_o, *attn_args)
    qkv, ctx, probs, rinv = zip(fwd_m, fwd_o)
    up_core = over_dp(tie(up_w, ctx[1]), CORE)
    mid, xhat, rstd, part, act_m, slope_m = ffn_front(
        ctx, tokens_in, w_outs, vectors, w_up, up_bias, w_down
    )
    up_y = tie(up_y, mid)
    w_up_o, w_down_o, up_bias_o = unpack(
        unpack_ffn_kernel,
        info,
        (up_w, up_y, tie(up_core, mid), over_dp(up_y, CORE)),
        (w_up, w_down, up_bias),
    )
    (
        tokens_out, pooled, act_o, grad_branch, upper_m, upper_o, grad_resid, grad_attended,
        sums, up_sum_m, up_sum_o,
    ) = ffn_back(
        info, pad_counts, mid, xhat, rstd, part, slope_m, cotangent, (w_up, w_up_o),
        (w_down, w_down_o), up_bias_o, vectors,
    )

    def attn_back(h, *after):
        g_att = tie(grad_attended, *after)
        return attn_bwd(tokens_in, g_att, w_outs[h], qkv[h], ctx[h], probs[h], rinv[h])

    def weight_grad(a, b, *after):
        return dot(tie(a, *after), b, TN).astype(BF16)

    def input_grad(h, grad_act, *after):
        return jnp.einsum(
            "cte,cde->td", tie(grad_act, *after), w_qkvs[h], preferred_element_type=F32
        )

    down = Chain(info, [CORE, "x", Y, Z1, Z2])
    up = Chain(info, [CORE, Z1, "x", Y, Z2])
    attn = Chain(info, [CORE, "x", Y, Z1, Z2])
    g = weight_grad(act_o, grad_branch)
    down.send("o", g)
    g = weight_grad(act_m, grad_branch, g)
    down.send("m", g)
    last = down.hop("o", g)
    g = weight_grad(mid, upper_o, last)
    up.send("o", g)
    last = down.hop("m", g)
    g = weight_grad(mid, upper_m, last)
    up.send("m", g)
    last = up.hop("o", g)
    dx_o, g_o, qv_o = attn_back(1, last)
    last = down.hop("m", g_o)
    last = up.hop("m", last)
    last = up.hop("o", last)
    attn.send("o", tie(g_o.reshape(-1, width), last))
    last = attn.hop("o", last)
    dx_m, g_m, qv_m = attn_back(0, last)
    attn.send("m", g_m.reshape(-1, width))
    small, small_send = pack_small(sums, (up_sum_m, up_sum_o), (qv_m, qv_o))
    small_got = over_mp(small_send)
    last = down.hop("m", small)
    last = up.hop("m", last)
    last = up.hop("m", last)
    total = input_grad(1, dx_o, last) + grad_resid
    total = total + input_grad(0, dx_m, last)
    grad_input = total.astype(BF16)
    last = attn.merge(grad_input)
    last = down.hop("m", last)
    last = small = tie(small, last) + small_got
    count, bit = lax.axis_size("dp"), 1
    while bit < count or attn.back or down.back or up.back:
        if bit < count:
            got = over_dp(small, bit)
        for one in (up, attn, down):
            if one.back:
                last = one.hop("m", last)
        if bit < count:
            last = small = tie(small, last) + got
        bit *= 2
    (grad_down,) = place(down.held, down.spots(me), w_down.shape)
    (grad_up,) = place(up.held, up.spots(me), w_up.shape)
    grad_qkv, grad_out = place(attn.held, attn.spots(me), w_qkv.shape, w_out.shape)
    vectors = [small[i] for i in (5, 3, 4, 2, 0, 1)]
    grad_up_bias = small[6:8].reshape(-1)
    grad_qv_bias = small[8].reshape(2, local)
    return (
        tokens_out,
        pooled,
        grad_input,
        grad_qkv,
        grad_qv_bias,
        grad_out,
        vectors[0],
        vectors[1],
        vectors[2],
        grad_up,
        grad_up_bias,
        grad_down,
        vectors[3],
        vectors[4],
        vectors[5],
    )


def solution(mesh):
    token = P(("dp", "mp"), None)
    in_specs = (
        token,
        P("dp", None),
        P("dp"),
        P(None, None, "mp"),
        P(None, "mp"),
        P("mp", None),
        P(),
        P(),
        P(),
        P(None, "mp"),
        P("mp"),
        P("mp", None),
        P(),
        P(),
        P(),
        token,
    )
    out_specs = (
        token,
        token,
        token,
        P(None, None, "mp"),
        P(None, "mp"),
        P("mp", None),
        P(),
        P(),
        P(),
        P(None, "mp"),
        P("mp"),
        P("mp", None),
        P(),
        P(),
        P(),
    )
    return jax.shard_map(shards, mesh=mesh, in_specs=in_specs, out_specs=out_specs, check_vma=False)
```

```python
import functools

import jax
import jax.numpy as jnp
from jax import lax
from jax.experimental import pallas as pl
from jax.experimental.pallas import tpu as pltpu
from jax.sharding import PartitionSpec as P

HD = 64
SEQ = 512
PAIR = 128
EPSILON = 1e-12
SCORE_SCALE = 0.125
GELU_COEF = 0.7978845608028654
LOG2_E = 1.4426950408889634
MASKED = -1e30
F32 = jnp.float32
BF16 = jnp.bfloat16

NT = (((1,), (1,)), ((), ()))
NN = (((1,), (0,)), ((), ()))
TN = (((0,), (0,)), ((), ()))


TILE = 256
HINT = 8.0
VMEM_LIMIT = 56 * 2**20
CORE, Y, Z1, Z2 = 1, 2, 4, 8
SLOT = {CORE: 5, Y: 6, Z1: 7, Z2: 8}


def cost(gflop, size):
    return pl.CostEstimate(
        flops=int(gflop * HINT * 1e9), bytes_accessed=int(size * HINT), transcendentals=0
    )


def dot(a, b, dims=NN):
    return lax.dot_general(a, b, dims, preferred_element_type=F32)


def attn_fwd_kernel(
    info_ref, pad_ref, x_ref, w_ref, bias_ref, qa_ref, ka_ref, qkv_ref, ctx_ref, e_ref, rinv_ref
):
    limit = SEQ - pad_ref[info_ref[4] + pl.program_id(0)]
    w = jnp.concatenate([w_ref[0], w_ref[1], w_ref[2]], axis=1)
    qkv = dot(x_ref[...], w)
    bias = bias_ref[...].astype(F32)
    q = (qkv[:, :PAIR] + bias[0:1]).astype(BF16)
    k = qkv[:, PAIR : 2 * PAIR].astype(BF16)
    v = (qkv[:, 2 * PAIR :] + bias[1:2]).astype(BF16)
    qkv_ref[0], qkv_ref[1], qkv_ref[2] = q, k, v
    v_t = v.astype(F32).T.astype(BF16)
    low = lax.broadcasted_iota(jnp.int32, (SEQ, PAIR), 1) < HD
    j = lax.broadcasted_iota(jnp.int32, (64, SEQ), 0) + (SEQ - 64)
    i = lax.broadcasted_iota(jnp.int32, (64, SEQ), 1)
    seen = (j < limit) | (j == i)
    scores, weights = [], []
    for h in range(2):
        own = low if h == 0 else ~low
        scores.append(dot(jnp.where(own, k, ka_ref[0]), jnp.where(own, q, qa_ref[0]), NT))
    for h in range(2):
        tail = jnp.where(seen, scores[h][SEQ - 64 :], MASKED)
        s = jnp.concatenate([scores[h][: SEQ - 64], tail], axis=0)
        peak = jnp.max(s, axis=0, keepdims=True)
        e = jnp.exp2((s - peak) * (SCORE_SCALE * LOG2_E))
        rinv = 1.0 / jnp.sum(e, axis=0, keepdims=True)
        eb = e.astype(BF16)
        e_ref[h] = eb
        rinv_ref[0, 0, h : h + 1, :] = rinv
        weights.append((eb, rinv))
    parts = [dot(v_t[h * HD : (h + 1) * HD], e) * rinv for h, (e, rinv) in enumerate(weights)]
    ctx_ref[...] = jnp.concatenate(parts, axis=0).T.astype(BF16)


def attn_fwd(tokens, w_qkv, bias, info, pads, q_aug, k_aug, span=None, into=None):
    rows, width = tokens.shape[0] // SEQ, w_qkv.shape[2]
    pairs, model = width // PAIR, tokens.shape[1]
    first, end = span or (0, pairs)
    aug = pl.BlockSpec((1, SEQ, PAIR), lambda r, p, *_: (r, 0, 0))
    into = list(into or ())
    kernel = attn_fwd_kernel
    if into:
        kernel = lambda *refs: attn_fwd_kernel(*refs[:7], *refs[7 + len(into) :])
    return pl.pallas_call(
        kernel,
        grid_spec=pltpu.PrefetchScalarGridSpec(
            num_scalar_prefetch=2,
            grid=(rows, end - first),
            in_specs=[
                pl.BlockSpec((SEQ, model), lambda r, p, *_: (r, 0)),
                pl.BlockSpec((3, model, PAIR), lambda r, p, *_: (0, 0, first + p)),
                pl.BlockSpec((2, PAIR), lambda r, p, *_: (0, first + p)),
                aug,
                aug,
            ]
            + [pl.BlockSpec(memory_space=pl.ANY)] * len(into),
            out_specs=[
                pl.BlockSpec((3, SEQ, PAIR), lambda r, p, *_: (0, r, first + p)),
                pl.BlockSpec((SEQ, PAIR), lambda r, p, *_: (r, first + p)),
                pl.BlockSpec((2, SEQ, SEQ), lambda r, p, *_: (r * pairs + first + p, 0, 0)),
                pl.BlockSpec((1, 1, 2, SEQ), lambda r, p, *_: (r, first + p, 0, 0)),
            ],
        ),
        out_shape=[
            jax.ShapeDtypeStruct((3, rows * SEQ, width), BF16),
            jax.ShapeDtypeStruct((rows * SEQ, width), BF16),
            jax.ShapeDtypeStruct((rows * pairs * 2, SEQ, SEQ), BF16),
            jax.ShapeDtypeStruct((rows, pairs, 2, SEQ), F32),
        ],
        input_output_aliases={7 + i: i for i in range(len(into))},
        compiler_params=pltpu.CompilerParams(vmem_limit_bytes=24 * 2**20),
        cost_estimate=cost(1e-4, 1e3),
        name="attn_fwd",
    )(info, pads, tokens, w_qkv, bias, q_aug, k_aug, *into)


def attn_bwd_kernel(
    info_ref, x_ref, ga_ref, wo_ref, qkv_ref, ctx_ref, e_ref, rinv_ref,
    out_ref, own_ref, away_ref, gb_ref, acc_ref,
):
    row, last = pl.program_id(1), pl.num_programs(1) - 1
    q, k, v = qkv_ref[0], qkv_ref[1], qkv_ref[2]
    k_t = k.astype(F32).T.astype(BF16)
    d_t = dot(wo_ref[...], ga_ref[...], NT).astype(BF16).astype(F32)
    c_t = ctx_ref[...].astype(F32).T
    lane = lax.broadcasted_iota(jnp.int32, (SEQ, PAIR), 1)
    row8 = lax.broadcasted_iota(jnp.int32, (8, SEQ), 0)
    low = lane < HD
    ones = jnp.where((lane & (HD - 1)) < 2, 1.0, 0.0).astype(BF16)
    dv, dk, dq = [], [], []
    for h in range(2):
        own = low if h == 0 else ~low
        rinv = rinv_ref[0, 0, h : h + 1, :]
        mine = d_t[h * HD : (h + 1) * HD] * rinv
        minus = -jnp.sum(mine * c_t[h * HD : (h + 1) * HD], axis=0, keepdims=True)
        high = minus.astype(BF16).astype(F32)
        extra = jnp.where(row8 == 0, high, jnp.where(row8 == 1, minus - high, 0.0))
        blank = jnp.zeros((HD - 8, SEQ), F32)
        stack = [mine, extra, blank] if h == 0 else [extra, blank, mine]
        g_t = jnp.concatenate(stack, axis=0).astype(BF16)
        v_h = jnp.where(own, v, ones)
        e = e_ref[h]
        d = e * dot(v_h, g_t).astype(BF16)
        dv.append(dot(e, g_t, NT))
        dk.append(dot(d, q))
        dq.append(dot(k_t[h * HD : (h + 1) * HD], d))
    dq_t = jnp.concatenate(dq, axis=0) * SCORE_SCALE
    dk = jnp.where(low, dk[0], dk[1]) * SCORE_SCALE
    dv = jnp.where(low, dv[0], dv[1])
    dq_b = dq_t.T.astype(BF16)
    dk_b, dv_b = dk.astype(BF16), dv.astype(BF16)
    out_ref[0], out_ref[1], out_ref[2] = dq_b, dk_b, dv_b
    left = jnp.concatenate([dq_t, dk.T, dv.T], axis=0).astype(BF16)
    g_w = dot(left, x_ref[...]).reshape(3, PAIR, x_ref.shape[1])
    g_o = dot(c_t.astype(BF16), ga_ref[...])
    g_b = jnp.concatenate(
        [
            jnp.sum(dq_b.astype(F32), axis=0, keepdims=True),
            jnp.sum(dv_b.astype(F32), axis=0, keepdims=True),
        ],
        axis=0,
    )

    @pl.when(row == 0)
    def _():
        acc_ref[:3] = g_w
        acc_ref[3] = g_o
        gb_ref[...] = g_b

    @pl.when(row > 0)
    def _():
        acc_ref[:3] += g_w
        acc_ref[3] += g_o
        gb_ref[...] += g_b

    @pl.when(row == last)
    def _():
        core = info_ref[SLOT[CORE]]
        own_ref[...] = acc_ref[pl.ds(2 * core, 2)].astype(BF16)
        away_ref[...] = acc_ref[pl.ds(2 * (1 - core), 2)].astype(BF16)


def attn_bwd(info, tokens, grad_att, w_out, qkv, ctx, e, rinv):
    rows, pairs = rinv.shape[0], rinv.shape[1]
    width, model = qkv.shape[2], tokens.shape[1]
    wide = pl.BlockSpec((SEQ, model), lambda p, r, _: (r, 0))
    triple = pl.BlockSpec((3, SEQ, PAIR), lambda p, r, _: (0, r, p))
    half = pl.BlockSpec((2, PAIR, model), lambda p, r, _: (0, p, 0))
    return pl.pallas_call(
        attn_bwd_kernel,
        grid_spec=pltpu.PrefetchScalarGridSpec(
            num_scalar_prefetch=1,
            grid=(pairs, rows),
            in_specs=[
                wide,
                wide,
                pl.BlockSpec((PAIR, model), lambda p, r, _: (p, 0)),
                triple,
                pl.BlockSpec((SEQ, PAIR), lambda p, r, _: (r, p)),
                pl.BlockSpec((2, SEQ, SEQ), lambda p, r, _: (r * pairs + p, 0, 0)),
                pl.BlockSpec((1, 1, 2, SEQ), lambda p, r, _: (r, p, 0, 0)),
            ],
            out_specs=[
                triple,
                half,
                half,
                pl.BlockSpec((2, PAIR), lambda p, r, _: (0, p)),
            ],
            scratch_shapes=[pltpu.VMEM((4, PAIR, model), F32)],
        ),
        out_shape=[
            jax.ShapeDtypeStruct((3, rows * SEQ, width), BF16),
            jax.ShapeDtypeStruct((2, width, model), BF16),
            jax.ShapeDtypeStruct((2, width, model), BF16),
            jax.ShapeDtypeStruct((2, width), F32),
        ],
        compiler_params=pltpu.CompilerParams(vmem_limit_bytes=56 * 2**20),
        cost_estimate=cost(8 * rows, rows * pairs * 2 * SEQ * SEQ * 2),
        name="attn_bwd",
    )(info, tokens, grad_att, w_out, qkv, ctx, e, rinv)


def vector(x):
    return pl.BlockSpec(memory_space=pltpu.VMEM)


def normalise(v):
    centered = v - jnp.mean(v, axis=-1, keepdims=True)
    rstd = lax.rsqrt(jnp.mean(centered * centered, axis=-1, keepdims=True) + EPSILON)
    return centered * rstd, rstd


def normalise_back(dy, xhat, rstd, gain):
    dg = dy * gain
    return rstd * (
        dg
        - jnp.mean(dg, axis=-1, keepdims=True)
        - xhat * jnp.mean(dg * xhat, axis=-1, keepdims=True)
    )


def gelu_and_slope(u):
    u2 = u * u
    t = jnp.tanh(u * (GELU_COEF + (GELU_COEF * 0.044715) * u2))
    half = 0.5 + 0.5 * t
    act = u * half
    slope = half * (1.0 + u * (1.0 - t) * (GELU_COEF + (3 * GELU_COEF * 0.044715) * u2))
    return act, slope


def flat_bias(ref):
    b = ref[...].astype(F32)
    return jnp.concatenate([b[i : i + 1] for i in range(b.shape[0])], axis=1)


def by_core(core, x, ref):
    half = x.shape[1] // 2
    ref[core] = x[:, :half]
    ref[1 - core] = x[:, half:]


def units(core, mid, acc, wu_ref, ub_ref, wd_ref, act_ref, slope_ref):
    act, slope = gelu_and_slope(dot(mid, wu_ref[...]) + flat_bias(ub_ref))
    act = act.astype(BF16)
    by_core(core, act, act_ref)
    slope_ref[...] = slope.astype(BF16)
    return acc + dot(act, wd_ref[...])


def ffn_front_kernel(
    info_ref, cm_ref, co_ref, x_ref, wm_ref, wo_ref, vec_ref, wu_ref, ub_ref, wd_ref,
    mid_ref, xhat_ref, rstd_ref, part_ref, act_ref, slope_ref,
):
    vec = vec_ref[...].astype(F32)
    attended = dot(cm_ref[...], wm_ref[...]) + dot(co_ref[...], wo_ref[...])
    resid = x_ref[...].astype(F32) + (attended + vec[0:1])
    xhat, rstd = normalise(resid)
    normed = xhat * vec[1:2] + vec[2:3]
    mid = normed.astype(BF16)
    mid_ref[...] = mid
    xhat_ref[...] = xhat
    rstd_ref[...] = rstd
    part_ref[...] = units(
        info_ref[SLOT[CORE]], mid, normed + vec[3:4], wu_ref, ub_ref, wd_ref,
        act_ref, slope_ref,
    )


def halves(hidden, n=None):
    if n is None:
        return pl.BlockSpec((2, TILE, hidden // 2), lambda t, *_: (0, t, 0))
    return jax.ShapeDtypeStruct((2, n, hidden // 2), BF16)


def ffn_front(info, ctx, tokens, w_outs, vectors, w_up, up_bias, w_down):
    n, model = tokens.shape
    width, hidden = ctx[0].shape[1], w_up.shape[1]
    row = lambda c: pl.BlockSpec((TILE, c), lambda t, *_: (t, 0))
    shape = lambda c, d: jax.ShapeDtypeStruct((n, c), d)
    fixed = [vectors, w_up, up_bias, w_down]
    outs = [(model, BF16), (model, F32), (1, F32), (model, F32)]
    return pl.pallas_call(
        ffn_front_kernel,
        grid_spec=pltpu.PrefetchScalarGridSpec(
            num_scalar_prefetch=1,
            grid=(n // TILE,),
            in_specs=[row(width), row(width), row(model)] + [vector(a) for a in (*w_outs, *fixed)],
            out_specs=[row(c) for c, _ in outs] + [halves(hidden), row(hidden)],
        ),
        out_shape=[shape(*o) for o in outs] + [halves(hidden, n), shape(hidden, BF16)],
        compiler_params=pltpu.CompilerParams(vmem_limit_bytes=48 * 2**20),
        cost_estimate=cost(10, n * model * 24),
        name="ffn_front",
    )(info, *ctx, tokens, *w_outs, *fixed)


def ffn_back_kernel(
    info_ref, pad_ref, mid_ref, xhat_ref, rstd_ref, part_ref, slope_m_ref, cot_ref,
    wu_m_ref, wd_m_ref, wu_o_ref, ub_o_ref, wd_o_ref, vec_ref,
    out_ref, pool_ref, act_ref, branch_ref, um_ref, uo_ref, resid_ref, att_ref, sums_ref, ub_m_sum_ref, ub_o_sum_ref, slope_ref,
):
    t = pl.program_id(0)
    per_row = SEQ // TILE
    mid = mid_ref[...]
    core = info_ref[SLOT[CORE]]
    second = units(
        core, mid, part_ref[...], wu_o_ref, ub_o_ref, wd_o_ref, act_ref, slope_ref
    )
    vec = vec_ref[...].astype(F32)
    gain_two = vec[4:5]
    xhat_two, rstd_two = normalise(second)
    final = xhat_two * gain_two + vec[5:6]
    out_ref[...] = final.astype(BF16)
    count = SEQ - pad_ref[info_ref[4] + t // per_row]
    slot = lax.broadcasted_iota(jnp.int32, (TILE, 1), 0) + (t % per_row) * TILE
    pooled = jnp.sum(jnp.where(slot < count, final, 0.0), axis=0, keepdims=True)
    pooled = pooled / count.astype(F32)
    which = lax.broadcasted_iota(jnp.int32, pool_ref.shape, 0) == t // per_row
    pooled = jnp.where(which, pooled, 0.0)

    dy = cot_ref[...].astype(F32)
    down = lambda v: jnp.sum(v, axis=0, keepdims=True)
    sums = [down(dy * xhat_two), down(dy)]
    second_grad = normalise_back(dy, xhat_two, rstd_two, gain_two)
    branch = second_grad.astype(BF16)
    branch_ref[...] = branch
    sums.append(down(branch.astype(F32)))
    normed_grad = second_grad
    bias_sums = []
    for wu_ref, wd_ref, s_ref, up_ref in (
        (wu_o_ref, wd_o_ref, slope_ref, uo_ref),
        (wu_m_ref, wd_m_ref, slope_m_ref, um_ref),
    ):
        upper = (dot(branch, wd_ref[...], NT) * s_ref[...].astype(F32)).astype(BF16)
        by_core(core, upper, up_ref)
        bias_sums.append(down(upper.astype(F32)))
        normed_grad = normed_grad + dot(upper, wu_ref[...], NT)
    xhat_one = xhat_ref[...]
    sums += [down(normed_grad * xhat_one), down(normed_grad)]
    resid = normalise_back(normed_grad, xhat_one, rstd_ref[...], vec[1:2])
    resid_ref[...] = resid
    att = resid.astype(BF16)
    att_ref[...] = att
    sums.append(down(att.astype(F32)))
    sums = jnp.concatenate(sums, axis=0)

    @pl.when(t == 0)
    def _():
        pool_ref[...] = pooled
        sums_ref[...] = sums
        ub_o_sum_ref[...] = bias_sums[0]
        ub_m_sum_ref[...] = bias_sums[1]

    @pl.when(t > 0)
    def _():
        pool_ref[...] += pooled
        sums_ref[...] += sums
        ub_o_sum_ref[...] += bias_sums[0]
        ub_m_sum_ref[...] += bias_sums[1]


def ffn_back(info, pads, mid, xhat, rstd, part, slope, cot, w_ups, w_downs, up_bias_o, vectors):
    n, model = mid.shape
    hidden, rows = slope.shape[1], n // SEQ
    row = lambda c: pl.BlockSpec((TILE, c), lambda t, *_: (t, 0))
    keep = lambda r, c: pl.BlockSpec((r, c), lambda t, *_: (0, 0))
    shape = lambda c, d: jax.ShapeDtypeStruct((n, c), d)
    fixed = [w_ups[0], w_downs[0], w_ups[1], up_bias_o, w_downs[1], vectors]
    return pl.pallas_call(
        ffn_back_kernel,
        grid_spec=pltpu.PrefetchScalarGridSpec(
            num_scalar_prefetch=2,
            grid=(n // TILE,),
            in_specs=[row(model), row(model), row(1), row(model), row(hidden), row(model)]
            + [vector(a) for a in fixed],
            out_specs=[row(model), keep(rows, model), halves(hidden), row(model)]
            + [halves(hidden)] * 2
            + [row(model), row(model), keep(6, model), keep(1, hidden), keep(1, hidden)],
            scratch_shapes=[pltpu.VMEM((TILE, hidden), BF16)],
        ),
        out_shape=[
            shape(model, BF16),
            jax.ShapeDtypeStruct((rows, model), F32),
            halves(hidden, n),
            shape(model, BF16),
        ]
        + [halves(hidden, n)] * 2
        + [
            shape(model, F32),
            shape(model, BF16),
            jax.ShapeDtypeStruct((6, model), F32),
            jax.ShapeDtypeStruct((1, hidden), F32),
            jax.ShapeDtypeStruct((1, hidden), F32),
        ],
        compiler_params=pltpu.CompilerParams(vmem_limit_bytes=40 * 2**20),
        cost_estimate=cost(25, n * model * 40),
        name="ffn_back",
    )(info, pads, mid, xhat, rstd, part, slope, cot, *fixed)


def pack_attn_kernel(info_ref, wq_ref, wo_ref, qb_ref, attn_ref):
    r, w = wq_ref.shape[1:]
    attn_ref[:r, :w] = wq_ref[0]
    attn_ref[:r, w:] = wq_ref[1]
    attn_ref[r : r + r // 2, :w] = wq_ref[2, : r // 2]
    attn_ref[r : r + r // 2, w:] = wq_ref[2, r // 2 :]
    at = r + r // 2
    attn_ref[at : at + wo_ref.shape[0], :] = wo_ref[...]
    at += wo_ref.shape[0]
    attn_ref[at:, :] = jnp.zeros((16, 2 * w), BF16)
    attn_ref[at : at + 2, :w] = qb_ref[...]


def pack_ffn_kernel(info_ref, seg_ref, wu_ref, wd_ref, ub_ref, up_ref, down_ref, qa_ref, ka_ref):
    u, c = wu_ref.shape[0], up_ref.shape[1]
    up_ref[:u, :] = wu_ref[:, :c]
    up_ref[u : 2 * u, :] = wu_ref[:, c:]
    up_ref[2 * u :, :] = jnp.zeros((16, c), BF16)
    up_ref[2 * u : 2 * u + 2, :] = ub_ref[...]
    down_ref[...] = wd_ref[...]
    segs = seg_ref.shape[1]
    slot = lax.broadcasted_iota(jnp.int32, (SEQ, PAIR), 0)
    lane = lax.broadcasted_iota(jnp.int32, (SEQ, PAIR), 1) & (HD - 1)
    for row in range(qa_ref.shape[0]):
        end, segment = 0, jnp.zeros((SEQ, PAIR), jnp.int32)
        for s in range(segs):
            end = end + seg_ref[info_ref[4] + row, s]
            segment = segment + jnp.where(slot >= end, 1, 0)
        same = lane == segment
        ka_ref[row] = jnp.where(same & (lane < segs), 1.0, 0.0).astype(BF16)
        qa_ref[row] = jnp.where((lane < segs) & ~same, MASKED, 0.0).astype(BF16)


def pack_attn(info, w_qkv, w_out, qv_bias):
    model, width = w_qkv.shape[1:]
    out_rows = w_out.shape[0] // 4
    shape = (3 * width // 4 + out_rows + 16, model)
    whole = lambda s: pl.BlockSpec(s, lambda i, *_: (0,) * len(s))
    return pl.pallas_call(
        pack_attn_kernel,
        grid_spec=pltpu.PrefetchScalarGridSpec(
            num_scalar_prefetch=1,
            grid=(1,),
            in_specs=[
                pl.BlockSpec((3, model // 4, width), lambda i, at: (0, at[0], 0)),
                pl.BlockSpec((out_rows, model), lambda i, at: (at[0], 0)),
                whole(qv_bias.shape),
            ],
            out_specs=whole(shape),
        ),
        out_shape=jax.ShapeDtypeStruct(shape, BF16),
        cost_estimate=cost(0, 2 * 2**20),
        name="pack_attn",
    )(info, w_qkv, w_out, qv_bias)


def pack_ffn(info, rows, seg_lengths, w_up, w_down, up_bias):
    model = w_up.shape[0]
    up_rows, down_rows = model // 4, w_down.shape[0] // 4
    whole = lambda s: pl.BlockSpec(s, lambda i, *_: (0,) * len(s))
    shapes = [(2 * up_rows + 16, model), (down_rows, model)] + [(rows, SEQ, PAIR)] * 2
    return pl.pallas_call(
        pack_ffn_kernel,
        grid_spec=pltpu.PrefetchScalarGridSpec(
            num_scalar_prefetch=2,
            grid=(1,),
            in_specs=[
                pl.BlockSpec((up_rows, w_up.shape[1]), lambda i, at, _: (at[0], 0)),
                pl.BlockSpec((down_rows, model), lambda i, at, _: (at[9], 0)),
                whole(up_bias.shape),
            ],
            out_specs=[whole(s) for s in shapes],
        ),
        out_shape=[jax.ShapeDtypeStruct(s, BF16) for s in shapes],
        cost_estimate=cost(0, 4 * 2**20),
        name="pack_ffn",
    )(info, seg_lengths, w_up, w_down, up_bias)


def unpack_attn_kernel(at_ref, *refs):
    pieces, (wq_ref, wo_ref, qb_ref) = refs[:4], refs[4:]
    r, w, o = wq_ref.shape[1] // 4, wq_ref.shape[2], wo_ref.shape[0] // 4
    for i, piece in enumerate(pieces):
        q = at_ref[i]
        rows = pl.ds(pl.multiple_of(q * r, 16), r)
        wq_ref[0, rows, :] = piece[:r, :w]
        wq_ref[1, rows, :] = piece[:r, w:]
        wq_ref[2, pl.ds(pl.multiple_of(q * r, 16), r // 2), :] = piece[r : r + r // 2, :w]
        wq_ref[2, pl.ds(pl.multiple_of(q * r + r // 2, 16), r // 2), :] = piece[r : r + r // 2, w:]
        at = r + r // 2
        wo_ref[pl.ds(pl.multiple_of(q * o, 16), o), :] = piece[at : at + o, :]
    at += o
    qb_ref[...] = pieces[0][at : at + 2, :w]


def unpack_ffn_kernel(at_ref, *refs):
    ups, downs, (wu_ref, wd_ref, ub_ref) = refs[:4], refs[4:8], refs[8:]
    r, c, d = wu_ref.shape[0] // 4, wu_ref.shape[1] // 2, wd_ref.shape[0] // 4
    for i in range(4):
        rows = pl.ds(pl.multiple_of(at_ref[i] * r, 16), r)
        wu_ref[rows, :c] = ups[i][:r, :]
        wu_ref[rows, c:] = ups[i][r : 2 * r, :]
        wd_ref[pl.ds(pl.multiple_of(at_ref[9 + i] * d, 16), d), :] = downs[i][...]
    ub_ref[...] = ups[0][2 * r : 2 * r + 2, :]


def unpack(kernel, at, pieces, like):
    whole = pl.BlockSpec(memory_space=pltpu.VMEM)
    return pl.pallas_call(
        kernel,
        in_specs=[pl.BlockSpec(memory_space=pltpu.SMEM)] + [whole] * len(pieces),
        out_specs=[whole] * len(like),
        out_shape=[pltpu.VMEM(a.shape, BF16) for a in like],
        compiler_params=pltpu.CompilerParams(vmem_limit_bytes=32 * 2**20),
        cost_estimate=cost(0, 5 * 2**20),
        name=kernel.__name__,
    )(at, *pieces)


def over_mp(x):
    n = lax.axis_size("mp")
    return lax.ppermute(x, "mp", [(i, i ^ 1) for i in range(n)])


def over_dp(x, bit):
    n = lax.axis_size("dp")
    return lax.ppermute(x, "dp", [(i, i ^ bit) for i in range(n)])


def gather_pieces(rows, at_ref, refs, store):
    k = 0
    for ref in refs:
        for i in range(ref.shape[0] // rows):
            spot = pl.ds(pl.multiple_of(at_ref[k] * rows, 16), rows)
            store(spot, ref[i * rows : (i + 1) * rows, :].astype(F32))
            k += 1


def place_kernel(rows, at_ref, *refs):
    out_ref = refs[-1]

    def store(spot, value):
        out_ref[spot, :] = value

    gather_pieces(rows, at_ref, refs[:-1], store)


def place_up_kernel(rows, at_ref, *refs):
    out_ref = refs[-1]
    height, width = out_ref.shape[0], out_ref.shape[1] // 2
    k = 0
    for ref in refs[:-1]:
        for i in range(ref.shape[0] // rows):
            place, count = at_ref[k], height // rows
            spot = pl.ds(pl.multiple_of(place % count * rows, 16), rows)
            columns = pl.ds(pl.multiple_of(place // count * width, 128), width)
            out_ref[spot, columns] = ref[i * rows : (i + 1) * rows, :].astype(F32)
            k += 1


def place_attn_kernel(rows, at_ref, *refs):
    qkv_ref, out_ref, held_ref = refs[-3:]

    def store(spot, value):
        held_ref[spot, :] = value

    gather_pieces(rows, at_ref, refs[:-3], store)
    width = qkv_ref.shape[2]
    for c in range(3):
        for e in range(0, width, PAIR):
            qkv_ref[c, :, e : e + PAIR] = held_ref[c * width + e : c * width + e + PAIR, :].T
    out_ref[...] = held_ref[3 * width :, :]


def place(kernel, pieces, at, *shapes):
    total, cols = sum(piece.shape[0] for piece in pieces), pieces[0].shape[1]
    whole = pl.BlockSpec(memory_space=pltpu.VMEM)
    return pl.pallas_call(
        functools.partial(kernel, total // at.shape[0]),
        in_specs=[pl.BlockSpec(memory_space=pltpu.SMEM)] + [whole] * len(pieces),
        out_specs=[whole] * len(shapes),
        out_shape=[jax.ShapeDtypeStruct(s, F32) for s in shapes],
        scratch_shapes=[] if len(shapes) == 1 else [pltpu.VMEM((total, cols), F32)],
        compiler_params=pltpu.CompilerParams(vmem_limit_bytes=32 * 2**20),
        cost_estimate=cost(0, 6 * total * cols),
        name=kernel.__name__,
    )(at, *pieces)


def tie(x, *after):
    return lax.optimization_barrier((x,) + after)[0]


def land(info, x, got, own=None, step=None):
    n = got.shape[0]
    if own is not None:
        x = lax.dynamic_slice_in_dim(x, info[own] * n, n, 0)
    total = (x.astype(F32) + got.astype(F32)).astype(BF16)
    if step is None:
        return total
    return total, lax.dynamic_slice_in_dim(total, (1 - info[step]) * (n // 2), n // 2, 0)


def arrive(after, *flights):
    held = [c.crossed if part == "x" else c.got[part] for c, part in flights]
    held = lax.optimization_barrier((*held, after))
    for (c, part), got in zip(flights, held):
        if part == "x":
            c.crossed = got
        else:
            c.got[part] = got


class Chain:
    def __init__(self, info, bits):
        self.info, self.bits = info, bits
        self.dp_bits = [b for b in bits if b != "x"]
        self.order = [0]
        for b in reversed(self.dp_bits):
            self.order += [o ^ b for o in self.order]
        self.x, self.got, self.own, self.at = {}, {}, {}, {}
        self.held, self.back = None, list(reversed(self.dp_bits))

    def send(self, part, own, away):
        self.got[part] = over_dp(away, self.bits[0])
        self.x[part], self.own[part], self.at[part] = own, None, 0

    def hop(self, part="m", *after):
        if self.held is not None:
            return self.double(*after)
        x, at = tie(self.x[part], *after), self.at[part]
        got = self.crossed if self.bits[at] == "x" else self.got[part]
        bit = self.bits[at + 1] if at + 1 < len(self.bits) else None
        self.at[part] = at + 1
        if bit is None or bit == "x":
            x = land(self.info, x, got, self.own[part])
            self.x[part], self.own[part] = x, None
            if bit is None:
                bit = 2 * max(self.dp_bits)
                while bit < lax.axis_size("dp"):
                    x = land(self.info, x, over_dp(x, bit))
                    bit *= 2
                self.held = [x]
                self.double()
            elif part == "o":
                self.crossed = over_mp(x)
            return x
        x, away = land(self.info, x, got, self.own[part], SLOT[bit])
        self.x[part], self.own[part], self.got[part] = x, SLOT[bit], over_dp(away, bit)
        return x

    def double(self, *after):
        full = jnp.concatenate(self.held, axis=0) if len(self.held) > 1 else self.held[0]
        full = tie(full, *after)
        self.held.append(over_dp(full, self.back.pop(0)))
        return full

    def spots(self, me):
        who = me ^ jnp.array(self.order, jnp.int32)
        spot = jnp.zeros_like(who)
        for b in self.dp_bits:
            spot = 2 * spot + (who & b) // b
        return spot


def pack_small_kernel(sums_ref, um_ref, uo_ref, qm_ref, qo_ref, keep_ref, send_ref):
    n, c, w = sums_ref.shape[0], sums_ref.shape[1], qm_ref.shape[1]
    for out_ref, u_ref, q_ref in ((keep_ref, um_ref, qm_ref), (send_ref, uo_ref, qo_ref)):
        out_ref[...] = jnp.zeros(out_ref.shape, F32)
        out_ref[:n, :] = sums_ref[...]
        for i in range(u_ref.shape[1] // c):
            out_ref[n + i : n + i + 1, :] = u_ref[:, i * c : (i + 1) * c]
        at = n + u_ref.shape[1] // c
        for i in range(2):
            out_ref[at : at + 1, i * w : (i + 1) * w] = q_ref[i : i + 1, :]


def pack_small(sums, up_sums, qv_sums):
    shape = jax.ShapeDtypeStruct((16, sums.shape[1]), F32)
    return pl.pallas_call(
        pack_small_kernel, out_shape=[shape, shape], cost_estimate=cost(0, 2**18), name="pack_small"
    )(sums, *up_sums, *qv_sums)


def shards(
    tokens_in,
    seg_lengths,
    pad_counts,
    w_qkv,
    qv_bias,
    w_out,
    out_bias,
    norm1_gain,
    norm1_bias,
    w_up,
    up_bias,
    w_down,
    down_bias,
    norm2_gain,
    norm2_bias,
    cotangent,
):
    tokens, width = tokens_in.shape
    local = w_qkv.shape[2]
    me = lax.axis_index("dp")
    rows_here = tokens // SEQ
    slot = jnp.arange(13, dtype=jnp.int32)
    start = lax.axis_index("mp") * rows_here
    quarters = jnp.array([0, 2, 1, 3, 0, 0, 0, 0, 0, 0, 2, 1, 3], jnp.int32)
    quarters = quarters ^ jnp.where(slot < 4, me & 3, (me & CORE) | ((me & Z1) // 2))
    bits = jnp.where(slot == 4, start, (me >> jnp.clip(slot - 5, 0, 3)) & 1)
    info = jnp.where((slot < 4) | (slot > 8), quarters, bits)
    vectors = jnp.stack([out_bias, norm1_gain, norm1_bias, down_bias, norm2_gain, norm2_bias])
    up_bias = up_bias.reshape(-1, width)

    attn_w = pack_attn(info, w_qkv, w_out, qv_bias)
    up_w, down_w, q_aug, k_aug = pack_ffn(
        info, rows_here, seg_lengths, w_up, w_down, tie(up_bias, attn_w)
    )
    attn_w, up_w, down_w = over_mp(attn_w), over_mp(up_w), over_mp(down_w)
    early = local // PAIR - 1
    attn_args = (info, pad_counts, q_aug, k_aug)
    fwd_m = attn_fwd(tokens_in, w_qkv, qv_bias, *attn_args, span=(0, early))
    attn_w = tie(attn_w, fwd_m[1])
    attn_y, attn_core = over_dp(attn_w, Y), over_dp(attn_w, CORE)
    bias_m = tie(qv_bias, attn_w)
    fwd_m = attn_fwd(
        tokens_in, w_qkv, bias_m, *attn_args, span=(early, local // PAIR), into=fwd_m
    )
    up_w = tie(up_w, fwd_m[1])
    up_y = over_dp(up_w, Y)
    attn_core = tie(attn_core, up_w)
    attn_y = tie(attn_y, attn_core)
    w_qkv_o, w_out_o, qv_bias_o = unpack(
        unpack_attn_kernel,
        info,
        (attn_w, attn_y, attn_core, over_dp(attn_y, CORE)),
        (w_qkv, w_out, qv_bias),
    )
    w_qkvs, w_outs = (w_qkv, w_qkv_o), (w_out, w_out_o)
    fwd_o = attn_fwd(tokens_in, w_qkv_o, qv_bias_o, *attn_args)
    qkv, ctx, probs, rinv = zip(fwd_m, fwd_o)
    down_w, up_y, up_w = lax.optimization_barrier((down_w, up_y, up_w, ctx[1]))[:3]
    down_z = over_dp(down_w, Z1)
    up_core, up_both, down_core = over_dp(up_w, CORE), over_dp(up_y, CORE), over_dp(down_w, CORE)
    mid, xhat, rstd, part, act_m, slope_m = ffn_front(
        info, (ctx[0], tie(ctx[1], down_w)), tokens_in, w_outs, vectors, w_up, up_bias, w_down
    )
    down_z, up_core, up_both, down_core = lax.optimization_barrier(
        (down_z, up_core, up_both, down_core, mid)
    )[:4]
    w_up_o, w_down_o, up_bias_o = unpack(
        unpack_ffn_kernel,
        info,
        (up_w, up_y, up_core, up_both, down_w, down_z, down_core, over_dp(down_z, CORE)),
        (w_up, w_down, up_bias),
    )
    (
        tokens_out, pooled, act_o, grad_branch, upper_m, upper_o, grad_resid, grad_attended,
        sums, up_sum_m, up_sum_o,
    ) = ffn_back(
        info, pad_counts, mid, xhat, rstd, part, slope_m, cotangent, (w_up, w_up_o),
        (w_down, w_down_o), up_bias_o, vectors,
    )

    down = Chain(info, [CORE, "x", Z1, Y, Z2])
    up = Chain(info, [CORE, "x", Z1, Y, Z2])
    attn = Chain(info, [CORE, Y, "x", Z1, Z2])

    def attn_back(h, *after):
        g_att = tie(grad_attended, *after)
        dx, own, away, qv = attn_bwd(
            info, tokens_in, g_att, w_outs[h], qkv[h], ctx[h], probs[h], rinv[h]
        )
        return dx, own.reshape(-1, width), away.reshape(-1, width), qv

    def weight_grad(a, b, *after):
        return dot(tie(a, *after), b, TN).astype(BF16)

    def input_grad(h, grad_act, *after):
        return jnp.einsum(
            "cte,cde->td", tie(grad_act, *after), w_qkvs[h], preferred_element_type=F32
        )

    away = weight_grad(act_o[1], grad_branch)
    own = weight_grad(act_o[0], grad_branch, away)
    down.send("o", own, away)
    away = weight_grad(act_m[1], grad_branch, own)
    last = down.hop("o", away)
    own = weight_grad(act_m[0], grad_branch, last)
    down.send("m", own, away)
    away = weight_grad(mid, upper_o[1], own)
    own = weight_grad(mid, upper_o[0], away)
    up.send("o", own, away)
    last = down.hop("m", own)
    away = weight_grad(mid, upper_m[1], last)
    last = up.hop("o", away)
    own = weight_grad(mid, upper_m[0], last)
    up.send("m", own, away)
    dx_o, own, away, qv_o = attn_back(1, own)
    attn.send("o", own, away)
    last = up.hop("m", own)
    last = down.hop("m", last)
    last = attn.hop("o", last)
    dx_m, own, away, qv_m = attn_back(0, last)
    attn.send("m", own, away)
    small, small_send = pack_small(sums, (up_sum_m, up_sum_o), (qv_m, qv_o))
    last = down.hop("m", small)
    last = attn.hop("o", last)
    last = up.hop("m", last)
    last = attn.hop("m", last)
    small_got = over_mp(tie(small_send, last))
    count, bit = lax.axis_size("dp"), 1
    for what in "duadsaudsaudsaudsausgaupa":
        if what == "s":
            last = small = tie(small, last) + small_got
            if bit < count:
                small_got = over_dp(small, bit)
                bit *= 2
        elif what == "g":
            total = input_grad(1, dx_o, last) + grad_resid
            total = total + input_grad(0, dx_m, last)
            grad_input = last = total.astype(BF16)
        elif what == "p":
            down.held[0] = tie(down.held[0], last)
            (grad_down,) = place(place_kernel, down.held, down.spots(me), w_down.shape)
            last = grad_down
        else:
            last = {"d": down, "u": up, "a": attn}[what].hop("m", last)
    if bit > 16:
        small = small + small_got
    while bit < count:
        small = small + over_dp(small, bit)
        bit *= 2
    (grad_up,) = place(place_up_kernel, up.held, up.spots(me), w_up.shape)
    grad_qkv, grad_out = place(
        place_attn_kernel, attn.held, attn.spots(me), w_qkv.shape, w_out.shape
    )
    vectors = [small[i] for i in (5, 3, 4, 2, 0, 1)]
    grad_up_bias = small[6:8].reshape(-1)
    grad_qv_bias = small[8].reshape(2, local)
    return (
        tokens_out,
        pooled,
        grad_input,
        grad_qkv,
        grad_qv_bias,
        grad_out,
        vectors[0],
        vectors[1],
        vectors[2],
        grad_up,
        grad_up_bias,
        grad_down,
        vectors[3],
        vectors[4],
        vectors[5],
    )


def solution(mesh):
    token = P(("dp", "mp"), None)
    in_specs = (
        token,
        P("dp", None),
        P("dp"),
        P(None, None, "mp"),
        P(None, "mp"),
        P("mp", None),
        P(),
        P(),
        P(),
        P(None, "mp"),
        P("mp"),
        P("mp", None),
        P(),
        P(),
        P(),
        token,
    )
    out_specs = (
        token,
        token,
        token,
        P(None, None, "mp"),
        P(None, "mp"),
        P("mp", None),
        P(),
        P(),
        P(),
        P(None, "mp"),
        P("mp"),
        P("mp", None),
        P(),
        P(),
        P(),
    )
    return jax.shard_map(shards, mesh=mesh, in_specs=in_specs, out_specs=out_specs, check_vma=False)
```

```python
import functools

import jax
import jax.numpy as jnp
from jax import lax
from jax.experimental import pallas as pl
from jax.experimental.pallas import tpu as pltpu
from jax.sharding import PartitionSpec as P

HD = 64
SEQ = 512
PAIR = 128
EPSILON = 1e-12
SCORE_SCALE = 0.125
GELU_COEF = 0.7978845608028654
LOG2_E = 1.4426950408889634
MASKED = -1e30
F32 = jnp.float32
BF16 = jnp.bfloat16

NT = (((1,), (1,)), ((), ()))
NN = (((1,), (0,)), ((), ()))
TN = (((0,), (0,)), ((), ()))


TILE = 256
HINT = 8.0
VMEM_LIMIT = 56 * 2**20
CORE, Y, Z1, Z2 = 1, 2, 4, 8
SLOT = {CORE: 5, Y: 6, Z1: 7, Z2: 8}


def cost(gflop, size):
    return pl.CostEstimate(
        flops=int(gflop * HINT * 1e9), bytes_accessed=int(size * HINT), transcendentals=0
    )


def dot(a, b, dims=NN):
    return lax.dot_general(a, b, dims, preferred_element_type=F32)


def attn_fwd_kernel(
    info_ref, pad_ref, x_ref, w_ref, bias_ref, qa_ref, ka_ref, qkv_ref, ctx_ref, e_ref, rinv_ref
):
    limit = SEQ - pad_ref[info_ref[4] + pl.program_id(0)]
    w = jnp.concatenate([w_ref[0], w_ref[1], w_ref[2]], axis=1)
    qkv = dot(x_ref[...], w)
    bias = bias_ref[...].astype(F32)
    q = (qkv[:, :PAIR] + bias[0:1]).astype(BF16)
    k = qkv[:, PAIR : 2 * PAIR].astype(BF16)
    v = (qkv[:, 2 * PAIR :] + bias[1:2]).astype(BF16)
    qkv_ref[0], qkv_ref[1], qkv_ref[2] = q, k, v
    v_t = v.astype(F32).T.astype(BF16)
    low = lax.broadcasted_iota(jnp.int32, (SEQ, PAIR), 1) < HD
    j = lax.broadcasted_iota(jnp.int32, (64, SEQ), 0) + (SEQ - 64)
    i = lax.broadcasted_iota(jnp.int32, (64, SEQ), 1)
    seen = (j < limit) | (j == i)
    scores, weights = [], []
    for h in range(2):
        own = low if h == 0 else ~low
        scores.append(dot(jnp.where(own, k, ka_ref[0]), jnp.where(own, q, qa_ref[0]), NT))
    for h in range(2):
        tail = jnp.where(seen, scores[h][SEQ - 64 :], MASKED)
        s = jnp.concatenate([scores[h][: SEQ - 64], tail], axis=0)
        peak = jnp.max(s, axis=0, keepdims=True)
        e = jnp.exp2((s - peak) * (SCORE_SCALE * LOG2_E))
        rinv = 1.0 / jnp.sum(e, axis=0, keepdims=True)
        eb = e.astype(BF16)
        e_ref[h] = eb
        rinv_ref[0, 0, h : h + 1, :] = rinv
        weights.append((eb, rinv))
    parts = [dot(v_t[h * HD : (h + 1) * HD], e) * rinv for h, (e, rinv) in enumerate(weights)]
    ctx_ref[...] = jnp.concatenate(parts, axis=0).T.astype(BF16)


def attn_fwd(tokens, w_qkv, bias, info, pads, q_aug, k_aug, span=None, into=None):
    rows, width = tokens.shape[0] // SEQ, w_qkv.shape[2]
    pairs, model = width // PAIR, tokens.shape[1]
    first, end = span or (0, pairs)
    aug = pl.BlockSpec((1, SEQ, PAIR), lambda r, p, *_: (r, 0, 0))
    into = list(into or ())
    kernel = attn_fwd_kernel
    if into:
        kernel = lambda *refs: attn_fwd_kernel(*refs[:7], *refs[7 + len(into) :])
    return pl.pallas_call(
        kernel,
        grid_spec=pltpu.PrefetchScalarGridSpec(
            num_scalar_prefetch=2,
            grid=(rows, end - first),
            in_specs=[
                pl.BlockSpec((SEQ, model), lambda r, p, *_: (r, 0)),
                pl.BlockSpec((3, model, PAIR), lambda r, p, *_: (0, 0, first + p)),
                pl.BlockSpec((2, PAIR), lambda r, p, *_: (0, first + p)),
                aug,
                aug,
            ]
            + [pl.BlockSpec(memory_space=pl.ANY)] * len(into),
            out_specs=[
                pl.BlockSpec((3, SEQ, PAIR), lambda r, p, *_: (0, r, first + p)),
                pl.BlockSpec((SEQ, PAIR), lambda r, p, *_: (r, first + p)),
                pl.BlockSpec((2, SEQ, SEQ), lambda r, p, *_: (r * pairs + first + p, 0, 0)),
                pl.BlockSpec((1, 1, 2, SEQ), lambda r, p, *_: (r, first + p, 0, 0)),
            ],
        ),
        out_shape=[
            pltpu.HBM((3, rows * SEQ, width), BF16),
            jax.ShapeDtypeStruct((rows * SEQ, width), BF16),
            pltpu.HBM((rows * pairs * 2, SEQ, SEQ), BF16),
            jax.ShapeDtypeStruct((rows, pairs, 2, SEQ), F32),
        ],
        input_output_aliases={7 + i: i for i in range(len(into))},
        compiler_params=pltpu.CompilerParams(vmem_limit_bytes=24 * 2**20),
        cost_estimate=cost(1e-4, 1e3),
        name="attn_fwd",
    )(info, pads, tokens, w_qkv, bias, q_aug, k_aug, *into)


def attn_bwd_kernel(
    info_ref, x_ref, ga_ref, wo_ref, qkv_ref, ctx_ref, e_ref, rinv_ref,
    out_ref, own_ref, away_ref, gb_ref, acc_ref,
):
    row, last = pl.program_id(1), pl.num_programs(1) - 1
    q, k, v = qkv_ref[0], qkv_ref[1], qkv_ref[2]
    k_t = k.astype(F32).T.astype(BF16)
    d_t = dot(wo_ref[...], ga_ref[...], NT).astype(BF16).astype(F32)
    c_t = ctx_ref[...].astype(F32).T
    lane = lax.broadcasted_iota(jnp.int32, (SEQ, PAIR), 1)
    row8 = lax.broadcasted_iota(jnp.int32, (8, SEQ), 0)
    low = lane < HD
    ones = jnp.where((lane & (HD - 1)) < 2, 1.0, 0.0).astype(BF16)
    dv, dk, dq = [], [], []
    for h in range(2):
        own = low if h == 0 else ~low
        rinv = rinv_ref[0, 0, h : h + 1, :]
        mine = d_t[h * HD : (h + 1) * HD] * rinv
        minus = -jnp.sum(mine * c_t[h * HD : (h + 1) * HD], axis=0, keepdims=True)
        high = minus.astype(BF16).astype(F32)
        extra = jnp.where(row8 == 0, high, jnp.where(row8 == 1, minus - high, 0.0))
        blank = jnp.zeros((HD - 8, SEQ), F32)
        stack = [mine, extra, blank] if h == 0 else [extra, blank, mine]
        g_t = jnp.concatenate(stack, axis=0).astype(BF16)
        v_h = jnp.where(own, v, ones)
        e = e_ref[h]
        d = e * dot(v_h, g_t).astype(BF16)
        dv.append(dot(e, g_t, NT))
        dk.append(dot(d, q))
        dq.append(dot(k_t[h * HD : (h + 1) * HD], d))
    dq_t = jnp.concatenate(dq, axis=0) * SCORE_SCALE
    dk = jnp.where(low, dk[0], dk[1]) * SCORE_SCALE
    dv = jnp.where(low, dv[0], dv[1])
    dq_b = dq_t.T.astype(BF16)
    dk_b, dv_b = dk.astype(BF16), dv.astype(BF16)
    out_ref[0], out_ref[1], out_ref[2] = dq_b, dk_b, dv_b
    left = jnp.concatenate([dq_t, dk.T, dv.T], axis=0).astype(BF16)
    g_w = dot(left, x_ref[...]).reshape(3, PAIR, x_ref.shape[1])
    g_o = dot(c_t.astype(BF16), ga_ref[...])
    g_b = jnp.concatenate(
        [
            jnp.sum(dq_b.astype(F32), axis=0, keepdims=True),
            jnp.sum(dv_b.astype(F32), axis=0, keepdims=True),
        ],
        axis=0,
    )

    @pl.when(row == 0)
    def _():
        acc_ref[:3] = g_w
        acc_ref[3] = g_o
        gb_ref[...] = g_b

    @pl.when(row > 0)
    def _():
        acc_ref[:3] += g_w
        acc_ref[3] += g_o
        gb_ref[...] += g_b

    @pl.when(row == last)
    def _():
        core = info_ref[SLOT[CORE]]
        own_ref[...] = acc_ref[pl.ds(2 * core, 2)].astype(BF16)
        away_ref[...] = acc_ref[pl.ds(2 * (1 - core), 2)].astype(BF16)


def attn_bwd(info, tokens, grad_att, w_out, qkv, ctx, e, rinv):
    rows, pairs = rinv.shape[0], rinv.shape[1]
    width, model = qkv.shape[2], tokens.shape[1]
    wide = pl.BlockSpec((SEQ, model), lambda p, r, _: (r, 0))
    triple = pl.BlockSpec((3, SEQ, PAIR), lambda p, r, _: (0, r, p))
    half = pl.BlockSpec((2, PAIR, model), lambda p, r, _: (0, p, 0))
    return pl.pallas_call(
        attn_bwd_kernel,
        grid_spec=pltpu.PrefetchScalarGridSpec(
            num_scalar_prefetch=1,
            grid=(pairs, rows),
            in_specs=[
                wide,
                wide,
                pl.BlockSpec((PAIR, model), lambda p, r, _: (p, 0)),
                triple,
                pl.BlockSpec((SEQ, PAIR), lambda p, r, _: (r, p)),
                pl.BlockSpec((2, SEQ, SEQ), lambda p, r, _: (r * pairs + p, 0, 0)),
                pl.BlockSpec((1, 1, 2, SEQ), lambda p, r, _: (r, p, 0, 0)),
            ],
            out_specs=[
                triple,
                half,
                half,
                pl.BlockSpec((2, PAIR), lambda p, r, _: (0, p)),
            ],
            scratch_shapes=[pltpu.VMEM((4, PAIR, model), F32)],
        ),
        out_shape=[
            pltpu.HBM((3, rows * SEQ, width), BF16),
            pltpu.HBM((2, width, model), BF16),
            pltpu.HBM((2, width, model), BF16),
            jax.ShapeDtypeStruct((2, width), F32),
        ],
        compiler_params=pltpu.CompilerParams(vmem_limit_bytes=24 * 2**20),
        cost_estimate=cost(8 * rows, rows * pairs * 2 * SEQ * SEQ * 2),
        name="attn_bwd",
    )(info, tokens, grad_att, w_out, qkv, ctx, pltpu.with_memory_space_constraint(e, pltpu.HBM), rinv)


def vector(x):
    return pl.BlockSpec(x.shape, lambda *_: (0,) * x.ndim)


def normalise(v):
    centered = v - jnp.mean(v, axis=-1, keepdims=True)
    rstd = lax.rsqrt(jnp.mean(centered * centered, axis=-1, keepdims=True) + EPSILON)
    return centered * rstd, rstd


def normalise_back(dy, xhat, rstd, gain):
    dg = dy * gain
    return rstd * (
        dg
        - jnp.mean(dg, axis=-1, keepdims=True)
        - xhat * jnp.mean(dg * xhat, axis=-1, keepdims=True)
    )


def gelu_and_slope(u):
    u2 = u * u
    t = jnp.tanh(u * (GELU_COEF + (GELU_COEF * 0.044715) * u2))
    half = 0.5 + 0.5 * t
    act = u * half
    slope = half * (1.0 + u * (1.0 - t) * (GELU_COEF + (3 * GELU_COEF * 0.044715) * u2))
    return act, slope


def flat_bias(ref):
    b = ref[...].astype(F32)
    return jnp.concatenate([b[i : i + 1] for i in range(b.shape[0])], axis=1)


def by_core(core, x, ref):
    half = x.shape[1] // 2
    ref[core] = x[:, :half]
    ref[1 - core] = x[:, half:]


def units(core, mid, acc, wu_ref, ub_ref, wd_ref, act_ref, slope_ref):
    act, slope = gelu_and_slope(dot(mid, wu_ref[...]) + flat_bias(ub_ref))
    act = act.astype(BF16)
    by_core(core, act, act_ref)
    slope_ref[...] = slope.astype(BF16)
    return acc + dot(act, wd_ref[...])


def ffn_front_kernel(
    info_ref, cm_ref, co_ref, x_ref, wm_ref, wo_ref, vec_ref, wu_ref, ub_ref, wd_ref,
    mid_ref, xhat_ref, rstd_ref, part_ref, act_ref, slope_ref,
):
    vec = vec_ref[...].astype(F32)
    attended = dot(cm_ref[...], wm_ref[...]) + dot(co_ref[...], wo_ref[...])
    resid = x_ref[...].astype(F32) + (attended + vec[0:1])
    xhat, rstd = normalise(resid)
    normed = xhat * vec[1:2] + vec[2:3]
    mid = normed.astype(BF16)
    mid_ref[...] = mid
    xhat_ref[...] = xhat
    rstd_ref[...] = rstd
    part_ref[...] = units(
        info_ref[SLOT[CORE]], mid, normed + vec[3:4], wu_ref, ub_ref, wd_ref,
        act_ref, slope_ref,
    )


def halves(hidden, n=None):
    if n is None:
        return pl.BlockSpec((2, TILE, hidden // 2), lambda t, *_: (0, t, 0))
    return jax.ShapeDtypeStruct((2, n, hidden // 2), BF16)


def ffn_front(info, ctx, tokens, w_outs, vectors, w_up, up_bias, w_down):
    n, model = tokens.shape
    width, hidden = ctx[0].shape[1], w_up.shape[1]
    row = lambda c: pl.BlockSpec((TILE, c), lambda t, *_: (t, 0))
    shape = lambda c, d: jax.ShapeDtypeStruct((n, c), d)
    fixed = [vectors, w_up, up_bias, w_down]
    outs = [(model, BF16), (model, F32), (1, F32), (model, F32)]
    return pl.pallas_call(
        ffn_front_kernel,
        grid_spec=pltpu.PrefetchScalarGridSpec(
            num_scalar_prefetch=1,
            grid=(n // TILE,),
            in_specs=[row(width), row(width), row(model)] + [vector(a) for a in (*w_outs, *fixed)],
            out_specs=[row(c) for c, _ in outs] + [halves(hidden), row(hidden)],
        ),
        out_shape=[shape(*o) for o in outs] + [halves(hidden, n), shape(hidden, BF16)],
        compiler_params=pltpu.CompilerParams(vmem_limit_bytes=48 * 2**20),
        cost_estimate=cost(10, n * model * 24),
        name="ffn_front",
    )(info, *ctx, tokens, *w_outs, *fixed)


def ffn_back_kernel(
    info_ref, pad_ref, mid_ref, xhat_ref, rstd_ref, part_ref, slope_m_ref, cot_ref,
    wu_m_ref, wd_m_ref, wu_o_ref, ub_o_ref, wd_o_ref, vec_ref,
    out_ref, pool_ref, act_ref, branch_ref, um_ref, uo_ref, resid_ref, att_ref, sums_ref, ub_m_sum_ref, ub_o_sum_ref, slope_ref,
):
    t = pl.program_id(0)
    per_row = SEQ // TILE
    mid = mid_ref[...]
    core = info_ref[SLOT[CORE]]
    second = units(
        core, mid, part_ref[...], wu_o_ref, ub_o_ref, wd_o_ref, act_ref, slope_ref
    )
    vec = vec_ref[...].astype(F32)
    gain_two = vec[4:5]
    xhat_two, rstd_two = normalise(second)
    final = xhat_two * gain_two + vec[5:6]
    out_ref[...] = final.astype(BF16)
    count = SEQ - pad_ref[info_ref[4] + t // per_row]
    slot = lax.broadcasted_iota(jnp.int32, (TILE, 1), 0) + (t % per_row) * TILE
    pooled = jnp.sum(jnp.where(slot < count, final, 0.0), axis=0, keepdims=True)
    pooled = pooled / count.astype(F32)
    which = lax.broadcasted_iota(jnp.int32, pool_ref.shape, 0) == t // per_row
    pooled = jnp.where(which, pooled, 0.0)

    dy = cot_ref[...].astype(F32)
    down = lambda v: jnp.sum(v, axis=0, keepdims=True)
    sums = [down(dy * xhat_two), down(dy)]
    second_grad = normalise_back(dy, xhat_two, rstd_two, gain_two)
    branch = second_grad.astype(BF16)
    branch_ref[...] = branch
    sums.append(down(branch.astype(F32)))
    normed_grad = second_grad
    bias_sums = []
    for wu_ref, wd_ref, s_ref, up_ref in (
        (wu_o_ref, wd_o_ref, slope_ref, uo_ref),
        (wu_m_ref, wd_m_ref, slope_m_ref, um_ref),
    ):
        upper = (dot(branch, wd_ref[...], NT) * s_ref[...].astype(F32)).astype(BF16)
        by_core(core, upper, up_ref)
        bias_sums.append(down(upper.astype(F32)))
        normed_grad = normed_grad + dot(upper, wu_ref[...], NT)
    xhat_one = xhat_ref[...]
    sums += [down(normed_grad * xhat_one), down(normed_grad)]
    resid = normalise_back(normed_grad, xhat_one, rstd_ref[...], vec[1:2])
    resid_ref[...] = resid
    att = resid.astype(BF16)
    att_ref[...] = att
    sums.append(down(att.astype(F32)))
    sums = jnp.concatenate(sums, axis=0)

    @pl.when(t == 0)
    def _():
        pool_ref[...] = pooled
        sums_ref[...] = sums
        ub_o_sum_ref[...] = bias_sums[0]
        ub_m_sum_ref[...] = bias_sums[1]

    @pl.when(t > 0)
    def _():
        pool_ref[...] += pooled
        sums_ref[...] += sums
        ub_o_sum_ref[...] += bias_sums[0]
        ub_m_sum_ref[...] += bias_sums[1]


def ffn_back(info, pads, mid, xhat, rstd, part, slope, cot, w_ups, w_downs, up_bias_o, vectors):
    n, model = mid.shape
    hidden, rows = slope.shape[1], n // SEQ
    row = lambda c: pl.BlockSpec((TILE, c), lambda t, *_: (t, 0))
    keep = lambda r, c: pl.BlockSpec((r, c), lambda t, *_: (0, 0))
    shape = lambda c, d: jax.ShapeDtypeStruct((n, c), d)
    fixed = [w_ups[0], w_downs[0], w_ups[1], up_bias_o, w_downs[1], vectors]
    return pl.pallas_call(
        ffn_back_kernel,
        grid_spec=pltpu.PrefetchScalarGridSpec(
            num_scalar_prefetch=2,
            grid=(n // TILE,),
            in_specs=[row(model), row(model), row(1), row(model), row(hidden), row(model)]
            + [vector(a) for a in fixed],
            out_specs=[row(model), keep(rows, model), halves(hidden), row(model)]
            + [halves(hidden)] * 2
            + [row(model), row(model), keep(6, model), keep(1, hidden), keep(1, hidden)],
            scratch_shapes=[pltpu.VMEM((TILE, hidden), BF16)],
        ),
        out_shape=[
            shape(model, BF16),
            jax.ShapeDtypeStruct((rows, model), F32),
            halves(hidden, n),
            shape(model, BF16),
        ]
        + [halves(hidden, n)] * 2
        + [
            shape(model, F32),
            shape(model, BF16),
            jax.ShapeDtypeStruct((6, model), F32),
            jax.ShapeDtypeStruct((1, hidden), F32),
            jax.ShapeDtypeStruct((1, hidden), F32),
        ],
        compiler_params=pltpu.CompilerParams(vmem_limit_bytes=40 * 2**20),
        cost_estimate=cost(25, n * model * 40),
        name="ffn_back",
    )(info, pads, mid, xhat, rstd, part, slope, cot, *fixed)


def pack_attn_kernel(info_ref, wq_ref, wo_ref, qb_ref, attn_ref):
    r, w = wq_ref.shape[1:]
    attn_ref[:r, :w] = wq_ref[0]
    attn_ref[:r, w:] = wq_ref[1]
    attn_ref[r : r + r // 2, :w] = wq_ref[2, : r // 2]
    attn_ref[r : r + r // 2, w:] = wq_ref[2, r // 2 :]
    at = r + r // 2
    attn_ref[at : at + wo_ref.shape[0], :] = wo_ref[...]
    at += wo_ref.shape[0]
    attn_ref[at:, :] = jnp.zeros((16, 2 * w), BF16)
    attn_ref[at : at + 2, :w] = qb_ref[...]


def pack_ffn_kernel(info_ref, seg_ref, wu_ref, wd_ref, ub_ref, up_ref, down_ref, qa_ref, ka_ref):
    u, c = wu_ref.shape[0], up_ref.shape[1]
    up_ref[:u, :] = wu_ref[:, :c]
    up_ref[u : 2 * u, :] = wu_ref[:, c:]
    up_ref[2 * u :, :] = jnp.zeros((16, c), BF16)
    up_ref[2 * u : 2 * u + 2, :] = ub_ref[...]
    down_ref[...] = wd_ref[...]
    segs = seg_ref.shape[1]
    slot = lax.broadcasted_iota(jnp.int32, (SEQ, PAIR), 0)
    lane = lax.broadcasted_iota(jnp.int32, (SEQ, PAIR), 1) & (HD - 1)
    for row in range(qa_ref.shape[0]):
        end, segment = 0, jnp.zeros((SEQ, PAIR), jnp.int32)
        for s in range(segs):
            end = end + seg_ref[info_ref[4] + row, s]
            segment = segment + jnp.where(slot >= end, 1, 0)
        same = lane == segment
        ka_ref[row] = jnp.where(same & (lane < segs), 1.0, 0.0).astype(BF16)
        qa_ref[row] = jnp.where((lane < segs) & ~same, MASKED, 0.0).astype(BF16)


def pack_attn(info, w_qkv, w_out, qv_bias):
    model, width = w_qkv.shape[1:]
    out_rows = w_out.shape[0] // 4
    shape = (3 * width // 4 + out_rows + 16, model)
    whole = lambda s: pl.BlockSpec(s, lambda i, *_: (0,) * len(s))
    return pl.pallas_call(
        pack_attn_kernel,
        grid_spec=pltpu.PrefetchScalarGridSpec(
            num_scalar_prefetch=1,
            grid=(1,),
            in_specs=[
                pl.BlockSpec((3, model // 4, width), lambda i, at: (0, at[0], 0)),
                pl.BlockSpec((out_rows, model), lambda i, at: (at[0], 0)),
                whole(qv_bias.shape),
            ],
            out_specs=whole(shape),
        ),
        out_shape=jax.ShapeDtypeStruct(shape, BF16),
        cost_estimate=cost(0, 2 * 2**20),
        name="pack_attn",
    )(info, w_qkv, w_out, qv_bias)


def pack_ffn(info, rows, seg_lengths, w_up, w_down, up_bias):
    model = w_up.shape[0]
    up_rows, down_rows = model // 4, w_down.shape[0] // 4
    whole = lambda s: pl.BlockSpec(s, lambda i, *_: (0,) * len(s))
    shapes = [(2 * up_rows + 16, model), (down_rows, model)] + [(rows, SEQ, PAIR)] * 2
    return pl.pallas_call(
        pack_ffn_kernel,
        grid_spec=pltpu.PrefetchScalarGridSpec(
            num_scalar_prefetch=2,
            grid=(1,),
            in_specs=[
                pl.BlockSpec((up_rows, w_up.shape[1]), lambda i, at, _: (at[0], 0)),
                pl.BlockSpec((down_rows, model), lambda i, at, _: (at[9], 0)),
                whole(up_bias.shape),
            ],
            out_specs=[whole(s) for s in shapes],
        ),
        out_shape=[jax.ShapeDtypeStruct(s, BF16) for s in shapes],
        cost_estimate=cost(0, 4 * 2**20),
        name="pack_ffn",
    )(info, seg_lengths, w_up, w_down, up_bias)


def unpack_attn_kernel(at_ref, *refs):
    pieces, (wq_ref, wo_ref, qb_ref) = refs[:4], refs[4:]
    r, w, o = wq_ref.shape[1] // 4, wq_ref.shape[2], wo_ref.shape[0] // 4
    for i, piece in enumerate(pieces):
        q = at_ref[i]
        rows = pl.ds(pl.multiple_of(q * r, 16), r)
        wq_ref[0, rows, :] = piece[:r, :w]
        wq_ref[1, rows, :] = piece[:r, w:]
        wq_ref[2, pl.ds(pl.multiple_of(q * r, 16), r // 2), :] = piece[r : r + r // 2, :w]
        wq_ref[2, pl.ds(pl.multiple_of(q * r + r // 2, 16), r // 2), :] = piece[r : r + r // 2, w:]
        at = r + r // 2
        wo_ref[pl.ds(pl.multiple_of(q * o, 16), o), :] = piece[at : at + o, :]
    at += o
    qb_ref[...] = pieces[0][at : at + 2, :w]


def unpack_ffn_kernel(at_ref, *refs):
    ups, downs, (wu_ref, wd_ref, ub_ref) = refs[:4], refs[4:8], refs[8:]
    r, c, d = wu_ref.shape[0] // 4, wu_ref.shape[1] // 2, wd_ref.shape[0] // 4
    for i in range(4):
        rows = pl.ds(pl.multiple_of(at_ref[i] * r, 16), r)
        wu_ref[rows, :c] = ups[i][:r, :]
        wu_ref[rows, c:] = ups[i][r : 2 * r, :]
        wd_ref[pl.ds(pl.multiple_of(at_ref[9 + i] * d, 16), d), :] = downs[i][...]
    ub_ref[...] = ups[0][2 * r : 2 * r + 2, :]


def unpack(kernel, at, pieces, like):
    whole = pl.BlockSpec(memory_space=pltpu.VMEM)
    return pl.pallas_call(
        kernel,
        in_specs=[pl.BlockSpec(memory_space=pltpu.SMEM)] + [whole] * len(pieces),
        out_specs=[whole] * len(like),
        out_shape=[jax.ShapeDtypeStruct(a.shape, BF16) for a in like],
        compiler_params=pltpu.CompilerParams(vmem_limit_bytes=32 * 2**20),
        cost_estimate=cost(0, 5 * 2**20),
        name=kernel.__name__,
    )(at, *pieces)


def over_mp(x):
    n = lax.axis_size("mp")
    return lax.ppermute(x, "mp", [(i, i ^ 1) for i in range(n)])


def over_dp(x, bit):
    n = lax.axis_size("dp")
    return lax.ppermute(x, "dp", [(i, i ^ bit) for i in range(n)])


def gather_pieces(rows, at_ref, refs, store):
    k = 0
    for ref in refs:
        for i in range(ref.shape[0] // rows):
            spot = pl.ds(pl.multiple_of(at_ref[k] * rows, 16), rows)
            store(spot, ref[i * rows : (i + 1) * rows, :].astype(F32))
            k += 1


def place_kernel(rows, at_ref, *refs):
    out_ref = refs[-1]

    def store(spot, value):
        out_ref[spot, :] = value

    gather_pieces(rows, at_ref, refs[:-1], store)


def place_up_kernel(rows, at_ref, *refs):
    out_ref = refs[-1]
    height, width = out_ref.shape[0], out_ref.shape[1] // 2
    k = 0
    for ref in refs[:-1]:
        for i in range(ref.shape[0] // rows):
            place, count = at_ref[k], height // rows
            spot = pl.ds(pl.multiple_of(place % count * rows, 16), rows)
            columns = pl.ds(pl.multiple_of(place // count * width, 128), width)
            out_ref[spot, columns] = ref[i * rows : (i + 1) * rows, :].astype(F32)
            k += 1


def place_attn_kernel(rows, at_ref, *refs):
    qkv_ref, out_ref, held_ref = refs[-3:]

    def store(spot, value):
        held_ref[spot, :] = value

    gather_pieces(rows, at_ref, refs[:-3], store)
    width = qkv_ref.shape[2]
    for c in range(3):
        for e in range(0, width, PAIR):
            qkv_ref[c, :, e : e + PAIR] = held_ref[c * width + e : c * width + e + PAIR, :].T
    out_ref[...] = held_ref[3 * width :, :]


def place(kernel, pieces, at, *shapes):
    total, cols = sum(piece.shape[0] for piece in pieces), pieces[0].shape[1]
    whole = pl.BlockSpec(memory_space=pltpu.VMEM)
    return pl.pallas_call(
        functools.partial(kernel, total // at.shape[0]),
        in_specs=[pl.BlockSpec(memory_space=pltpu.SMEM)] + [whole] * len(pieces),
        out_specs=[whole] * len(shapes),
        out_shape=[jax.ShapeDtypeStruct(s, F32) for s in shapes],
        scratch_shapes=[] if len(shapes) == 1 else [pltpu.VMEM((total, cols), F32)],
        compiler_params=pltpu.CompilerParams(vmem_limit_bytes=32 * 2**20),
        cost_estimate=cost(0, 6 * total * cols),
        name=kernel.__name__,
    )(at, *pieces)


def tie(x, *after):
    return lax.optimization_barrier((x,) + after)[0]


def land(info, x, got, own=None, step=None):
    n = got.shape[0]
    if own is not None:
        x = lax.dynamic_slice_in_dim(x, info[own] * n, n, 0)
    total = (x.astype(F32) + got.astype(F32)).astype(BF16)
    if step is None:
        return total
    return total, lax.dynamic_slice_in_dim(total, (1 - info[step]) * (n // 2), n // 2, 0)


def arrive(after, *flights):
    held = [c.crossed if part == "x" else c.got[part] for c, part in flights]
    held = lax.optimization_barrier((*held, after))
    for (c, part), got in zip(flights, held):
        if part == "x":
            c.crossed = got
        else:
            c.got[part] = got


class Chain:
    def __init__(self, info, bits):
        self.info, self.bits = info, bits
        self.dp_bits = [b for b in bits if b != "x"]
        self.order = [0]
        for b in reversed(self.dp_bits):
            self.order += [o ^ b for o in self.order]
        self.x, self.got, self.own, self.at = {}, {}, {}, {}
        self.held, self.back = None, list(reversed(self.dp_bits))

    def send(self, part, own, away):
        self.got[part] = over_dp(away, self.bits[0])
        self.x[part], self.own[part], self.at[part] = own, None, 0

    def hop(self, part="m", *after):
        if self.held is not None:
            return self.double(*after)
        x, at = tie(self.x[part], *after), self.at[part]
        got = self.crossed if self.bits[at] == "x" else self.got[part]
        bit = self.bits[at + 1] if at + 1 < len(self.bits) else None
        self.at[part] = at + 1
        if bit is None or bit == "x":
            x = land(self.info, x, got, self.own[part])
            self.x[part], self.own[part] = x, None
            if bit is None:
                bit = 2 * max(self.dp_bits)
                while bit < lax.axis_size("dp"):
                    x = land(self.info, x, over_dp(x, bit))
                    bit *= 2
                self.held = [x]
                self.double()
            elif part == "o":
                self.crossed = over_mp(x)
            return x
        x, away = land(self.info, x, got, self.own[part], SLOT[bit])
        self.x[part], self.own[part], self.got[part] = x, SLOT[bit], over_dp(away, bit)
        return x

    def double(self, *after):
        full = jnp.concatenate(self.held, axis=0) if len(self.held) > 1 else self.held[0]
        full = tie(full, *after)
        self.held.append(over_dp(full, self.back.pop(0)))
        return full

    def spots(self, me):
        who = me ^ jnp.array(self.order, jnp.int32)
        spot = jnp.zeros_like(who)
        for b in self.dp_bits:
            spot = 2 * spot + (who & b) // b
        return spot


def pack_small_kernel(sums_ref, um_ref, uo_ref, qm_ref, qo_ref, keep_ref, send_ref):
    n, c, w = sums_ref.shape[0], sums_ref.shape[1], qm_ref.shape[1]
    for out_ref, u_ref, q_ref in ((keep_ref, um_ref, qm_ref), (send_ref, uo_ref, qo_ref)):
        out_ref[...] = jnp.zeros(out_ref.shape, F32)
        out_ref[:n, :] = sums_ref[...]
        for i in range(u_ref.shape[1] // c):
            out_ref[n + i : n + i + 1, :] = u_ref[:, i * c : (i + 1) * c]
        at = n + u_ref.shape[1] // c
        for i in range(2):
            out_ref[at : at + 1, i * w : (i + 1) * w] = q_ref[i : i + 1, :]


def pack_small(sums, up_sums, qv_sums):
    shape = jax.ShapeDtypeStruct((16, sums.shape[1]), F32)
    return pl.pallas_call(
        pack_small_kernel, out_shape=[shape, shape], cost_estimate=cost(0, 2**18), name="pack_small"
    )(sums, *up_sums, *qv_sums)


def shards(
    tokens_in,
    seg_lengths,
    pad_counts,
    w_qkv,
    qv_bias,
    w_out,
    out_bias,
    norm1_gain,
    norm1_bias,
    w_up,
    up_bias,
    w_down,
    down_bias,
    norm2_gain,
    norm2_bias,
    cotangent,
):
    tokens, width = tokens_in.shape
    local = w_qkv.shape[2]
    me = lax.axis_index("dp")
    rows_here = tokens // SEQ
    slot = jnp.arange(13, dtype=jnp.int32)
    start = lax.axis_index("mp") * rows_here
    quarters = jnp.array([0, 2, 1, 3, 0, 0, 0, 0, 0, 0, 2, 1, 3], jnp.int32)
    quarters = quarters ^ jnp.where(slot < 4, me & 3, (me & CORE) | ((me & Z1) // 2))
    bits = jnp.where(slot == 4, start, (me >> jnp.clip(slot - 5, 0, 3)) & 1)
    info = jnp.where((slot < 4) | (slot > 8), quarters, bits)
    vectors = jnp.stack([out_bias, norm1_gain, norm1_bias, down_bias, norm2_gain, norm2_bias])
    up_bias = up_bias.reshape(-1, width)

    attn_w = pack_attn(info, w_qkv, w_out, qv_bias)
    up_w, down_w, q_aug, k_aug = pack_ffn(
        info, rows_here, seg_lengths, w_up, w_down, tie(up_bias, attn_w)
    )
    attn_w, up_w, down_w = over_mp(attn_w), over_mp(up_w), over_mp(down_w)
    early = local // PAIR - 1
    attn_args = (info, pad_counts, q_aug, k_aug)
    fwd_m = attn_fwd(tokens_in, w_qkv, qv_bias, *attn_args, span=(0, early))
    attn_w = tie(attn_w, fwd_m[1])
    attn_y, attn_core = over_dp(attn_w, Y), over_dp(attn_w, CORE)
    bias_m = tie(qv_bias, attn_w)
    fwd_m = attn_fwd(
        tokens_in, w_qkv, bias_m, *attn_args, span=(early, local // PAIR), into=fwd_m
    )
    up_w = tie(up_w, fwd_m[1])
    up_y = over_dp(up_w, Y)
    attn_core = tie(attn_core, up_w)
    attn_y = tie(attn_y, attn_core)
    w_qkv_o, w_out_o, qv_bias_o = unpack(
        unpack_attn_kernel,
        info,
        (attn_w, attn_y, attn_core, over_dp(attn_y, CORE)),
        (w_qkv, w_out, qv_bias),
    )
    w_qkvs, w_outs = (w_qkv, w_qkv_o), (w_out, w_out_o)
    fwd_o = attn_fwd(tokens_in, w_qkv_o, qv_bias_o, *attn_args)
    qkv, ctx, probs, rinv = zip(fwd_m, fwd_o)
    down_w, up_y, up_w = lax.optimization_barrier((down_w, up_y, up_w, ctx[1]))[:3]
    down_z = over_dp(down_w, Z1)
    up_core, up_both, down_core = over_dp(up_w, CORE), over_dp(up_y, CORE), over_dp(down_w, CORE)
    mid, xhat, rstd, part, act_m, slope_m = ffn_front(
        info, (ctx[0], tie(ctx[1], down_w)), tokens_in, w_outs, vectors, w_up, up_bias, w_down
    )
    down_z, up_core, up_both, down_core = lax.optimization_barrier(
        (down_z, up_core, up_both, down_core, mid)
    )[:4]
    w_up_o, w_down_o, up_bias_o = unpack(
        unpack_ffn_kernel,
        info,
        (up_w, up_y, up_core, up_both, down_w, down_z, down_core, over_dp(down_z, CORE)),
        (w_up, w_down, up_bias),
    )
    (
        tokens_out, pooled, act_o, grad_branch, upper_m, upper_o, grad_resid, grad_attended,
        sums, up_sum_m, up_sum_o,
    ) = ffn_back(
        info, pad_counts, mid, xhat, rstd, part, slope_m, cotangent, (w_up, w_up_o),
        (w_down, w_down_o), up_bias_o, vectors,
    )

    down = Chain(info, [CORE, "x", Z1, Y, Z2])
    up = Chain(info, [CORE, "x", Z1, Y, Z2])
    attn = Chain(info, [CORE, Y, "x", Z1, Z2])

    def attn_back(h, *after):
        g_att = tie(grad_attended, *after)
        dx, own, away, qv = attn_bwd(
            info, tokens_in, g_att, w_outs[h], qkv[h], ctx[h], probs[h], rinv[h]
        )
        return dx, own.reshape(-1, width), away.reshape(-1, width), qv

    def weight_grad(a, b, *after):
        return dot(tie(a, *after), b, TN).astype(BF16)

    def input_grad(h, grad_act, *after):
        return jnp.einsum(
            "cte,cde->td", tie(grad_act, *after), w_qkvs[h], preferred_element_type=F32
        )

    away = weight_grad(act_o[1], grad_branch)
    own = weight_grad(act_o[0], grad_branch, away)
    down.send("o", own, away)
    away = weight_grad(act_m[1], grad_branch, own)
    last = down.hop("o", away)
    own = weight_grad(act_m[0], grad_branch, last)
    down.send("m", own, away)
    away = weight_grad(mid, upper_o[1], own)
    own = weight_grad(mid, upper_o[0], away)
    up.send("o", own, away)
    last = down.hop("m", own)
    away = weight_grad(mid, upper_m[1], last)
    last = up.hop("o", away)
    own = weight_grad(mid, upper_m[0], last)
    up.send("m", own, away)
    dx_o, own, away, qv_o = attn_back(1, own)
    attn.send("o", own, away)
    last = up.hop("m", own)
    last = down.hop("m", last)
    last = attn.hop("o", last)
    dx_m, own, away, qv_m = attn_back(0, last)
    attn.send("m", own, away)
    small, small_send = pack_small(sums, (up_sum_m, up_sum_o), (qv_m, qv_o))
    last = down.hop("m", small)
    last = attn.hop("o", last)
    last = up.hop("m", last)
    last = attn.hop("m", last)
    small_got = over_mp(tie(small_send, last))
    count, bit = lax.axis_size("dp"), 1
    for what in "duadsaudsaudsaudsausgauap":
        if what == "s":
            last = small = tie(small, last) + small_got
            if bit < count:
                small_got = over_dp(small, bit)
                bit *= 2
        elif what == "g":
            total = input_grad(1, dx_o, last) + grad_resid
            total = total + input_grad(0, dx_m, last)
            grad_input = last = total.astype(BF16)
        elif what == "p":
            down.held[0] = tie(down.held[0], last)
            (grad_down,) = place(place_kernel, down.held, down.spots(me), w_down.shape)
            last = grad_down
        else:
            last = {"d": down, "u": up, "a": attn}[what].hop("m", last)
    if bit > 16:
        small = small + small_got
    while bit < count:
        small = small + over_dp(small, bit)
        bit *= 2
    (grad_up,) = place(place_up_kernel, up.held, up.spots(me), w_up.shape)
    grad_qkv, grad_out = place(
        place_attn_kernel, attn.held, attn.spots(me), w_qkv.shape, w_out.shape
    )
    vectors = [small[i] for i in (5, 3, 4, 2, 0, 1)]
    grad_up_bias = small[6:8].reshape(-1)
    grad_qv_bias = small[8].reshape(2, local)
    return (
        tokens_out,
        pooled,
        grad_input,
        grad_qkv,
        grad_qv_bias,
        grad_out,
        vectors[0],
        vectors[1],
        vectors[2],
        grad_up,
        grad_up_bias,
        grad_down,
        vectors[3],
        vectors[4],
        vectors[5],
    )


def solution(mesh):
    token = P(("dp", "mp"), None)
    in_specs = (
        token,
        P("dp", None),
        P("dp"),
        P(None, None, "mp"),
        P(None, "mp"),
        P("mp", None),
        P(),
        P(),
        P(),
        P(None, "mp"),
        P("mp"),
        P("mp", None),
        P(),
        P(),
        P(),
        token,
    )
    out_specs = (
        token,
        token,
        token,
        P(None, None, "mp"),
        P(None, "mp"),
        P("mp", None),
        P(),
        P(),
        P(),
        P(None, "mp"),
        P("mp"),
        P("mp", None),
        P(),
        P(),
        P(),
    )
    return jax.shard_map(shards, mesh=mesh, in_specs=in_specs, out_specs=out_specs, check_vma=False)
```

```python
import functools

import jax
import jax.numpy as jnp
from jax import lax
from jax.experimental import pallas as pl
from jax.experimental.pallas import tpu as pltpu
from jax.sharding import PartitionSpec as P

HD = 64
SEQ = 512
PAIR = 128
EPSILON = 1e-12
SCORE_SCALE = 0.125
GELU_COEF = 0.7978845608028654
LOG2_E = 1.4426950408889634
MASKED = -1e30
F32 = jnp.float32
BF16 = jnp.bfloat16

NT = (((1,), (1,)), ((), ()))
NN = (((1,), (0,)), ((), ()))
TN = (((0,), (0,)), ((), ()))


TILE = 256
HINT = 8.0
VMEM_LIMIT = 56 * 2**20
CORE, Y, Z1, Z2 = 1, 2, 4, 8
SLOT = {CORE: 5, Y: 6, Z1: 7, Z2: 8}


def cost(gflop, size):
    return pl.CostEstimate(
        flops=int(gflop * HINT * 1e9), bytes_accessed=int(size * HINT), transcendentals=0
    )


def dot(a, b, dims=NN):
    return lax.dot_general(a, b, dims, preferred_element_type=F32)


def attn_fwd_kernel(
    info_ref, pad_ref, x_ref, w_ref, bias_ref, qa_ref, ka_ref, qkv_ref, ctx_ref, e_ref, rinv_ref
):
    limit = SEQ - pad_ref[info_ref[4] + pl.program_id(0)]
    w = jnp.concatenate([w_ref[0], w_ref[1], w_ref[2]], axis=1)
    qkv = dot(x_ref[...], w)
    bias = bias_ref[...].astype(F32)
    q = (qkv[:, :PAIR] + bias[0:1]).astype(BF16)
    k = qkv[:, PAIR : 2 * PAIR].astype(BF16)
    v = (qkv[:, 2 * PAIR :] + bias[1:2]).astype(BF16)
    qkv_ref[0], qkv_ref[1], qkv_ref[2] = q, k, v
    v_t = v.astype(F32).T.astype(BF16)
    low = lax.broadcasted_iota(jnp.int32, (SEQ, PAIR), 1) < HD
    j = lax.broadcasted_iota(jnp.int32, (64, SEQ), 0) + (SEQ - 64)
    i = lax.broadcasted_iota(jnp.int32, (64, SEQ), 1)
    seen = (j < limit) | (j == i)
    scores, weights = [], []
    for h in range(2):
        own = low if h == 0 else ~low
        scores.append(dot(jnp.where(own, k, ka_ref[0]), jnp.where(own, q, qa_ref[0]), NT))
    for h in range(2):
        tail = jnp.where(seen, scores[h][SEQ - 64 :], MASKED)
        s = jnp.concatenate([scores[h][: SEQ - 64], tail], axis=0)
        peak = jnp.max(s, axis=0, keepdims=True)
        e = jnp.exp2((s - peak) * (SCORE_SCALE * LOG2_E))
        rinv = 1.0 / jnp.sum(e, axis=0, keepdims=True)
        eb = e.astype(BF16)
        e_ref[h] = eb
        rinv_ref[0, 0, h : h + 1, :] = rinv
        weights.append((eb, rinv))
    parts = [dot(v_t[h * HD : (h + 1) * HD], e) * rinv for h, (e, rinv) in enumerate(weights)]
    ctx_ref[...] = jnp.concatenate(parts, axis=0).T.astype(BF16)


def attn_fwd(tokens, w_qkv, bias, info, pads, q_aug, k_aug, span=None, into=None):
    rows, width = tokens.shape[0] // SEQ, w_qkv.shape[2]
    pairs, model = width // PAIR, tokens.shape[1]
    first, end = span or (0, pairs)
    aug = pl.BlockSpec((1, SEQ, PAIR), lambda r, p, *_: (r, 0, 0))
    into = list(into or ())
    kernel = attn_fwd_kernel
    if into:
        kernel = lambda *refs: attn_fwd_kernel(*refs[:7], *refs[7 + len(into) :])
    return pl.pallas_call(
        kernel,
        grid_spec=pltpu.PrefetchScalarGridSpec(
            num_scalar_prefetch=2,
            grid=(rows, end - first),
            in_specs=[
                pl.BlockSpec((SEQ, model), lambda r, p, *_: (r, 0)),
                pl.BlockSpec((3, model, PAIR), lambda r, p, *_: (0, 0, first + p)),
                pl.BlockSpec((2, PAIR), lambda r, p, *_: (0, first + p)),
                aug,
                aug,
            ]
            + [pl.BlockSpec(memory_space=pl.ANY)] * len(into),
            out_specs=[
                pl.BlockSpec((3, SEQ, PAIR), lambda r, p, *_: (0, r, first + p)),
                pl.BlockSpec((SEQ, PAIR), lambda r, p, *_: (r, first + p)),
                pl.BlockSpec((2, SEQ, SEQ), lambda r, p, *_: (r * pairs + first + p, 0, 0)),
                pl.BlockSpec((1, 1, 2, SEQ), lambda r, p, *_: (r, first + p, 0, 0)),
            ],
        ),
        out_shape=[
            pltpu.HBM((3, rows * SEQ, width), BF16),
            jax.ShapeDtypeStruct((rows * SEQ, width), BF16),
            pltpu.HBM((rows * pairs * 2, SEQ, SEQ), BF16),
            jax.ShapeDtypeStruct((rows, pairs, 2, SEQ), F32),
        ],
        input_output_aliases={7 + i: i for i in range(len(into))},
        compiler_params=pltpu.CompilerParams(vmem_limit_bytes=24 * 2**20),
        cost_estimate=cost(1e-4, 1e3),
        name="attn_fwd",
    )(info, pads, tokens, w_qkv, bias, q_aug, k_aug, *into)


def attn_bwd_kernel(
    info_ref, x_ref, ga_ref, wo_ref, qkv_ref, ctx_ref, e_ref, rinv_ref,
    out_ref, own_ref, away_ref, gb_ref, acc_ref,
):
    row, last = pl.program_id(1), pl.num_programs(1) - 1
    q, k, v = qkv_ref[0], qkv_ref[1], qkv_ref[2]
    k_t = k.astype(F32).T.astype(BF16)
    d_t = dot(wo_ref[...], ga_ref[...], NT).astype(BF16).astype(F32)
    c_t = ctx_ref[...].astype(F32).T
    lane = lax.broadcasted_iota(jnp.int32, (SEQ, PAIR), 1)
    row8 = lax.broadcasted_iota(jnp.int32, (8, SEQ), 0)
    low = lane < HD
    ones = jnp.where((lane & (HD - 1)) < 2, 1.0, 0.0).astype(BF16)
    dv, dk, dq = [], [], []
    for h in range(2):
        own = low if h == 0 else ~low
        rinv = rinv_ref[0, 0, h : h + 1, :]
        mine = d_t[h * HD : (h + 1) * HD] * rinv
        minus = -jnp.sum(mine * c_t[h * HD : (h + 1) * HD], axis=0, keepdims=True)
        high = minus.astype(BF16).astype(F32)
        extra = jnp.where(row8 == 0, high, jnp.where(row8 == 1, minus - high, 0.0))
        blank = jnp.zeros((HD - 8, SEQ), F32)
        stack = [mine, extra, blank] if h == 0 else [extra, blank, mine]
        g_t = jnp.concatenate(stack, axis=0).astype(BF16)
        v_h = jnp.where(own, v, ones)
        e = e_ref[h]
        d = e * dot(v_h, g_t).astype(BF16)
        dv.append(dot(e, g_t, NT))
        dk.append(dot(d, q))
        dq.append(dot(k_t[h * HD : (h + 1) * HD], d))
    dq_t = jnp.concatenate(dq, axis=0) * SCORE_SCALE
    dk = jnp.where(low, dk[0], dk[1]) * SCORE_SCALE
    dv = jnp.where(low, dv[0], dv[1])
    dq_b = dq_t.T.astype(BF16)
    dk_b, dv_b = dk.astype(BF16), dv.astype(BF16)
    out_ref[0], out_ref[1], out_ref[2] = dq_b, dk_b, dv_b
    left = jnp.concatenate([dq_t, dk.T, dv.T], axis=0).astype(BF16)
    g_w = dot(left, x_ref[...]).reshape(3, PAIR, x_ref.shape[1])
    g_o = dot(c_t.astype(BF16), ga_ref[...])
    g_b = jnp.concatenate(
        [
            jnp.sum(dq_b.astype(F32), axis=0, keepdims=True),
            jnp.sum(dv_b.astype(F32), axis=0, keepdims=True),
        ],
        axis=0,
    )

    @pl.when(row == 0)
    def _():
        acc_ref[:3] = g_w
        acc_ref[3] = g_o
        gb_ref[...] = g_b

    @pl.when(row > 0)
    def _():
        acc_ref[:3] += g_w
        acc_ref[3] += g_o
        gb_ref[...] += g_b

    @pl.when(row == last)
    def _():
        core = info_ref[SLOT[CORE]]
        own_ref[...] = acc_ref[pl.ds(2 * core, 2)].astype(BF16)
        away_ref[...] = acc_ref[pl.ds(2 * (1 - core), 2)].astype(BF16)


def attn_bwd(info, tokens, grad_att, w_out, qkv, ctx, e, rinv):
    rows, pairs = rinv.shape[0], rinv.shape[1]
    width, model = qkv.shape[2], tokens.shape[1]
    wide = pl.BlockSpec((SEQ, model), lambda p, r, _: (r, 0))
    triple = pl.BlockSpec((3, SEQ, PAIR), lambda p, r, _: (0, r, p))
    half = pl.BlockSpec((2, PAIR, model), lambda p, r, _: (0, p, 0))
    return pl.pallas_call(
        attn_bwd_kernel,
        grid_spec=pltpu.PrefetchScalarGridSpec(
            num_scalar_prefetch=1,
            grid=(pairs, rows),
            in_specs=[
                wide,
                wide,
                pl.BlockSpec((PAIR, model), lambda p, r, _: (p, 0)),
                triple,
                pl.BlockSpec((SEQ, PAIR), lambda p, r, _: (r, p)),
                pl.BlockSpec((2, SEQ, SEQ), lambda p, r, _: (r * pairs + p, 0, 0)),
                pl.BlockSpec((1, 1, 2, SEQ), lambda p, r, _: (r, p, 0, 0)),
            ],
            out_specs=[
                triple,
                half,
                half,
                pl.BlockSpec((2, PAIR), lambda p, r, _: (0, p)),
            ],
            scratch_shapes=[pltpu.VMEM((4, PAIR, model), F32)],
        ),
        out_shape=[
            pltpu.HBM((3, rows * SEQ, width), BF16),
            pltpu.HBM((2, width, model), BF16),
            pltpu.HBM((2, width, model), BF16),
            jax.ShapeDtypeStruct((2, width), F32),
        ],
        compiler_params=pltpu.CompilerParams(vmem_limit_bytes=24 * 2**20),
        cost_estimate=cost(8 * rows, rows * pairs * 2 * SEQ * SEQ * 2),
        name="attn_bwd",
    )(info, tokens, grad_att, w_out, qkv, ctx, pltpu.with_memory_space_constraint(e, pltpu.HBM), rinv)


def vector(x):
    return pl.BlockSpec(x.shape, lambda *_: (0,) * x.ndim)


def normalise(v):
    centered = v - jnp.mean(v, axis=-1, keepdims=True)
    rstd = lax.rsqrt(jnp.mean(centered * centered, axis=-1, keepdims=True) + EPSILON)
    return centered * rstd, rstd


def normalise_back(dy, xhat, rstd, gain):
    dg = dy * gain
    return rstd * (
        dg
        - jnp.mean(dg, axis=-1, keepdims=True)
        - xhat * jnp.mean(dg * xhat, axis=-1, keepdims=True)
    )


def gelu_and_slope(u):
    u2 = u * u
    t = jnp.tanh(u * (GELU_COEF + (GELU_COEF * 0.044715) * u2))
    half = 0.5 + 0.5 * t
    act = u * half
    slope = half * (1.0 + u * (1.0 - t) * (GELU_COEF + (3 * GELU_COEF * 0.044715) * u2))
    return act, slope


def flat_bias(ref):
    b = ref[...].astype(F32)
    return jnp.concatenate([b[i : i + 1] for i in range(b.shape[0])], axis=1)


def by_core(core, x, ref):
    half = x.shape[1] // 2
    ref[core] = x[:, :half]
    ref[1 - core] = x[:, half:]


def units(core, mid, acc, wu_ref, ub_ref, wd_ref, act_ref, slope_ref):
    act, slope = gelu_and_slope(dot(mid, wu_ref[...]) + flat_bias(ub_ref))
    act = act.astype(BF16)
    by_core(core, act, act_ref)
    slope_ref[...] = slope.astype(BF16)
    return acc + dot(act, wd_ref[...])


def ffn_front_kernel(
    info_ref, cm_ref, co_ref, x_ref, wm_ref, wo_ref, vec_ref, wu_ref, ub_ref, wd_ref,
    mid_ref, xhat_ref, rstd_ref, part_ref, act_ref, slope_ref,
):
    vec = vec_ref[...].astype(F32)
    attended = dot(cm_ref[...], wm_ref[...]) + dot(co_ref[...], wo_ref[...])
    resid = x_ref[...].astype(F32) + (attended + vec[0:1])
    xhat, rstd = normalise(resid)
    normed = xhat * vec[1:2] + vec[2:3]
    mid = normed.astype(BF16)
    mid_ref[...] = mid
    xhat_ref[...] = xhat
    rstd_ref[...] = rstd
    part_ref[...] = units(
        info_ref[SLOT[CORE]], mid, normed + vec[3:4], wu_ref, ub_ref, wd_ref,
        act_ref, slope_ref,
    )


def halves(hidden, n=None):
    if n is None:
        return pl.BlockSpec((2, TILE, hidden // 2), lambda t, *_: (0, t, 0))
    return jax.ShapeDtypeStruct((2, n, hidden // 2), BF16)


def ffn_front(info, ctx, tokens, w_outs, vectors, w_up, up_bias, w_down):
    n, model = tokens.shape
    width, hidden = ctx[0].shape[1], w_up.shape[1]
    row = lambda c: pl.BlockSpec((TILE, c), lambda t, *_: (t, 0))
    shape = lambda c, d: jax.ShapeDtypeStruct((n, c), d)
    fixed = [vectors, w_up, up_bias, w_down]
    outs = [(model, BF16), (model, F32), (1, F32), (model, F32)]
    return pl.pallas_call(
        ffn_front_kernel,
        grid_spec=pltpu.PrefetchScalarGridSpec(
            num_scalar_prefetch=1,
            grid=(n // TILE,),
            in_specs=[row(width), row(width), row(model)] + [vector(a) for a in (*w_outs, *fixed)],
            out_specs=[row(c) for c, _ in outs] + [halves(hidden), row(hidden)],
        ),
        out_shape=[shape(*o) for o in outs] + [halves(hidden, n), shape(hidden, BF16)],
        compiler_params=pltpu.CompilerParams(vmem_limit_bytes=48 * 2**20),
        cost_estimate=cost(10, n * model * 24),
        name="ffn_front",
    )(info, *ctx, tokens, *w_outs, *fixed)


def ffn_back_kernel(
    info_ref, pad_ref, mid_ref, xhat_ref, rstd_ref, part_ref, slope_m_ref, cot_ref,
    wu_m_ref, wd_m_ref, wu_o_ref, ub_o_ref, wd_o_ref, vec_ref,
    out_ref, pool_ref, act_ref, branch_ref, um_ref, uo_ref, resid_ref, att_ref, sums_ref, ub_m_sum_ref, ub_o_sum_ref, slope_ref,
):
    t = pl.program_id(0)
    per_row = SEQ // TILE
    mid = mid_ref[...]
    core = info_ref[SLOT[CORE]]
    second = units(
        core, mid, part_ref[...], wu_o_ref, ub_o_ref, wd_o_ref, act_ref, slope_ref
    )
    vec = vec_ref[...].astype(F32)
    gain_two = vec[4:5]
    xhat_two, rstd_two = normalise(second)
    final = xhat_two * gain_two + vec[5:6]
    out_ref[...] = final.astype(BF16)
    count = SEQ - pad_ref[info_ref[4] + t // per_row]
    slot = lax.broadcasted_iota(jnp.int32, (TILE, 1), 0) + (t % per_row) * TILE
    pooled = jnp.sum(jnp.where(slot < count, final, 0.0), axis=0, keepdims=True)
    pooled = pooled / count.astype(F32)
    which = lax.broadcasted_iota(jnp.int32, pool_ref.shape, 0) == t // per_row
    pooled = jnp.where(which, pooled, 0.0)

    dy = cot_ref[...].astype(F32)
    down = lambda v: jnp.sum(v, axis=0, keepdims=True)
    sums = [down(dy * xhat_two), down(dy)]
    second_grad = normalise_back(dy, xhat_two, rstd_two, gain_two)
    branch = second_grad.astype(BF16)
    branch_ref[...] = branch
    sums.append(down(branch.astype(F32)))
    normed_grad = second_grad
    bias_sums = []
    for wu_ref, wd_ref, s_ref, up_ref in (
        (wu_o_ref, wd_o_ref, slope_ref, uo_ref),
        (wu_m_ref, wd_m_ref, slope_m_ref, um_ref),
    ):
        upper = (dot(branch, wd_ref[...], NT) * s_ref[...].astype(F32)).astype(BF16)
        by_core(core, upper, up_ref)
        bias_sums.append(down(upper.astype(F32)))
        normed_grad = normed_grad + dot(upper, wu_ref[...], NT)
    xhat_one = xhat_ref[...]
    sums += [down(normed_grad * xhat_one), down(normed_grad)]
    resid = normalise_back(normed_grad, xhat_one, rstd_ref[...], vec[1:2])
    resid_ref[...] = resid
    att = resid.astype(BF16)
    att_ref[...] = att
    sums.append(down(att.astype(F32)))
    sums = jnp.concatenate(sums, axis=0)

    @pl.when(t == 0)
    def _():
        pool_ref[...] = pooled
        sums_ref[...] = sums
        ub_o_sum_ref[...] = bias_sums[0]
        ub_m_sum_ref[...] = bias_sums[1]

    @pl.when(t > 0)
    def _():
        pool_ref[...] += pooled
        sums_ref[...] += sums
        ub_o_sum_ref[...] += bias_sums[0]
        ub_m_sum_ref[...] += bias_sums[1]


def ffn_back(info, pads, mid, xhat, rstd, part, slope, cot, w_ups, w_downs, up_bias_o, vectors):
    n, model = mid.shape
    hidden, rows = slope.shape[1], n // SEQ
    row = lambda c: pl.BlockSpec((TILE, c), lambda t, *_: (t, 0))
    keep = lambda r, c: pl.BlockSpec((r, c), lambda t, *_: (0, 0))
    shape = lambda c, d: jax.ShapeDtypeStruct((n, c), d)
    fixed = [w_ups[0], w_downs[0], w_ups[1], up_bias_o, w_downs[1], vectors]
    return pl.pallas_call(
        ffn_back_kernel,
        grid_spec=pltpu.PrefetchScalarGridSpec(
            num_scalar_prefetch=2,
            grid=(n // TILE,),
            in_specs=[row(model), row(model), row(1), row(model), row(hidden), row(model)]
            + [vector(a) for a in fixed],
            out_specs=[row(model), keep(rows, model), halves(hidden), row(model)]
            + [halves(hidden)] * 2
            + [row(model), row(model), keep(6, model), keep(1, hidden), keep(1, hidden)],
            scratch_shapes=[pltpu.VMEM((TILE, hidden), BF16)],
        ),
        out_shape=[
            shape(model, BF16),
            jax.ShapeDtypeStruct((rows, model), F32),
            halves(hidden, n),
            shape(model, BF16),
        ]
        + [halves(hidden, n)] * 2
        + [
            shape(model, F32),
            shape(model, BF16),
            jax.ShapeDtypeStruct((6, model), F32),
            jax.ShapeDtypeStruct((1, hidden), F32),
            jax.ShapeDtypeStruct((1, hidden), F32),
        ],
        compiler_params=pltpu.CompilerParams(vmem_limit_bytes=40 * 2**20),
        cost_estimate=cost(25, n * model * 40),
        name="ffn_back",
    )(info, pads, mid, xhat, rstd, part, slope, cot, *fixed)


def pack_attn_kernel(info_ref, wq_ref, wo_ref, qb_ref, attn_ref):
    r, w = wq_ref.shape[1:]
    attn_ref[:r, :w] = wq_ref[0]
    attn_ref[:r, w:] = wq_ref[1]
    attn_ref[r : r + r // 2, :w] = wq_ref[2, : r // 2]
    attn_ref[r : r + r // 2, w:] = wq_ref[2, r // 2 :]
    at = r + r // 2
    attn_ref[at : at + wo_ref.shape[0], :] = wo_ref[...]
    at += wo_ref.shape[0]
    attn_ref[at:, :] = jnp.zeros((16, 2 * w), BF16)
    attn_ref[at : at + 2, :w] = qb_ref[...]


def pack_ffn_kernel(info_ref, seg_ref, wu_ref, wd_ref, ub_ref, up_ref, down_ref, qa_ref, ka_ref):
    u, c = wu_ref.shape[0], up_ref.shape[1]
    up_ref[:u, :] = wu_ref[:, :c]
    up_ref[u : 2 * u, :] = wu_ref[:, c:]
    up_ref[2 * u :, :] = jnp.zeros((16, c), BF16)
    up_ref[2 * u : 2 * u + 2, :] = ub_ref[...]
    down_ref[...] = wd_ref[...]
    segs = seg_ref.shape[1]
    slot = lax.broadcasted_iota(jnp.int32, (SEQ, PAIR), 0)
    lane = lax.broadcasted_iota(jnp.int32, (SEQ, PAIR), 1) & (HD - 1)
    for row in range(qa_ref.shape[0]):
        end, segment = 0, jnp.zeros((SEQ, PAIR), jnp.int32)
        for s in range(segs):
            end = end + seg_ref[info_ref[4] + row, s]
            segment = segment + jnp.where(slot >= end, 1, 0)
        same = lane == segment
        ka_ref[row] = jnp.where(same & (lane < segs), 1.0, 0.0).astype(BF16)
        qa_ref[row] = jnp.where((lane < segs) & ~same, MASKED, 0.0).astype(BF16)


def pack_attn(info, w_qkv, w_out, qv_bias):
    model, width = w_qkv.shape[1:]
    out_rows = w_out.shape[0] // 4
    shape = (3 * width // 4 + out_rows + 16, model)
    whole = lambda s: pl.BlockSpec(s, lambda i, *_: (0,) * len(s))
    return pl.pallas_call(
        pack_attn_kernel,
        grid_spec=pltpu.PrefetchScalarGridSpec(
            num_scalar_prefetch=1,
            grid=(1,),
            in_specs=[
                pl.BlockSpec((3, model // 4, width), lambda i, at: (0, at[0], 0)),
                pl.BlockSpec((out_rows, model), lambda i, at: (at[0], 0)),
                whole(qv_bias.shape),
            ],
            out_specs=whole(shape),
        ),
        out_shape=jax.ShapeDtypeStruct(shape, BF16),
        cost_estimate=cost(0, 2 * 2**20),
        name="pack_attn",
    )(info, w_qkv, w_out, qv_bias)


def pack_ffn(info, rows, seg_lengths, w_up, w_down, up_bias):
    model = w_up.shape[0]
    up_rows, down_rows = model // 4, w_down.shape[0] // 4
    whole = lambda s: pl.BlockSpec(s, lambda i, *_: (0,) * len(s))
    shapes = [(2 * up_rows + 16, model), (down_rows, model)] + [(rows, SEQ, PAIR)] * 2
    return pl.pallas_call(
        pack_ffn_kernel,
        grid_spec=pltpu.PrefetchScalarGridSpec(
            num_scalar_prefetch=2,
            grid=(1,),
            in_specs=[
                pl.BlockSpec((up_rows, w_up.shape[1]), lambda i, at, _: (at[0], 0)),
                pl.BlockSpec((down_rows, model), lambda i, at, _: (at[9], 0)),
                whole(up_bias.shape),
            ],
            out_specs=[whole(s) for s in shapes],
        ),
        out_shape=[jax.ShapeDtypeStruct(s, BF16) for s in shapes],
        cost_estimate=cost(0, 4 * 2**20),
        name="pack_ffn",
    )(info, seg_lengths, w_up, w_down, up_bias)


def unpack_attn_kernel(at_ref, *refs):
    pieces, (wq_ref, wo_ref, qb_ref) = refs[:4], refs[4:]
    r, w, o = wq_ref.shape[1] // 4, wq_ref.shape[2], wo_ref.shape[0] // 4
    for i, piece in enumerate(pieces):
        q = at_ref[i]
        rows = pl.ds(pl.multiple_of(q * r, 16), r)
        wq_ref[0, rows, :] = piece[:r, :w]
        wq_ref[1, rows, :] = piece[:r, w:]
        wq_ref[2, pl.ds(pl.multiple_of(q * r, 16), r // 2), :] = piece[r : r + r // 2, :w]
        wq_ref[2, pl.ds(pl.multiple_of(q * r + r // 2, 16), r // 2), :] = piece[r : r + r // 2, w:]
        at = r + r // 2
        wo_ref[pl.ds(pl.multiple_of(q * o, 16), o), :] = piece[at : at + o, :]
    at += o
    qb_ref[...] = pieces[0][at : at + 2, :w]


def unpack_ffn_kernel(at_ref, *refs):
    ups, downs, (wu_ref, wd_ref, ub_ref) = refs[:4], refs[4:8], refs[8:]
    r, c, d = wu_ref.shape[0] // 4, wu_ref.shape[1] // 2, wd_ref.shape[0] // 4
    for i in range(4):
        rows = pl.ds(pl.multiple_of(at_ref[i] * r, 16), r)
        wu_ref[rows, :c] = ups[i][:r, :]
        wu_ref[rows, c:] = ups[i][r : 2 * r, :]
        wd_ref[pl.ds(pl.multiple_of(at_ref[9 + i] * d, 16), d), :] = downs[i][...]
    ub_ref[...] = ups[0][2 * r : 2 * r + 2, :]


def unpack(kernel, at, pieces, like):
    whole = pl.BlockSpec(memory_space=pltpu.VMEM)
    return pl.pallas_call(
        kernel,
        in_specs=[pl.BlockSpec(memory_space=pltpu.SMEM)] + [whole] * len(pieces),
        out_specs=[whole] * len(like),
        out_shape=[jax.ShapeDtypeStruct(a.shape, BF16) for a in like],
        compiler_params=pltpu.CompilerParams(vmem_limit_bytes=32 * 2**20),
        cost_estimate=cost(0, 5 * 2**20),
        name=kernel.__name__,
    )(at, *pieces)


def over_mp(x):
    n = lax.axis_size("mp")
    return lax.ppermute(x, "mp", [(i, i ^ 1) for i in range(n)])


def over_dp(x, bit):
    n = lax.axis_size("dp")
    return lax.ppermute(x, "dp", [(i, i ^ bit) for i in range(n)])


def gather_pieces(rows, at_ref, refs, store):
    k = 0
    for ref in refs:
        for i in range(ref.shape[0] // rows):
            spot = pl.ds(pl.multiple_of(at_ref[k] * rows, 16), rows)
            store(spot, ref[i * rows : (i + 1) * rows, :].astype(F32))
            k += 1


def place_kernel(rows, at_ref, *refs):
    out_ref = refs[-1]

    def store(spot, value):
        out_ref[spot, :] = value

    gather_pieces(rows, at_ref, refs[:-1], store)


def place_up_kernel(rows, at_ref, *refs):
    out_ref = refs[-1]
    height, width = out_ref.shape[0], out_ref.shape[1] // 2
    k = 0
    for ref in refs[:-1]:
        for i in range(ref.shape[0] // rows):
            place, count = at_ref[k], height // rows
            spot = pl.ds(pl.multiple_of(place % count * rows, 16), rows)
            columns = pl.ds(pl.multiple_of(place // count * width, 128), width)
            out_ref[spot, columns] = ref[i * rows : (i + 1) * rows, :].astype(F32)
            k += 1


def place_attn_kernel(rows, at_ref, *refs):
    qkv_ref, out_ref, held_ref = refs[-3:]

    def store(spot, value):
        held_ref[spot, :] = value

    gather_pieces(rows, at_ref, refs[:-3], store)
    width = qkv_ref.shape[2]
    for c in range(3):
        for e in range(0, width, PAIR):
            qkv_ref[c, :, e : e + PAIR] = held_ref[c * width + e : c * width + e + PAIR, :].T
    out_ref[...] = held_ref[3 * width :, :]


def place(kernel, pieces, at, *shapes):
    total, cols = sum(piece.shape[0] for piece in pieces), pieces[0].shape[1]
    whole = pl.BlockSpec(memory_space=pltpu.VMEM)
    return pl.pallas_call(
        functools.partial(kernel, total // at.shape[0]),
        in_specs=[pl.BlockSpec(memory_space=pltpu.SMEM)] + [whole] * len(pieces),
        out_specs=[whole] * len(shapes),
        out_shape=[jax.ShapeDtypeStruct(s, F32) for s in shapes],
        scratch_shapes=[] if len(shapes) == 1 else [pltpu.VMEM((total, cols), F32)],
        compiler_params=pltpu.CompilerParams(vmem_limit_bytes=32 * 2**20),
        cost_estimate=cost(0, 6 * total * cols),
        name=kernel.__name__,
    )(at, *pieces)


def tie(x, *after):
    return lax.optimization_barrier((x,) + after)[0]


def land(info, x, got, own=None, step=None):
    n = got.shape[0]
    if own is not None:
        x = lax.dynamic_slice_in_dim(x, info[own] * n, n, 0)
    total = (x.astype(F32) + got.astype(F32)).astype(BF16)
    if step is None:
        return total
    return total, lax.dynamic_slice_in_dim(total, (1 - info[step]) * (n // 2), n // 2, 0)


def arrive(after, *flights):
    held = [c.crossed if part == "x" else c.got[part] for c, part in flights]
    held = lax.optimization_barrier((*held, after))
    for (c, part), got in zip(flights, held):
        if part == "x":
            c.crossed = got
        else:
            c.got[part] = got


class Chain:
    def __init__(self, info, bits):
        self.info, self.bits = info, bits
        self.dp_bits = [b for b in bits if b != "x"]
        self.order = [0]
        for b in reversed(self.dp_bits):
            self.order += [o ^ b for o in self.order]
        self.x, self.got, self.own, self.at = {}, {}, {}, {}
        self.held, self.back = None, list(reversed(self.dp_bits))

    def send(self, part, own, away):
        self.got[part] = over_dp(away, self.bits[0])
        self.x[part], self.own[part], self.at[part] = own, None, 0

    def hop(self, part="m", *after):
        if self.held is not None:
            return self.double(*after)
        x, at = tie(self.x[part], *after), self.at[part]
        got = self.crossed if self.bits[at] == "x" else self.got[part]
        bit = self.bits[at + 1] if at + 1 < len(self.bits) else None
        self.at[part] = at + 1
        if bit is None or bit == "x":
            x = land(self.info, x, got, self.own[part])
            self.x[part], self.own[part] = x, None
            if bit is None:
                bit = 2 * max(self.dp_bits)
                while bit < lax.axis_size("dp"):
                    x = land(self.info, x, over_dp(x, bit))
                    bit *= 2
                self.held = [x]
                self.double()
            elif part == "o":
                self.crossed = over_mp(x)
            return x
        x, away = land(self.info, x, got, self.own[part], SLOT[bit])
        self.x[part], self.own[part], self.got[part] = x, SLOT[bit], over_dp(away, bit)
        return x

    def double(self, *after):
        full = jnp.concatenate(self.held, axis=0) if len(self.held) > 1 else self.held[0]
        full = tie(full, *after)
        self.held.append(over_dp(full, self.back.pop(0)))
        return full

    def spots(self, me):
        who = me ^ jnp.array(self.order, jnp.int32)
        spot = jnp.zeros_like(who)
        for b in self.dp_bits:
            spot = 2 * spot + (who & b) // b
        return spot


def pack_small_kernel(sums_ref, um_ref, uo_ref, qm_ref, qo_ref, keep_ref, send_ref):
    n, c, w = sums_ref.shape[0], sums_ref.shape[1], qm_ref.shape[1]
    for out_ref, u_ref, q_ref in ((keep_ref, um_ref, qm_ref), (send_ref, uo_ref, qo_ref)):
        out_ref[...] = jnp.zeros(out_ref.shape, F32)
        out_ref[:n, :] = sums_ref[...]
        for i in range(u_ref.shape[1] // c):
            out_ref[n + i : n + i + 1, :] = u_ref[:, i * c : (i + 1) * c]
        at = n + u_ref.shape[1] // c
        for i in range(2):
            out_ref[at : at + 1, i * w : (i + 1) * w] = q_ref[i : i + 1, :]


def pack_small(sums, up_sums, qv_sums):
    shape = jax.ShapeDtypeStruct((16, sums.shape[1]), F32)
    return pl.pallas_call(
        pack_small_kernel, out_shape=[shape, shape], cost_estimate=cost(0, 2**18), name="pack_small"
    )(sums, *up_sums, *qv_sums)


def shards(
    tokens_in,
    seg_lengths,
    pad_counts,
    w_qkv,
    qv_bias,
    w_out,
    out_bias,
    norm1_gain,
    norm1_bias,
    w_up,
    up_bias,
    w_down,
    down_bias,
    norm2_gain,
    norm2_bias,
    cotangent,
):
    tokens, width = tokens_in.shape
    local = w_qkv.shape[2]
    me = lax.axis_index("dp")
    rows_here = tokens // SEQ
    slot = jnp.arange(13, dtype=jnp.int32)
    start = lax.axis_index("mp") * rows_here
    quarters = jnp.array([0, 2, 1, 3, 0, 0, 0, 0, 0, 0, 2, 1, 3], jnp.int32)
    quarters = quarters ^ jnp.where(slot < 4, me & 3, (me & CORE) | ((me & Z1) // 2))
    bits = jnp.where(slot == 4, start, (me >> jnp.clip(slot - 5, 0, 3)) & 1)
    info = jnp.where((slot < 4) | (slot > 8), quarters, bits)
    vectors = jnp.stack([out_bias, norm1_gain, norm1_bias, down_bias, norm2_gain, norm2_bias])
    up_bias = up_bias.reshape(-1, width)

    attn_w = pack_attn(info, w_qkv, w_out, qv_bias)
    up_w, down_w, q_aug, k_aug = pack_ffn(
        info, rows_here, seg_lengths, w_up, w_down, tie(up_bias, attn_w)
    )
    attn_w, up_w, down_w = over_mp(attn_w), over_mp(up_w), over_mp(down_w)
    early = local // PAIR - 1
    attn_args = (info, pad_counts, q_aug, k_aug)
    fwd_m = attn_fwd(tokens_in, w_qkv, qv_bias, *attn_args, span=(0, early))
    attn_w = tie(attn_w, fwd_m[1])
    attn_y, attn_core = over_dp(attn_w, Y), over_dp(attn_w, CORE)
    bias_m = tie(qv_bias, attn_w)
    fwd_m = attn_fwd(
        tokens_in, w_qkv, bias_m, *attn_args, span=(early, local // PAIR), into=fwd_m
    )
    up_w = tie(up_w, fwd_m[1])
    up_y = over_dp(up_w, Y)
    attn_core = tie(attn_core, up_w)
    attn_y = tie(attn_y, attn_core)
    w_qkv_o, w_out_o, qv_bias_o = unpack(
        unpack_attn_kernel,
        info,
        (attn_w, attn_y, attn_core, over_dp(attn_y, CORE)),
        (w_qkv, w_out, qv_bias),
    )
    w_qkvs, w_outs = (w_qkv, w_qkv_o), (w_out, w_out_o)
    fwd_o = attn_fwd(tokens_in, w_qkv_o, qv_bias_o, *attn_args)
    qkv, ctx, probs, rinv = zip(fwd_m, fwd_o)
    down_w, up_y, up_w = lax.optimization_barrier((down_w, up_y, up_w, ctx[1]))[:3]
    down_z = over_dp(down_w, Z1)
    up_core, up_both, down_core = over_dp(up_w, CORE), over_dp(up_y, CORE), over_dp(down_w, CORE)
    mid, xhat, rstd, part, act_m, slope_m = ffn_front(
        info, (ctx[0], tie(ctx[1], down_w)), tokens_in, w_outs, vectors, w_up, up_bias, w_down
    )
    down_z, up_core, up_both, down_core = lax.optimization_barrier(
        (down_z, up_core, up_both, down_core, mid)
    )[:4]
    w_up_o, w_down_o, up_bias_o = unpack(
        unpack_ffn_kernel,
        info,
        (up_w, up_y, up_core, up_both, down_w, down_z, down_core, over_dp(down_z, CORE)),
        (w_up, w_down, up_bias),
    )
    (
        tokens_out, pooled, act_o, grad_branch, upper_m, upper_o, grad_resid, grad_attended,
        sums, up_sum_m, up_sum_o,
    ) = ffn_back(
        info, pad_counts, mid, xhat, rstd, part, slope_m, cotangent, (w_up, w_up_o),
        (w_down, w_down_o), up_bias_o, vectors,
    )

    down = Chain(info, [CORE, "x", Z1, Y, Z2])
    up = Chain(info, [CORE, "x", Z1, Y, Z2])
    attn = Chain(info, [CORE, Y, "x", Z1, Z2])

    def attn_back(h, *after):
        g_att = tie(grad_attended, *after)
        dx, own, away, qv = attn_bwd(
            info, tokens_in, g_att, w_outs[h], qkv[h], ctx[h], probs[h], rinv[h]
        )
        return dx, own.reshape(-1, width), away.reshape(-1, width), qv

    def weight_grad(a, b, *after):
        return dot(tie(a, *after), b, TN).astype(BF16)

    def input_grad(h, grad_act, *after):
        return jnp.einsum(
            "cte,cde->td", tie(grad_act, *after), w_qkvs[h], preferred_element_type=F32
        )

    away = weight_grad(act_o[1], grad_branch)
    own = weight_grad(act_o[0], grad_branch, away)
    down.send("o", own, away)
    away = weight_grad(act_m[1], grad_branch, own)
    last = down.hop("o", away)
    own = weight_grad(act_m[0], grad_branch, last)
    down.send("m", own, away)
    away = weight_grad(mid, upper_o[1], own)
    own = weight_grad(mid, upper_o[0], away)
    up.send("o", own, away)
    last = down.hop("m", own)
    away = weight_grad(mid, upper_m[1], last)
    last = up.hop("o", away)
    own = weight_grad(mid, upper_m[0], last)
    up.send("m", own, away)
    dx_o, own, away, qv_o = attn_back(1, own)
    attn.send("o", own, away)
    last = up.hop("m", own)
    last = down.hop("m", last)
    last = attn.hop("o", last)
    dx_m, own, away, qv_m = attn_back(0, last)
    attn.send("m", own, away)
    small, small_send = pack_small(sums, (up_sum_m, up_sum_o), (qv_m, qv_o))
    last = down.hop("m", small)
    last = attn.hop("o", last)
    last = up.hop("m", last)
    last = attn.hop("m", last)
    small_got = over_mp(tie(small_send, last))
    count, bit = lax.axis_size("dp"), 1
    for what in "duadsaudsaudsaudasusgapua":
        if what == "s":
            last = small = tie(small, last) + small_got
            if bit < count:
                small_got = over_dp(small, bit)
                bit *= 2
        elif what == "g":
            total = input_grad(1, dx_o, last) + grad_resid
            total = total + input_grad(0, dx_m, last)
            grad_input = last = total.astype(BF16)
        elif what == "p":
            down.held[0] = tie(down.held[0], last)
            (grad_down,) = place(place_kernel, down.held, down.spots(me), w_down.shape)
            last = grad_down
            up.held[-1] = tie(up.held[-1], last)
            attn.held[-1] = tie(attn.held[-1], last)
        else:
            last = {"d": down, "u": up, "a": attn}[what].hop("m", last)
    if bit > 16:
        small = small + small_got
    while bit < count:
        small = small + over_dp(small, bit)
        bit *= 2
    (grad_up,) = place(place_up_kernel, up.held, up.spots(me), w_up.shape)
    grad_qkv, grad_out = place(
        place_attn_kernel, attn.held, attn.spots(me), w_qkv.shape, w_out.shape
    )
    vectors = [small[i] for i in (5, 3, 4, 2, 0, 1)]
    grad_up_bias = small[6:8].reshape(-1)
    grad_qv_bias = small[8].reshape(2, local)
    return (
        tokens_out,
        pooled,
        grad_input,
        grad_qkv,
        grad_qv_bias,
        grad_out,
        vectors[0],
        vectors[1],
        vectors[2],
        grad_up,
        grad_up_bias,
        grad_down,
        vectors[3],
        vectors[4],
        vectors[5],
    )


def solution(mesh):
    token = P(("dp", "mp"), None)
    in_specs = (
        token,
        P("dp", None),
        P("dp"),
        P(None, None, "mp"),
        P(None, "mp"),
        P("mp", None),
        P(),
        P(),
        P(),
        P(None, "mp"),
        P("mp"),
        P("mp", None),
        P(),
        P(),
        P(),
        token,
    )
    out_specs = (
        token,
        token,
        token,
        P(None, None, "mp"),
        P(None, "mp"),
        P("mp", None),
        P(),
        P(),
        P(),
        P(None, "mp"),
        P("mp"),
        P("mp", None),
        P(),
        P(),
        P(),
    )
    return jax.shard_map(shards, mesh=mesh, in_specs=in_specs, out_specs=out_specs, check_vma=False)
```

```python
import functools

import jax
import jax.numpy as jnp
from jax import lax
from jax.experimental import pallas as pl
from jax.experimental.pallas import tpu as pltpu
from jax.sharding import PartitionSpec as P

HD = 64
SEQ = 512
PAIR = 128
EPSILON = 1e-12
SCORE_SCALE = 0.125
GELU_COEF = 0.7978845608028654
LOG2_E = 1.4426950408889634
MASKED = -1e30
F32 = jnp.float32
BF16 = jnp.bfloat16

NT = (((1,), (1,)), ((), ()))
NN = (((1,), (0,)), ((), ()))
TN = (((0,), (0,)), ((), ()))


TILE = 256
HINT = 8.0
VMEM_LIMIT = 56 * 2**20
CORE, Y, Z1, Z2 = 1, 2, 4, 8
SLOT = {CORE: 5, Y: 6, Z1: 7, Z2: 8}


def cost(gflop, size):
    return pl.CostEstimate(
        flops=int(gflop * HINT * 1e9), bytes_accessed=int(size * HINT), transcendentals=0
    )


def dot(a, b, dims=NN):
    return lax.dot_general(a, b, dims, preferred_element_type=F32)


def attn_fwd_kernel(
    info_ref, pad_ref, x_ref, w_ref, bias_ref, qa_ref, ka_ref, qkv_ref, ctx_ref, e_ref, rinv_ref
):
    limit = SEQ - pad_ref[info_ref[4] + pl.program_id(0)]
    w = jnp.concatenate([w_ref[0], w_ref[1], w_ref[2]], axis=1)
    qkv = dot(x_ref[...], w)
    bias = bias_ref[...].astype(F32)
    q = (qkv[:, :PAIR] + bias[0:1]).astype(BF16)
    k = qkv[:, PAIR : 2 * PAIR].astype(BF16)
    v = (qkv[:, 2 * PAIR :] + bias[1:2]).astype(BF16)
    qkv_ref[0], qkv_ref[1], qkv_ref[2] = q, k, v
    v_t = v.astype(F32).T.astype(BF16)
    low = lax.broadcasted_iota(jnp.int32, (SEQ, PAIR), 1) < HD
    j = lax.broadcasted_iota(jnp.int32, (64, SEQ), 0) + (SEQ - 64)
    i = lax.broadcasted_iota(jnp.int32, (64, SEQ), 1)
    seen = (j < limit) | (j == i)
    scores, weights = [], []
    for h in range(2):
        own = low if h == 0 else ~low
        scores.append(dot(jnp.where(own, k, ka_ref[0]), jnp.where(own, q, qa_ref[0]), NT))
    for h in range(2):
        tail = jnp.where(seen, scores[h][SEQ - 64 :], MASKED)
        s = jnp.concatenate([scores[h][: SEQ - 64], tail], axis=0)
        peak = jnp.max(s, axis=0, keepdims=True)
        e = jnp.exp2((s - peak) * (SCORE_SCALE * LOG2_E))
        rinv = 1.0 / jnp.sum(e, axis=0, keepdims=True)
        eb = e.astype(BF16)
        e_ref[h] = eb
        rinv_ref[0, 0, h : h + 1, :] = rinv
        weights.append((eb, rinv))
    parts = [dot(v_t[h * HD : (h + 1) * HD], e) * rinv for h, (e, rinv) in enumerate(weights)]
    ctx_ref[...] = jnp.concatenate(parts, axis=0).T.astype(BF16)


def attn_fwd(tokens, w_qkv, bias, info, pads, q_aug, k_aug, span=None, into=None):
    rows, width = tokens.shape[0] // SEQ, w_qkv.shape[2]
    pairs, model = width // PAIR, tokens.shape[1]
    first, end = span or (0, pairs)
    aug = pl.BlockSpec((1, SEQ, PAIR), lambda r, p, *_: (r, 0, 0))
    into = list(into or ())
    kernel = attn_fwd_kernel
    if into:
        kernel = lambda *refs: attn_fwd_kernel(*refs[:7], *refs[7 + len(into) :])
    return pl.pallas_call(
        kernel,
        grid_spec=pltpu.PrefetchScalarGridSpec(
            num_scalar_prefetch=2,
            grid=(rows, end - first),
            in_specs=[
                pl.BlockSpec((SEQ, model), lambda r, p, *_: (r, 0)),
                pl.BlockSpec((3, model, PAIR), lambda r, p, *_: (0, 0, first + p)),
                pl.BlockSpec((2, PAIR), lambda r, p, *_: (0, first + p)),
                aug,
                aug,
            ]
            + [pl.BlockSpec(memory_space=pl.ANY)] * len(into),
            out_specs=[
                pl.BlockSpec((3, SEQ, PAIR), lambda r, p, *_: (0, r, first + p)),
                pl.BlockSpec((SEQ, PAIR), lambda r, p, *_: (r, first + p)),
                pl.BlockSpec((2, SEQ, SEQ), lambda r, p, *_: (r * pairs + first + p, 0, 0)),
                pl.BlockSpec((1, 1, 2, SEQ), lambda r, p, *_: (r, first + p, 0, 0)),
            ],
        ),
        out_shape=[
            pltpu.HBM((3, rows * SEQ, width), BF16),
            jax.ShapeDtypeStruct((rows * SEQ, width), BF16),
            pltpu.HBM((rows * pairs * 2, SEQ, SEQ), BF16),
            jax.ShapeDtypeStruct((rows, pairs, 2, SEQ), F32),
        ],
        input_output_aliases={7 + i: i for i in range(len(into))},
        compiler_params=pltpu.CompilerParams(vmem_limit_bytes=24 * 2**20),
        cost_estimate=cost(1e-4, 1e3),
        name="attn_fwd",
    )(info, pads, tokens, w_qkv, bias, q_aug, k_aug, *into)


def attn_bwd_kernel(
    info_ref, x_ref, ga_ref, wo_ref, qkv_ref, ctx_ref, e_ref, rinv_ref,
    out_ref, own_ref, away_ref, gb_ref, acc_ref,
):
    row, last = pl.program_id(1), pl.num_programs(1) - 1
    q, k, v = qkv_ref[0], qkv_ref[1], qkv_ref[2]
    k_t = k.astype(F32).T.astype(BF16)
    d_t = dot(wo_ref[...], ga_ref[...], NT).astype(BF16).astype(F32)
    c_t = ctx_ref[...].astype(F32).T
    lane = lax.broadcasted_iota(jnp.int32, (SEQ, PAIR), 1)
    row8 = lax.broadcasted_iota(jnp.int32, (8, SEQ), 0)
    low = lane < HD
    ones = jnp.where((lane & (HD - 1)) < 2, 1.0, 0.0).astype(BF16)
    dv, dk, dq = [], [], []
    for h in range(2):
        own = low if h == 0 else ~low
        rinv = rinv_ref[0, 0, h : h + 1, :]
        mine = d_t[h * HD : (h + 1) * HD] * rinv
        minus = -jnp.sum(mine * c_t[h * HD : (h + 1) * HD], axis=0, keepdims=True)
        high = minus.astype(BF16).astype(F32)
        extra = jnp.where(row8 == 0, high, jnp.where(row8 == 1, minus - high, 0.0))
        blank = jnp.zeros((HD - 8, SEQ), F32)
        stack = [mine, extra, blank] if h == 0 else [extra, blank, mine]
        g_t = jnp.concatenate(stack, axis=0).astype(BF16)
        v_h = jnp.where(own, v, ones)
        e = e_ref[h]
        d = e * dot(v_h, g_t).astype(BF16)
        dv.append(dot(e, g_t, NT))
        dk.append(dot(d, q))
        dq.append(dot(k_t[h * HD : (h + 1) * HD], d))
    dq_t = jnp.concatenate(dq, axis=0) * SCORE_SCALE
    dk = jnp.where(low, dk[0], dk[1]) * SCORE_SCALE
    dv = jnp.where(low, dv[0], dv[1])
    dq_b = dq_t.T.astype(BF16)
    dk_b, dv_b = dk.astype(BF16), dv.astype(BF16)
    out_ref[0], out_ref[1], out_ref[2] = dq_b, dk_b, dv_b
    left = jnp.concatenate([dq_t, dk.T, dv.T], axis=0).astype(BF16)
    g_w = dot(left, x_ref[...]).reshape(3, PAIR, x_ref.shape[1])
    g_o = dot(c_t.astype(BF16), ga_ref[...])
    g_b = jnp.concatenate(
        [
            jnp.sum(dq_b.astype(F32), axis=0, keepdims=True),
            jnp.sum(dv_b.astype(F32), axis=0, keepdims=True),
        ],
        axis=0,
    )

    @pl.when(row == 0)
    def _():
        acc_ref[:3] = g_w
        acc_ref[3] = g_o
        gb_ref[...] = g_b

    @pl.when(row > 0)
    def _():
        acc_ref[:3] += g_w
        acc_ref[3] += g_o
        gb_ref[...] += g_b

    @pl.when(row == last)
    def _():
        core = info_ref[SLOT[CORE]]
        own_ref[...] = acc_ref[pl.ds(2 * core, 2)].astype(BF16)
        away_ref[...] = acc_ref[pl.ds(2 * (1 - core), 2)].astype(BF16)


def attn_bwd(info, tokens, grad_att, w_out, qkv, ctx, e, rinv):
    rows, pairs = rinv.shape[0], rinv.shape[1]
    width, model = qkv.shape[2], tokens.shape[1]
    wide = pl.BlockSpec((SEQ, model), lambda p, r, _: (r, 0))
    triple = pl.BlockSpec((3, SEQ, PAIR), lambda p, r, _: (0, r, p))
    half = pl.BlockSpec((2, PAIR, model), lambda p, r, _: (0, p, 0))
    return pl.pallas_call(
        attn_bwd_kernel,
        grid_spec=pltpu.PrefetchScalarGridSpec(
            num_scalar_prefetch=1,
            grid=(pairs, rows),
            in_specs=[
                wide,
                wide,
                pl.BlockSpec((PAIR, model), lambda p, r, _: (p, 0)),
                triple,
                pl.BlockSpec((SEQ, PAIR), lambda p, r, _: (r, p)),
                pl.BlockSpec((2, SEQ, SEQ), lambda p, r, _: (r * pairs + p, 0, 0)),
                pl.BlockSpec((1, 1, 2, SEQ), lambda p, r, _: (r, p, 0, 0)),
            ],
            out_specs=[
                triple,
                half,
                half,
                pl.BlockSpec((2, PAIR), lambda p, r, _: (0, p)),
            ],
            scratch_shapes=[pltpu.VMEM((4, PAIR, model), F32)],
        ),
        out_shape=[
            pltpu.HBM((3, rows * SEQ, width), BF16),
            pltpu.HBM((2, width, model), BF16),
            pltpu.HBM((2, width, model), BF16),
            jax.ShapeDtypeStruct((2, width), F32),
        ],
        compiler_params=pltpu.CompilerParams(vmem_limit_bytes=24 * 2**20),
        cost_estimate=cost(8 * rows, rows * pairs * 2 * SEQ * SEQ * 2),
        name="attn_bwd",
    )(info, tokens, grad_att, w_out, qkv, ctx, pltpu.with_memory_space_constraint(e, pltpu.HBM), rinv)


def vector(x):
    return pl.BlockSpec(x.shape, lambda *_: (0,) * x.ndim)


def normalise(v):
    centered = v - jnp.mean(v, axis=-1, keepdims=True)
    rstd = lax.rsqrt(jnp.mean(centered * centered, axis=-1, keepdims=True) + EPSILON)
    return centered * rstd, rstd


def normalise_back(dy, xhat, rstd, gain):
    dg = dy * gain
    return rstd * (
        dg
        - jnp.mean(dg, axis=-1, keepdims=True)
        - xhat * jnp.mean(dg * xhat, axis=-1, keepdims=True)
    )


def gelu_and_slope(u):
    u2 = u * u
    t = jnp.tanh(u * (GELU_COEF + (GELU_COEF * 0.044715) * u2))
    half = 0.5 + 0.5 * t
    act = u * half
    slope = half * (1.0 + u * (1.0 - t) * (GELU_COEF + (3 * GELU_COEF * 0.044715) * u2))
    return act, slope


def flat_bias(ref):
    b = ref[...].astype(F32)
    return jnp.concatenate([b[i : i + 1] for i in range(b.shape[0])], axis=1)


def by_core(core, x, ref):
    half = x.shape[1] // 2
    ref[core] = x[:, :half]
    ref[1 - core] = x[:, half:]


def units(core, mid, acc, wu_ref, ub_ref, wd_ref, act_ref, slope_ref):
    act, slope = gelu_and_slope(dot(mid, wu_ref[...]) + flat_bias(ub_ref))
    act = act.astype(BF16)
    by_core(core, act, act_ref)
    slope_ref[...] = slope.astype(BF16)
    return acc + dot(act, wd_ref[...])


def ffn_front_kernel(
    info_ref, cm_ref, co_ref, x_ref, wm_ref, wo_ref, vec_ref, wu_ref, ub_ref, wd_ref,
    mid_ref, xhat_ref, rstd_ref, part_ref, act_ref, slope_ref,
):
    vec = vec_ref[...].astype(F32)
    attended = dot(cm_ref[...], wm_ref[...]) + dot(co_ref[...], wo_ref[...])
    resid = x_ref[...].astype(F32) + (attended + vec[0:1])
    xhat, rstd = normalise(resid)
    normed = xhat * vec[1:2] + vec[2:3]
    mid = normed.astype(BF16)
    mid_ref[...] = mid
    xhat_ref[...] = xhat
    rstd_ref[...] = rstd
    part_ref[...] = units(
        info_ref[SLOT[CORE]], mid, normed + vec[3:4], wu_ref, ub_ref, wd_ref,
        act_ref, slope_ref,
    )


def halves(hidden, n=None):
    if n is None:
        return pl.BlockSpec((2, TILE, hidden // 2), lambda t, *_: (0, t, 0))
    return jax.ShapeDtypeStruct((2, n, hidden // 2), BF16)


def ffn_front(info, ctx, tokens, w_outs, vectors, w_up, up_bias, w_down):
    n, model = tokens.shape
    width, hidden = ctx[0].shape[1], w_up.shape[1]
    row = lambda c: pl.BlockSpec((TILE, c), lambda t, *_: (t, 0))
    shape = lambda c, d: jax.ShapeDtypeStruct((n, c), d)
    fixed = [vectors, w_up, up_bias, w_down]
    outs = [(model, BF16), (model, F32), (1, F32), (model, F32)]
    return pl.pallas_call(
        ffn_front_kernel,
        grid_spec=pltpu.PrefetchScalarGridSpec(
            num_scalar_prefetch=1,
            grid=(n // TILE,),
            in_specs=[row(width), row(width), row(model)] + [vector(a) for a in (*w_outs, *fixed)],
            out_specs=[row(c) for c, _ in outs] + [halves(hidden), row(hidden)],
        ),
        out_shape=[shape(*o) for o in outs] + [halves(hidden, n), shape(hidden, BF16)],
        compiler_params=pltpu.CompilerParams(vmem_limit_bytes=48 * 2**20),
        cost_estimate=cost(10, n * model * 24),
        name="ffn_front",
    )(info, *ctx, tokens, *w_outs, *fixed)


def ffn_back_kernel(
    info_ref, pad_ref, mid_ref, xhat_ref, rstd_ref, part_ref, slope_m_ref, cot_ref,
    wu_m_ref, wd_m_ref, wu_o_ref, ub_o_ref, wd_o_ref, vec_ref,
    out_ref, pool_ref, act_ref, branch_ref, um_ref, uo_ref, resid_ref, att_ref, sums_ref, ub_m_sum_ref, ub_o_sum_ref, slope_ref,
):
    t = pl.program_id(0)
    per_row = SEQ // TILE
    mid = mid_ref[...]
    core = info_ref[SLOT[CORE]]
    second = units(
        core, mid, part_ref[...], wu_o_ref, ub_o_ref, wd_o_ref, act_ref, slope_ref
    )
    vec = vec_ref[...].astype(F32)
    gain_two = vec[4:5]
    xhat_two, rstd_two = normalise(second)
    final = xhat_two * gain_two + vec[5:6]
    out_ref[...] = final.astype(BF16)
    count = SEQ - pad_ref[info_ref[4] + t // per_row]
    slot = lax.broadcasted_iota(jnp.int32, (TILE, 1), 0) + (t % per_row) * TILE
    pooled = jnp.sum(jnp.where(slot < count, final, 0.0), axis=0, keepdims=True)
    pooled = pooled / count.astype(F32)
    which = lax.broadcasted_iota(jnp.int32, pool_ref.shape, 0) == t // per_row
    pooled = jnp.where(which, pooled, 0.0)

    dy = cot_ref[...].astype(F32)
    down = lambda v: jnp.sum(v, axis=0, keepdims=True)
    sums = [down(dy * xhat_two), down(dy)]
    second_grad = normalise_back(dy, xhat_two, rstd_two, gain_two)
    branch = second_grad.astype(BF16)
    branch_ref[...] = branch
    sums.append(down(branch.astype(F32)))
    normed_grad = second_grad
    bias_sums = []
    for wu_ref, wd_ref, s_ref, up_ref in (
        (wu_o_ref, wd_o_ref, slope_ref, uo_ref),
        (wu_m_ref, wd_m_ref, slope_m_ref, um_ref),
    ):
        upper = (dot(branch, wd_ref[...], NT) * s_ref[...].astype(F32)).astype(BF16)
        by_core(core, upper, up_ref)
        bias_sums.append(down(upper.astype(F32)))
        normed_grad = normed_grad + dot(upper, wu_ref[...], NT)
    xhat_one = xhat_ref[...]
    sums += [down(normed_grad * xhat_one), down(normed_grad)]
    resid = normalise_back(normed_grad, xhat_one, rstd_ref[...], vec[1:2])
    resid_ref[...] = resid
    att = resid.astype(BF16)
    att_ref[...] = att
    sums.append(down(att.astype(F32)))
    sums = jnp.concatenate(sums, axis=0)

    @pl.when(t == 0)
    def _():
        pool_ref[...] = pooled
        sums_ref[...] = sums
        ub_o_sum_ref[...] = bias_sums[0]
        ub_m_sum_ref[...] = bias_sums[1]

    @pl.when(t > 0)
    def _():
        pool_ref[...] += pooled
        sums_ref[...] += sums
        ub_o_sum_ref[...] += bias_sums[0]
        ub_m_sum_ref[...] += bias_sums[1]


def ffn_back(info, pads, mid, xhat, rstd, part, slope, cot, w_ups, w_downs, up_bias_o, vectors):
    n, model = mid.shape
    hidden, rows = slope.shape[1], n // SEQ
    row = lambda c: pl.BlockSpec((TILE, c), lambda t, *_: (t, 0))
    keep = lambda r, c: pl.BlockSpec((r, c), lambda t, *_: (0, 0))
    shape = lambda c, d: jax.ShapeDtypeStruct((n, c), d)
    fixed = [w_ups[0], w_downs[0], w_ups[1], up_bias_o, w_downs[1], vectors]
    return pl.pallas_call(
        ffn_back_kernel,
        grid_spec=pltpu.PrefetchScalarGridSpec(
            num_scalar_prefetch=2,
            grid=(n // TILE,),
            in_specs=[row(model), row(model), row(1), row(model), row(hidden), row(model)]
            + [vector(a) for a in fixed],
            out_specs=[row(model), keep(rows, model), halves(hidden), row(model)]
            + [halves(hidden)] * 2
            + [row(model), row(model), keep(6, model), keep(1, hidden), keep(1, hidden)],
            scratch_shapes=[pltpu.VMEM((TILE, hidden), BF16)],
        ),
        out_shape=[
            shape(model, BF16),
            jax.ShapeDtypeStruct((rows, model), F32),
            halves(hidden, n),
            shape(model, BF16),
        ]
        + [halves(hidden, n)] * 2
        + [
            shape(model, F32),
            shape(model, BF16),
            jax.ShapeDtypeStruct((6, model), F32),
            jax.ShapeDtypeStruct((1, hidden), F32),
            jax.ShapeDtypeStruct((1, hidden), F32),
        ],
        compiler_params=pltpu.CompilerParams(vmem_limit_bytes=40 * 2**20),
        cost_estimate=cost(25, n * model * 40),
        name="ffn_back",
    )(info, pads, mid, xhat, rstd, part, slope, cot, *fixed)


def pack_attn_kernel(info_ref, wq_ref, wo_ref, qb_ref, attn_ref):
    r, w = wq_ref.shape[1:]
    attn_ref[:r, :w] = wq_ref[0]
    attn_ref[:r, w:] = wq_ref[1]
    attn_ref[r : r + r // 2, :w] = wq_ref[2, : r // 2]
    attn_ref[r : r + r // 2, w:] = wq_ref[2, r // 2 :]
    at = r + r // 2
    attn_ref[at : at + wo_ref.shape[0], :] = wo_ref[...]
    at += wo_ref.shape[0]
    attn_ref[at:, :] = jnp.zeros((16, 2 * w), BF16)
    attn_ref[at : at + 2, :w] = qb_ref[...]


def pack_ffn_kernel(info_ref, seg_ref, wu_ref, wd_ref, ub_ref, up_ref, down_ref, qa_ref, ka_ref):
    u, c = wu_ref.shape[0], up_ref.shape[1]
    up_ref[:u, :] = wu_ref[:, :c]
    up_ref[u : 2 * u, :] = wu_ref[:, c:]
    up_ref[2 * u :, :] = jnp.zeros((16, c), BF16)
    up_ref[2 * u : 2 * u + 2, :] = ub_ref[...]
    down_ref[...] = wd_ref[...]
    segs = seg_ref.shape[1]
    slot = lax.broadcasted_iota(jnp.int32, (SEQ, PAIR), 0)
    lane = lax.broadcasted_iota(jnp.int32, (SEQ, PAIR), 1) & (HD - 1)
    for row in range(qa_ref.shape[0]):
        end, segment = 0, jnp.zeros((SEQ, PAIR), jnp.int32)
        for s in range(segs):
            end = end + seg_ref[info_ref[4] + row, s]
            segment = segment + jnp.where(slot >= end, 1, 0)
        same = lane == segment
        ka_ref[row] = jnp.where(same & (lane < segs), 1.0, 0.0).astype(BF16)
        qa_ref[row] = jnp.where((lane < segs) & ~same, MASKED, 0.0).astype(BF16)


def pack_attn(info, w_qkv, w_out, qv_bias):
    model, width = w_qkv.shape[1:]
    out_rows = w_out.shape[0] // 4
    shape = (3 * width // 4 + out_rows + 16, model)
    whole = lambda s: pl.BlockSpec(s, lambda i, *_: (0,) * len(s))
    return pl.pallas_call(
        pack_attn_kernel,
        grid_spec=pltpu.PrefetchScalarGridSpec(
            num_scalar_prefetch=1,
            grid=(1,),
            in_specs=[
                pl.BlockSpec((3, model // 4, width), lambda i, at: (0, at[0], 0)),
                pl.BlockSpec((out_rows, model), lambda i, at: (at[0], 0)),
                whole(qv_bias.shape),
            ],
            out_specs=whole(shape),
        ),
        out_shape=jax.ShapeDtypeStruct(shape, BF16),
        cost_estimate=cost(0, 2 * 2**20),
        name="pack_attn",
    )(info, w_qkv, w_out, qv_bias)


def pack_ffn(info, rows, seg_lengths, w_up, w_down, up_bias):
    model = w_up.shape[0]
    up_rows, down_rows = model // 4, w_down.shape[0] // 4
    whole = lambda s: pl.BlockSpec(s, lambda i, *_: (0,) * len(s))
    shapes = [(2 * up_rows + 16, model), (down_rows, model)] + [(rows, SEQ, PAIR)] * 2
    return pl.pallas_call(
        pack_ffn_kernel,
        grid_spec=pltpu.PrefetchScalarGridSpec(
            num_scalar_prefetch=2,
            grid=(1,),
            in_specs=[
                pl.BlockSpec((up_rows, w_up.shape[1]), lambda i, at, _: (at[0], 0)),
                pl.BlockSpec((down_rows, model), lambda i, at, _: (at[9], 0)),
                whole(up_bias.shape),
            ],
            out_specs=[whole(s) for s in shapes],
        ),
        out_shape=[jax.ShapeDtypeStruct(s, BF16) for s in shapes],
        cost_estimate=cost(0, 4 * 2**20),
        name="pack_ffn",
    )(info, seg_lengths, w_up, w_down, up_bias)


def unpack_attn_kernel(at_ref, *refs):
    pieces, (wq_ref, wo_ref, qb_ref) = refs[:4], refs[4:]
    r, w, o = wq_ref.shape[1] // 4, wq_ref.shape[2], wo_ref.shape[0] // 4
    for i, piece in enumerate(pieces):
        q = at_ref[i]
        rows = pl.ds(pl.multiple_of(q * r, 16), r)
        wq_ref[0, rows, :] = piece[:r, :w]
        wq_ref[1, rows, :] = piece[:r, w:]
        wq_ref[2, pl.ds(pl.multiple_of(q * r, 16), r // 2), :] = piece[r : r + r // 2, :w]
        wq_ref[2, pl.ds(pl.multiple_of(q * r + r // 2, 16), r // 2), :] = piece[r : r + r // 2, w:]
        at = r + r // 2
        wo_ref[pl.ds(pl.multiple_of(q * o, 16), o), :] = piece[at : at + o, :]
    at += o
    qb_ref[...] = pieces[0][at : at + 2, :w]


def unpack_ffn_kernel(at_ref, *refs):
    ups, downs, (wu_ref, wd_ref, ub_ref) = refs[:4], refs[4:8], refs[8:]
    r, c, d = wu_ref.shape[0] // 4, wu_ref.shape[1] // 2, wd_ref.shape[0] // 4
    for i in range(4):
        rows = pl.ds(pl.multiple_of(at_ref[i] * r, 16), r)
        wu_ref[rows, :c] = ups[i][:r, :]
        wu_ref[rows, c:] = ups[i][r : 2 * r, :]
        wd_ref[pl.ds(pl.multiple_of(at_ref[9 + i] * d, 16), d), :] = downs[i][...]
    ub_ref[...] = ups[0][2 * r : 2 * r + 2, :]


def unpack(kernel, at, pieces, like):
    whole = pl.BlockSpec(memory_space=pltpu.VMEM)
    return pl.pallas_call(
        kernel,
        in_specs=[pl.BlockSpec(memory_space=pltpu.SMEM)] + [whole] * len(pieces),
        out_specs=[whole] * len(like),
        out_shape=[jax.ShapeDtypeStruct(a.shape, BF16) for a in like],
        compiler_params=pltpu.CompilerParams(vmem_limit_bytes=32 * 2**20),
        cost_estimate=cost(0, 5 * 2**20),
        name=kernel.__name__,
    )(at, *pieces)


def over_mp(x):
    n = lax.axis_size("mp")
    return lax.ppermute(x, "mp", [(i, i ^ 1) for i in range(n)])


def over_dp(x, bit):
    n = lax.axis_size("dp")
    return lax.ppermute(x, "dp", [(i, i ^ bit) for i in range(n)])


def gather_pieces(rows, at_ref, refs, store):
    k = 0
    for ref in refs:
        for i in range(ref.shape[0] // rows):
            spot = pl.ds(pl.multiple_of(at_ref[k] * rows, 16), rows)
            store(spot, ref[i * rows : (i + 1) * rows, :].astype(F32))
            k += 1


def place_kernel(rows, at_ref, *refs):
    out_ref = refs[-1]

    def store(spot, value):
        out_ref[spot, :] = value

    gather_pieces(rows, at_ref, refs[:-1], store)


def place_up_kernel(rows, at_ref, *refs):
    out_ref = refs[-1]
    height, width = out_ref.shape[0], out_ref.shape[1] // 2
    k = 0
    for ref in refs[:-1]:
        for i in range(ref.shape[0] // rows):
            place, count = at_ref[k], height // rows
            spot = pl.ds(pl.multiple_of(place % count * rows, 16), rows)
            columns = pl.ds(pl.multiple_of(place // count * width, 128), width)
            out_ref[spot, columns] = ref[i * rows : (i + 1) * rows, :].astype(F32)
            k += 1


def place_attn_kernel(rows, at_ref, *refs):
    qkv_ref, out_ref, held_ref = refs[-3:]

    def store(spot, value):
        held_ref[spot, :] = value

    gather_pieces(rows, at_ref, refs[:-3], store)
    width = qkv_ref.shape[2]
    for c in range(3):
        for e in range(0, width, PAIR):
            qkv_ref[c, :, e : e + PAIR] = held_ref[c * width + e : c * width + e + PAIR, :].T
    out_ref[...] = held_ref[3 * width :, :]


def place(kernel, pieces, at, *shapes):
    total, cols = sum(piece.shape[0] for piece in pieces), pieces[0].shape[1]
    whole = pl.BlockSpec(memory_space=pltpu.VMEM)
    return pl.pallas_call(
        functools.partial(kernel, total // at.shape[0]),
        in_specs=[pl.BlockSpec(memory_space=pltpu.SMEM)] + [whole] * len(pieces),
        out_specs=[whole] * len(shapes),
        out_shape=[jax.ShapeDtypeStruct(s, F32) for s in shapes],
        scratch_shapes=[] if len(shapes) == 1 else [pltpu.VMEM((total, cols), F32)],
        compiler_params=pltpu.CompilerParams(vmem_limit_bytes=32 * 2**20),
        cost_estimate=cost(0, 6 * total * cols),
        name=kernel.__name__,
    )(at, *pieces)


def tie(x, *after):
    return lax.optimization_barrier((x,) + after)[0]


def land(info, x, got, own=None, step=None):
    n = got.shape[0]
    if own is not None:
        x = lax.dynamic_slice_in_dim(x, info[own] * n, n, 0)
    total = (x.astype(F32) + got.astype(F32)).astype(BF16)
    if step is None:
        return total
    return total, lax.dynamic_slice_in_dim(total, (1 - info[step]) * (n // 2), n // 2, 0)


def arrive(after, *flights):
    held = [c.crossed if part == "x" else c.got[part] for c, part in flights]
    held = lax.optimization_barrier((*held, after))
    for (c, part), got in zip(flights, held):
        if part == "x":
            c.crossed = got
        else:
            c.got[part] = got


class Chain:
    def __init__(self, info, bits):
        self.info, self.bits = info, bits
        self.dp_bits = [b for b in bits if b != "x"]
        self.order = [0]
        for b in reversed(self.dp_bits):
            self.order += [o ^ b for o in self.order]
        self.x, self.got, self.own, self.at = {}, {}, {}, {}
        self.held, self.back = None, list(reversed(self.dp_bits))

    def send(self, part, own, away):
        self.got[part] = over_dp(away, self.bits[0])
        self.x[part], self.own[part], self.at[part] = own, None, 0

    def hop(self, part="m", *after):
        if self.held is not None:
            return self.double(*after)
        x, at = tie(self.x[part], *after), self.at[part]
        got = self.crossed if self.bits[at] == "x" else self.got[part]
        bit = self.bits[at + 1] if at + 1 < len(self.bits) else None
        self.at[part] = at + 1
        if bit is None or bit == "x":
            x = land(self.info, x, got, self.own[part])
            self.x[part], self.own[part] = x, None
            if bit is None:
                bit = 2 * max(self.dp_bits)
                while bit < lax.axis_size("dp"):
                    x = land(self.info, x, over_dp(x, bit))
                    bit *= 2
                self.held = [x]
                self.double()
            elif part == "o":
                self.crossed = over_mp(x)
            return x
        x, away = land(self.info, x, got, self.own[part], SLOT[bit])
        self.x[part], self.own[part], self.got[part] = x, SLOT[bit], over_dp(away, bit)
        return x

    def double(self, *after):
        full = jnp.concatenate(self.held, axis=0) if len(self.held) > 1 else self.held[0]
        full = tie(full, *after)
        self.held.append(over_dp(full, self.back.pop(0)))
        return full

    def spots(self, me):
        who = me ^ jnp.array(self.order, jnp.int32)
        spot = jnp.zeros_like(who)
        for b in self.dp_bits:
            spot = 2 * spot + (who & b) // b
        return spot


def pack_small_kernel(sums_ref, um_ref, uo_ref, qm_ref, qo_ref, keep_ref, send_ref):
    n, c, w = sums_ref.shape[0], sums_ref.shape[1], qm_ref.shape[1]
    for out_ref, u_ref, q_ref in ((keep_ref, um_ref, qm_ref), (send_ref, uo_ref, qo_ref)):
        out_ref[...] = jnp.zeros(out_ref.shape, F32)
        out_ref[:n, :] = sums_ref[...]
        for i in range(u_ref.shape[1] // c):
            out_ref[n + i : n + i + 1, :] = u_ref[:, i * c : (i + 1) * c]
        at = n + u_ref.shape[1] // c
        for i in range(2):
            out_ref[at : at + 1, i * w : (i + 1) * w] = q_ref[i : i + 1, :]


def pack_small(sums, up_sums, qv_sums):
    shape = jax.ShapeDtypeStruct((16, sums.shape[1]), F32)
    return pl.pallas_call(
        pack_small_kernel, out_shape=[shape, shape], cost_estimate=cost(0, 2**18), name="pack_small"
    )(sums, *up_sums, *qv_sums)


def shards(
    tokens_in,
    seg_lengths,
    pad_counts,
    w_qkv,
    qv_bias,
    w_out,
    out_bias,
    norm1_gain,
    norm1_bias,
    w_up,
    up_bias,
    w_down,
    down_bias,
    norm2_gain,
    norm2_bias,
    cotangent,
):
    tokens, width = tokens_in.shape
    local = w_qkv.shape[2]
    me = lax.axis_index("dp")
    rows_here = tokens // SEQ
    slot = jnp.arange(13, dtype=jnp.int32)
    start = lax.axis_index("mp") * rows_here
    quarters = jnp.array([0, 2, 1, 3, 0, 0, 0, 0, 0, 0, 2, 1, 3], jnp.int32)
    quarters = quarters ^ jnp.where(slot < 4, me & 3, (me & CORE) | ((me & Z1) // 2))
    bits = jnp.where(slot == 4, start, (me >> jnp.clip(slot - 5, 0, 3)) & 1)
    info = jnp.where((slot < 4) | (slot > 8), quarters, bits)
    vectors = jnp.stack([out_bias, norm1_gain, norm1_bias, down_bias, norm2_gain, norm2_bias])
    up_bias = up_bias.reshape(-1, width)

    attn_w = pack_attn(info, w_qkv, w_out, qv_bias)
    up_w, down_w, q_aug, k_aug = pack_ffn(
        info, rows_here, seg_lengths, w_up, w_down, tie(up_bias, attn_w)
    )
    attn_w, up_w, down_w = over_mp(attn_w), over_mp(up_w), over_mp(down_w)
    early = local // PAIR - 1
    attn_args = (info, pad_counts, q_aug, k_aug)
    fwd_m = attn_fwd(tokens_in, w_qkv, qv_bias, *attn_args, span=(0, early))
    attn_w = tie(attn_w, fwd_m[1])
    attn_y, attn_core = over_dp(attn_w, Y), over_dp(attn_w, CORE)
    bias_m = tie(qv_bias, attn_w)
    fwd_m = attn_fwd(
        tokens_in, w_qkv, bias_m, *attn_args, span=(early, local // PAIR), into=fwd_m
    )
    up_w = tie(up_w, fwd_m[1])
    up_y = over_dp(up_w, Y)
    attn_core = tie(attn_core, up_w)
    attn_y = tie(attn_y, attn_core)
    w_qkv_o, w_out_o, qv_bias_o = unpack(
        unpack_attn_kernel,
        info,
        (attn_w, attn_y, attn_core, over_dp(attn_y, CORE)),
        (w_qkv, w_out, qv_bias),
    )
    w_qkvs, w_outs = (w_qkv, w_qkv_o), (w_out, w_out_o)
    fwd_o = attn_fwd(tokens_in, w_qkv_o, qv_bias_o, *attn_args)
    qkv, ctx, probs, rinv = zip(fwd_m, fwd_o)
    down_w, up_y, up_w = lax.optimization_barrier((down_w, up_y, up_w, ctx[1]))[:3]
    down_z = over_dp(down_w, Z1)
    up_core, up_both, down_core = over_dp(up_w, CORE), over_dp(up_y, CORE), over_dp(down_w, CORE)
    mid, xhat, rstd, part, act_m, slope_m = ffn_front(
        info, (ctx[0], tie(ctx[1], down_w)), tokens_in, w_outs, vectors, w_up, up_bias, w_down
    )
    down_z, up_core, up_both, down_core = lax.optimization_barrier(
        (down_z, up_core, up_both, down_core, mid)
    )[:4]
    w_up_o, w_down_o, up_bias_o = unpack(
        unpack_ffn_kernel,
        info,
        (up_w, up_y, up_core, up_both, down_w, down_z, down_core, over_dp(down_z, CORE)),
        (w_up, w_down, up_bias),
    )
    (
        tokens_out, pooled, act_o, grad_branch, upper_m, upper_o, grad_resid, grad_attended,
        sums, up_sum_m, up_sum_o,
    ) = ffn_back(
        info, pad_counts, mid, xhat, rstd, part, slope_m, cotangent, (w_up, w_up_o),
        (w_down, w_down_o), up_bias_o, vectors,
    )

    down = Chain(info, [CORE, "x", Z1, Y, Z2])
    up = Chain(info, [CORE, "x", Z1, Y, Z2])
    attn = Chain(info, [CORE, Y, "x", Z1, Z2])

    def attn_back(h, *after):
        g_att = tie(grad_attended, *after)
        dx, own, away, qv = attn_bwd(
            info, tokens_in, g_att, w_outs[h], qkv[h], ctx[h], probs[h], rinv[h]
        )
        return dx, own.reshape(-1, width), away.reshape(-1, width), qv

    def weight_grad(a, b, *after):
        return dot(tie(a, *after), b, TN).astype(BF16)

    def input_grad(h, grad_act, *after):
        return jnp.einsum(
            "cte,cde->td", tie(grad_act, *after), w_qkvs[h], preferred_element_type=F32
        )

    away = weight_grad(act_o[1], grad_branch)
    own = weight_grad(act_o[0], grad_branch, away)
    down.send("o", own, away)
    away = weight_grad(act_m[1], grad_branch, own)
    last = down.hop("o", away)
    own = weight_grad(act_m[0], grad_branch, last)
    down.send("m", own, away)
    away = weight_grad(mid, upper_o[1], own)
    own = weight_grad(mid, upper_o[0], away)
    up.send("o", own, away)
    last = down.hop("m", own)
    away = weight_grad(mid, upper_m[1], last)
    last = up.hop("o", away)
    own = weight_grad(mid, upper_m[0], last)
    up.send("m", own, away)
    dx_o, own, away, qv_o = attn_back(1, own)
    attn.send("o", own, away)
    last = up.hop("m", own)
    last = down.hop("m", last)
    last = attn.hop("o", last)
    dx_m, own, away, qv_m = attn_back(0, last)
    attn.send("m", own, away)
    small, small_send = pack_small(sums, (up_sum_m, up_sum_o), (qv_m, qv_o))
    last = down.hop("m", small)
    last = attn.hop("o", last)
    last = up.hop("m", last)
    last = attn.hop("m", last)
    small_got = over_mp(tie(small_send, last))
    count, bit = lax.axis_size("dp"), 1
    for what in "dsuadaudsaudasudasusgapua":
        if what == "s":
            last = small = tie(small, last) + small_got
            if bit < count:
                small_got = over_dp(small, bit)
                bit *= 2
        elif what == "g":
            total = input_grad(1, dx_o, last) + grad_resid
            total = total + input_grad(0, dx_m, last)
            grad_input = last = total.astype(BF16)
        elif what == "p":
            down.held[0] = tie(down.held[0], last)
            (grad_down,) = place(place_kernel, down.held, down.spots(me), w_down.shape)
            last = grad_down
            up.held[-1] = tie(up.held[-1], last)
            attn.held[-1] = tie(attn.held[-1], last)
        else:
            last = {"d": down, "u": up, "a": attn}[what].hop("m", last)
    if bit > 16:
        small = small + small_got
    while bit < count:
        small = small + over_dp(small, bit)
        bit *= 2
    (grad_up,) = place(place_up_kernel, up.held, up.spots(me), w_up.shape)
    grad_qkv, grad_out = place(
        place_attn_kernel, attn.held, attn.spots(me), w_qkv.shape, w_out.shape
    )
    vectors = [small[i] for i in (5, 3, 4, 2, 0, 1)]
    grad_up_bias = small[6:8].reshape(-1)
    grad_qv_bias = small[8].reshape(2, local)
    return (
        tokens_out,
        pooled,
        grad_input,
        grad_qkv,
        grad_qv_bias,
        grad_out,
        vectors[0],
        vectors[1],
        vectors[2],
        grad_up,
        grad_up_bias,
        grad_down,
        vectors[3],
        vectors[4],
        vectors[5],
    )


def solution(mesh):
    token = P(("dp", "mp"), None)
    in_specs = (
        token,
        P("dp", None),
        P("dp"),
        P(None, None, "mp"),
        P(None, "mp"),
        P("mp", None),
        P(),
        P(),
        P(),
        P(None, "mp"),
        P("mp"),
        P("mp", None),
        P(),
        P(),
        P(),
        token,
    )
    out_specs = (
        token,
        token,
        token,
        P(None, None, "mp"),
        P(None, "mp"),
        P("mp", None),
        P(),
        P(),
        P(),
        P(None, "mp"),
        P("mp"),
        P("mp", None),
        P(),
        P(),
        P(),
    )
    return jax.shard_map(shards, mesh=mesh, in_specs=in_specs, out_specs=out_specs, check_vma=False)
```

```python
import functools

import jax
import jax.numpy as jnp
from jax import lax
from jax.experimental import pallas as pl
from jax.experimental.pallas import tpu as pltpu
from jax.sharding import PartitionSpec as P

HD = 64
SEQ = 512
PAIR = 128
EPSILON = 1e-12
SCORE_SCALE = 0.125
GELU_COEF = 0.7978845608028654
LOG2_E = 1.4426950408889634
MASKED = -1e30
F32 = jnp.float32
BF16 = jnp.bfloat16

NT = (((1,), (1,)), ((), ()))
NN = (((1,), (0,)), ((), ()))
TN = (((0,), (0,)), ((), ()))


TILE = 256
HINT = 8.0
VMEM_LIMIT = 56 * 2**20
CORE, Y, Z1, Z2 = 1, 2, 4, 8
SLOT = {CORE: 5, Y: 6, Z1: 7, Z2: 8}


def cost(gflop, size):
    return pl.CostEstimate(
        flops=int(gflop * HINT * 1e9), bytes_accessed=int(size * HINT), transcendentals=0
    )


def dot(a, b, dims=NN):
    return lax.dot_general(a, b, dims, preferred_element_type=F32)


def attn_fwd_kernel(
    info_ref, pad_ref, x_ref, w_ref, bias_ref, qa_ref, ka_ref, qkv_ref, ctx_ref, e_ref, rinv_ref
):
    limit = SEQ - pad_ref[info_ref[4] + pl.program_id(0)]
    w = jnp.concatenate([w_ref[0], w_ref[1], w_ref[2]], axis=1)
    qkv = dot(x_ref[...], w)
    bias = bias_ref[...].astype(F32)
    q = (qkv[:, :PAIR] + bias[0:1]).astype(BF16)
    k = qkv[:, PAIR : 2 * PAIR].astype(BF16)
    v = (qkv[:, 2 * PAIR :] + bias[1:2]).astype(BF16)
    qkv_ref[0], qkv_ref[1], qkv_ref[2] = q, k, v
    v_t = v.astype(F32).T.astype(BF16)
    low = lax.broadcasted_iota(jnp.int32, (SEQ, PAIR), 1) < HD
    j = lax.broadcasted_iota(jnp.int32, (64, SEQ), 0) + (SEQ - 64)
    i = lax.broadcasted_iota(jnp.int32, (64, SEQ), 1)
    seen = (j < limit) | (j == i)
    scores, weights = [], []
    for h in range(2):
        own = low if h == 0 else ~low
        scores.append(dot(jnp.where(own, k, ka_ref[0]), jnp.where(own, q, qa_ref[0]), NT))
    for h in range(2):
        tail = jnp.where(seen, scores[h][SEQ - 64 :], MASKED)
        s = jnp.concatenate([scores[h][: SEQ - 64], tail], axis=0)
        peak = jnp.max(s, axis=0, keepdims=True)
        e = jnp.exp2((s - peak) * (SCORE_SCALE * LOG2_E))
        rinv = 1.0 / jnp.sum(e, axis=0, keepdims=True)
        eb = e.astype(BF16)
        e_ref[h] = eb
        rinv_ref[0, 0, h : h + 1, :] = rinv
        weights.append((eb, rinv))
    parts = [dot(v_t[h * HD : (h + 1) * HD], e) * rinv for h, (e, rinv) in enumerate(weights)]
    ctx_ref[...] = jnp.concatenate(parts, axis=0).T.astype(BF16)


def attn_fwd(tokens, w_qkv, bias, info, pads, q_aug, k_aug, span=None, into=None):
    rows, width = tokens.shape[0] // SEQ, w_qkv.shape[2]
    pairs, model = width // PAIR, tokens.shape[1]
    first, end = span or (0, pairs)
    aug = pl.BlockSpec((1, SEQ, PAIR), lambda r, p, *_: (r, 0, 0))
    into = list(into or ())
    kernel = attn_fwd_kernel
    if into:
        kernel = lambda *refs: attn_fwd_kernel(*refs[:7], *refs[7 + len(into) :])
    return pl.pallas_call(
        kernel,
        grid_spec=pltpu.PrefetchScalarGridSpec(
            num_scalar_prefetch=2,
            grid=(rows, end - first),
            in_specs=[
                pl.BlockSpec((SEQ, model), lambda r, p, *_: (r, 0)),
                pl.BlockSpec((3, model, PAIR), lambda r, p, *_: (0, 0, first + p)),
                pl.BlockSpec((2, PAIR), lambda r, p, *_: (0, first + p)),
                aug,
                aug,
            ]
            + [pl.BlockSpec(memory_space=pl.ANY)] * len(into),
            out_specs=[
                pl.BlockSpec((3, SEQ, PAIR), lambda r, p, *_: (0, r, first + p)),
                pl.BlockSpec((SEQ, PAIR), lambda r, p, *_: (r, first + p)),
                pl.BlockSpec((2, SEQ, SEQ), lambda r, p, *_: (r * pairs + first + p, 0, 0)),
                pl.BlockSpec((1, 1, 2, SEQ), lambda r, p, *_: (r, first + p, 0, 0)),
            ],
        ),
        out_shape=[
            pltpu.HBM((3, rows * SEQ, width), BF16),
            jax.ShapeDtypeStruct((rows * SEQ, width), BF16),
            pltpu.HBM((rows * pairs * 2, SEQ, SEQ), BF16),
            jax.ShapeDtypeStruct((rows, pairs, 2, SEQ), F32),
        ],
        input_output_aliases={7 + i: i for i in range(len(into))},
        compiler_params=pltpu.CompilerParams(vmem_limit_bytes=24 * 2**20),
        cost_estimate=cost(1e-4, 1e3),
        name="attn_fwd",
    )(info, pads, tokens, w_qkv, bias, q_aug, k_aug, *into)


def attn_bwd_kernel(
    info_ref, x_ref, ga_ref, wo_ref, qkv_ref, ctx_ref, e_ref, rinv_ref,
    out_ref, own_ref, away_ref, gb_ref, acc_ref,
):
    row, last = pl.program_id(1), pl.num_programs(1) - 1
    q, k, v = qkv_ref[0], qkv_ref[1], qkv_ref[2]
    k_t = k.astype(F32).T.astype(BF16)
    d_t = dot(wo_ref[...], ga_ref[...], NT).astype(BF16).astype(F32)
    c_t = ctx_ref[...].astype(F32).T
    lane = lax.broadcasted_iota(jnp.int32, (SEQ, PAIR), 1)
    row8 = lax.broadcasted_iota(jnp.int32, (8, SEQ), 0)
    low = lane < HD
    ones = jnp.where((lane & (HD - 1)) < 2, 1.0, 0.0).astype(BF16)
    dv, dk, dq = [], [], []
    for h in range(2):
        own = low if h == 0 else ~low
        rinv = rinv_ref[0, 0, h : h + 1, :]
        mine = d_t[h * HD : (h + 1) * HD] * rinv
        minus = -jnp.sum(mine * c_t[h * HD : (h + 1) * HD], axis=0, keepdims=True)
        high = minus.astype(BF16).astype(F32)
        extra = jnp.where(row8 == 0, high, jnp.where(row8 == 1, minus - high, 0.0))
        blank = jnp.zeros((HD - 8, SEQ), F32)
        stack = [mine, extra, blank] if h == 0 else [extra, blank, mine]
        g_t = jnp.concatenate(stack, axis=0).astype(BF16)
        v_h = jnp.where(own, v, ones)
        e = e_ref[h]
        d = e * dot(v_h, g_t).astype(BF16)
        dv.append(dot(e, g_t, NT))
        dk.append(dot(d, q))
        dq.append(dot(k_t[h * HD : (h + 1) * HD], d))
    dq_t = jnp.concatenate(dq, axis=0) * SCORE_SCALE
    dk = jnp.where(low, dk[0], dk[1]) * SCORE_SCALE
    dv = jnp.where(low, dv[0], dv[1])
    dq_b = dq_t.T.astype(BF16)
    dk_b, dv_b = dk.astype(BF16), dv.astype(BF16)
    out_ref[0], out_ref[1], out_ref[2] = dq_b, dk_b, dv_b
    left = jnp.concatenate([dq_t, dk.T, dv.T], axis=0).astype(BF16)
    g_w = dot(left, x_ref[...]).reshape(3, PAIR, x_ref.shape[1])
    g_o = dot(c_t.astype(BF16), ga_ref[...])
    g_b = jnp.concatenate(
        [
            jnp.sum(dq_b.astype(F32), axis=0, keepdims=True),
            jnp.sum(dv_b.astype(F32), axis=0, keepdims=True),
        ],
        axis=0,
    )

    @pl.when(row == 0)
    def _():
        acc_ref[:3] = g_w
        acc_ref[3] = g_o
        gb_ref[...] = g_b

    @pl.when(row > 0)
    def _():
        acc_ref[:3] += g_w
        acc_ref[3] += g_o
        gb_ref[...] += g_b

    @pl.when(row == last)
    def _():
        core = info_ref[SLOT[CORE]]
        own_ref[...] = acc_ref[pl.ds(2 * core, 2)].astype(BF16)
        away_ref[...] = acc_ref[pl.ds(2 * (1 - core), 2)].astype(BF16)


def attn_bwd(info, tokens, grad_att, w_out, qkv, ctx, e, rinv):
    rows, pairs = rinv.shape[0], rinv.shape[1]
    width, model = qkv.shape[2], tokens.shape[1]
    wide = pl.BlockSpec((SEQ, model), lambda p, r, _: (r, 0))
    triple = pl.BlockSpec((3, SEQ, PAIR), lambda p, r, _: (0, r, p))
    half = pl.BlockSpec((2, PAIR, model), lambda p, r, _: (0, p, 0))
    return pl.pallas_call(
        attn_bwd_kernel,
        grid_spec=pltpu.PrefetchScalarGridSpec(
            num_scalar_prefetch=1,
            grid=(pairs, rows),
            in_specs=[
                wide,
                wide,
                pl.BlockSpec((PAIR, model), lambda p, r, _: (p, 0)),
                triple,
                pl.BlockSpec((SEQ, PAIR), lambda p, r, _: (r, p)),
                pl.BlockSpec((2, SEQ, SEQ), lambda p, r, _: (r * pairs + p, 0, 0)),
                pl.BlockSpec((1, 1, 2, SEQ), lambda p, r, _: (r, p, 0, 0)),
            ],
            out_specs=[
                triple,
                half,
                half,
                pl.BlockSpec((2, PAIR), lambda p, r, _: (0, p)),
            ],
            scratch_shapes=[pltpu.VMEM((4, PAIR, model), F32)],
        ),
        out_shape=[
            pltpu.HBM((3, rows * SEQ, width), BF16),
            pltpu.HBM((2, width, model), BF16),
            pltpu.HBM((2, width, model), BF16),
            jax.ShapeDtypeStruct((2, width), F32),
        ],
        compiler_params=pltpu.CompilerParams(vmem_limit_bytes=24 * 2**20),
        cost_estimate=cost(8 * rows, rows * pairs * 2 * SEQ * SEQ * 2),
        name="attn_bwd",
    )(info, tokens, grad_att, w_out, qkv, ctx, pltpu.with_memory_space_constraint(e, pltpu.HBM), rinv)


def vector(x):
    return pl.BlockSpec(x.shape, lambda *_: (0,) * x.ndim)


def normalise(v):
    centered = v - jnp.mean(v, axis=-1, keepdims=True)
    rstd = lax.rsqrt(jnp.mean(centered * centered, axis=-1, keepdims=True) + EPSILON)
    return centered * rstd, rstd


def normalise_back(dy, xhat, rstd, gain):
    dg = dy * gain
    return rstd * (
        dg
        - jnp.mean(dg, axis=-1, keepdims=True)
        - xhat * jnp.mean(dg * xhat, axis=-1, keepdims=True)
    )


def gelu_and_slope(u):
    u2 = u * u
    t = jnp.tanh(u * (GELU_COEF + (GELU_COEF * 0.044715) * u2))
    half = 0.5 + 0.5 * t
    act = u * half
    slope = half * (1.0 + u * (1.0 - t) * (GELU_COEF + (3 * GELU_COEF * 0.044715) * u2))
    return act, slope


def flat_bias(ref):
    b = ref[...].astype(F32)
    return jnp.concatenate([b[i : i + 1] for i in range(b.shape[0])], axis=1)


def by_core(core, x, ref):
    half = x.shape[1] // 2
    ref[core] = x[:, :half]
    ref[1 - core] = x[:, half:]


def units(core, mid, acc, wu_ref, ub_ref, wd_ref, act_ref, slope_ref):
    act, slope = gelu_and_slope(dot(mid, wu_ref[...]) + flat_bias(ub_ref))
    act = act.astype(BF16)
    by_core(core, act, act_ref)
    slope_ref[...] = slope.astype(BF16)
    return acc + dot(act, wd_ref[...])


def ffn_front_kernel(
    info_ref, cm_ref, co_ref, x_ref, wm_ref, wo_ref, vec_ref, wu_ref, ub_ref, wd_ref,
    mid_ref, xhat_ref, rstd_ref, part_ref, act_ref, slope_ref,
):
    vec = vec_ref[...].astype(F32)
    attended = dot(cm_ref[...], wm_ref[...]) + dot(co_ref[...], wo_ref[...])
    resid = x_ref[...].astype(F32) + (attended + vec[0:1])
    xhat, rstd = normalise(resid)
    normed = xhat * vec[1:2] + vec[2:3]
    mid = normed.astype(BF16)
    mid_ref[...] = mid
    xhat_ref[...] = xhat
    rstd_ref[...] = rstd
    part_ref[...] = units(
        info_ref[SLOT[CORE]], mid, normed + vec[3:4], wu_ref, ub_ref, wd_ref,
        act_ref, slope_ref,
    )


def halves(hidden, n=None):
    if n is None:
        return pl.BlockSpec((2, TILE, hidden // 2), lambda t, *_: (0, t, 0))
    return jax.ShapeDtypeStruct((2, n, hidden // 2), BF16)


def ffn_front(info, ctx, tokens, w_outs, vectors, w_up, up_bias, w_down):
    n, model = tokens.shape
    width, hidden = ctx[0].shape[1], w_up.shape[1]
    row = lambda c: pl.BlockSpec((TILE, c), lambda t, *_: (t, 0))
    shape = lambda c, d: jax.ShapeDtypeStruct((n, c), d)
    fixed = [vectors, w_up, up_bias, w_down]
    outs = [(model, BF16), (model, F32), (1, F32), (model, F32)]
    return pl.pallas_call(
        ffn_front_kernel,
        grid_spec=pltpu.PrefetchScalarGridSpec(
            num_scalar_prefetch=1,
            grid=(n // TILE,),
            in_specs=[row(width), row(width), row(model)] + [vector(a) for a in (*w_outs, *fixed)],
            out_specs=[row(c) for c, _ in outs] + [halves(hidden), row(hidden)],
        ),
        out_shape=[shape(*o) for o in outs] + [halves(hidden, n), shape(hidden, BF16)],
        compiler_params=pltpu.CompilerParams(vmem_limit_bytes=48 * 2**20),
        cost_estimate=cost(10, n * model * 24),
        name="ffn_front",
    )(info, *ctx, tokens, *w_outs, *fixed)


def ffn_back_kernel(
    info_ref, pad_ref, mid_ref, xhat_ref, rstd_ref, part_ref, slope_m_ref, cot_ref,
    wu_m_ref, wd_m_ref, wu_o_ref, ub_o_ref, wd_o_ref, vec_ref,
    out_ref, pool_ref, act_ref, branch_ref, um_ref, uo_ref, resid_ref, att_ref, sums_ref, ub_m_sum_ref, ub_o_sum_ref, slope_ref,
):
    t = pl.program_id(0)
    per_row = SEQ // TILE
    mid = mid_ref[...]
    core = info_ref[SLOT[CORE]]
    second = units(
        core, mid, part_ref[...], wu_o_ref, ub_o_ref, wd_o_ref, act_ref, slope_ref
    )
    vec = vec_ref[...].astype(F32)
    gain_two = vec[4:5]
    xhat_two, rstd_two = normalise(second)
    final = xhat_two * gain_two + vec[5:6]
    out_ref[...] = final.astype(BF16)
    count = SEQ - pad_ref[info_ref[4] + t // per_row]
    slot = lax.broadcasted_iota(jnp.int32, (TILE, 1), 0) + (t % per_row) * TILE
    pooled = jnp.sum(jnp.where(slot < count, final, 0.0), axis=0, keepdims=True)
    pooled = pooled / count.astype(F32)
    which = lax.broadcasted_iota(jnp.int32, pool_ref.shape, 0) == t // per_row
    pooled = jnp.where(which, pooled, 0.0)

    dy = cot_ref[...].astype(F32)
    down = lambda v: jnp.sum(v, axis=0, keepdims=True)
    sums = [down(dy * xhat_two), down(dy)]
    second_grad = normalise_back(dy, xhat_two, rstd_two, gain_two)
    branch = second_grad.astype(BF16)
    branch_ref[...] = branch
    sums.append(down(branch.astype(F32)))
    normed_grad = second_grad
    bias_sums = []
    for wu_ref, wd_ref, s_ref, up_ref in (
        (wu_o_ref, wd_o_ref, slope_ref, uo_ref),
        (wu_m_ref, wd_m_ref, slope_m_ref, um_ref),
    ):
        upper = (dot(branch, wd_ref[...], NT) * s_ref[...].astype(F32)).astype(BF16)
        by_core(core, upper, up_ref)
        bias_sums.append(down(upper.astype(F32)))
        normed_grad = normed_grad + dot(upper, wu_ref[...], NT)
    xhat_one = xhat_ref[...]
    sums += [down(normed_grad * xhat_one), down(normed_grad)]
    resid = normalise_back(normed_grad, xhat_one, rstd_ref[...], vec[1:2])
    resid_ref[...] = resid
    att = resid.astype(BF16)
    att_ref[...] = att
    sums.append(down(att.astype(F32)))
    sums = jnp.concatenate(sums, axis=0)

    @pl.when(t == 0)
    def _():
        pool_ref[...] = pooled
        sums_ref[...] = sums
        ub_o_sum_ref[...] = bias_sums[0]
        ub_m_sum_ref[...] = bias_sums[1]

    @pl.when(t > 0)
    def _():
        pool_ref[...] += pooled
        sums_ref[...] += sums
        ub_o_sum_ref[...] += bias_sums[0]
        ub_m_sum_ref[...] += bias_sums[1]


def ffn_back(info, pads, mid, xhat, rstd, part, slope, cot, w_ups, w_downs, up_bias_o, vectors):
    n, model = mid.shape
    hidden, rows = slope.shape[1], n // SEQ
    row = lambda c: pl.BlockSpec((TILE, c), lambda t, *_: (t, 0))
    keep = lambda r, c: pl.BlockSpec((r, c), lambda t, *_: (0, 0))
    shape = lambda c, d: jax.ShapeDtypeStruct((n, c), d)
    fixed = [w_ups[0], w_downs[0], w_ups[1], up_bias_o, w_downs[1], vectors]
    return pl.pallas_call(
        ffn_back_kernel,
        grid_spec=pltpu.PrefetchScalarGridSpec(
            num_scalar_prefetch=2,
            grid=(n // TILE,),
            in_specs=[row(model), row(model), row(1), row(model), row(hidden), row(model)]
            + [vector(a) for a in fixed],
            out_specs=[row(model), keep(rows, model), halves(hidden), row(model)]
            + [halves(hidden)] * 2
            + [row(model), row(model), keep(6, model), keep(1, hidden), keep(1, hidden)],
            scratch_shapes=[pltpu.VMEM((TILE, hidden), BF16)],
        ),
        out_shape=[
            shape(model, BF16),
            jax.ShapeDtypeStruct((rows, model), F32),
            halves(hidden, n),
            shape(model, BF16),
        ]
        + [halves(hidden, n)] * 2
        + [
            shape(model, F32),
            shape(model, BF16),
            jax.ShapeDtypeStruct((6, model), F32),
            jax.ShapeDtypeStruct((1, hidden), F32),
            jax.ShapeDtypeStruct((1, hidden), F32),
        ],
        compiler_params=pltpu.CompilerParams(vmem_limit_bytes=40 * 2**20),
        cost_estimate=cost(25, n * model * 40),
        name="ffn_back",
    )(info, pads, mid, xhat, rstd, part, slope, cot, *fixed)


def pack_attn_kernel(info_ref, wq_ref, wo_ref, qb_ref, attn_ref):
    r, w = wq_ref.shape[1:]
    attn_ref[:r, :w] = wq_ref[0]
    attn_ref[:r, w:] = wq_ref[1]
    attn_ref[r : r + r // 2, :w] = wq_ref[2, : r // 2]
    attn_ref[r : r + r // 2, w:] = wq_ref[2, r // 2 :]
    at = r + r // 2
    attn_ref[at : at + wo_ref.shape[0], :] = wo_ref[...]
    at += wo_ref.shape[0]
    attn_ref[at:, :] = jnp.zeros((16, 2 * w), BF16)
    attn_ref[at : at + 2, :w] = qb_ref[...]


def pack_ffn_kernel(info_ref, seg_ref, wu_ref, wd_ref, ub_ref, up_ref, down_ref, qa_ref, ka_ref):
    u, c = wu_ref.shape[0], up_ref.shape[1]
    up_ref[:u, :] = wu_ref[:, :c]
    up_ref[u : 2 * u, :] = wu_ref[:, c:]
    up_ref[2 * u :, :] = jnp.zeros((16, c), BF16)
    up_ref[2 * u : 2 * u + 2, :] = ub_ref[...]
    down_ref[...] = wd_ref[...]
    segs = seg_ref.shape[1]
    slot = lax.broadcasted_iota(jnp.int32, (SEQ, PAIR), 0)
    lane = lax.broadcasted_iota(jnp.int32, (SEQ, PAIR), 1) & (HD - 1)
    for row in range(qa_ref.shape[0]):
        end, segment = 0, jnp.zeros((SEQ, PAIR), jnp.int32)
        for s in range(segs):
            end = end + seg_ref[info_ref[4] + row, s]
            segment = segment + jnp.where(slot >= end, 1, 0)
        same = lane == segment
        ka_ref[row] = jnp.where(same & (lane < segs), 1.0, 0.0).astype(BF16)
        qa_ref[row] = jnp.where((lane < segs) & ~same, MASKED, 0.0).astype(BF16)


def pack_attn(info, w_qkv, w_out, qv_bias):
    model, width = w_qkv.shape[1:]
    out_rows = w_out.shape[0] // 4
    shape = (3 * width // 4 + out_rows + 16, model)
    whole = lambda s: pl.BlockSpec(s, lambda i, *_: (0,) * len(s))
    return pl.pallas_call(
        pack_attn_kernel,
        grid_spec=pltpu.PrefetchScalarGridSpec(
            num_scalar_prefetch=1,
            grid=(1,),
            in_specs=[
                pl.BlockSpec((3, model // 4, width), lambda i, at: (0, at[0], 0)),
                pl.BlockSpec((out_rows, model), lambda i, at: (at[0], 0)),
                whole(qv_bias.shape),
            ],
            out_specs=whole(shape),
        ),
        out_shape=jax.ShapeDtypeStruct(shape, BF16),
        cost_estimate=cost(0, 2 * 2**20),
        name="pack_attn",
    )(info, w_qkv, w_out, qv_bias)


def pack_ffn(info, rows, seg_lengths, w_up, w_down, up_bias):
    model = w_up.shape[0]
    up_rows, down_rows = model // 4, w_down.shape[0] // 4
    whole = lambda s: pl.BlockSpec(s, lambda i, *_: (0,) * len(s))
    shapes = [(2 * up_rows + 16, model), (down_rows, model)] + [(rows, SEQ, PAIR)] * 2
    return pl.pallas_call(
        pack_ffn_kernel,
        grid_spec=pltpu.PrefetchScalarGridSpec(
            num_scalar_prefetch=2,
            grid=(1,),
            in_specs=[
                pl.BlockSpec((up_rows, w_up.shape[1]), lambda i, at, _: (at[0], 0)),
                pl.BlockSpec((down_rows, model), lambda i, at, _: (at[9], 0)),
                whole(up_bias.shape),
            ],
            out_specs=[whole(s) for s in shapes],
        ),
        out_shape=[jax.ShapeDtypeStruct(s, BF16) for s in shapes],
        cost_estimate=cost(0, 4 * 2**20),
        name="pack_ffn",
    )(info, seg_lengths, w_up, w_down, up_bias)


def unpack_attn_kernel(at_ref, *refs):
    pieces, (wq_ref, wo_ref, qb_ref) = refs[:4], refs[4:]
    r, w, o = wq_ref.shape[1] // 4, wq_ref.shape[2], wo_ref.shape[0] // 4
    for i, piece in enumerate(pieces):
        q = at_ref[i]
        rows = pl.ds(pl.multiple_of(q * r, 16), r)
        wq_ref[0, rows, :] = piece[:r, :w]
        wq_ref[1, rows, :] = piece[:r, w:]
        wq_ref[2, pl.ds(pl.multiple_of(q * r, 16), r // 2), :] = piece[r : r + r // 2, :w]
        wq_ref[2, pl.ds(pl.multiple_of(q * r + r // 2, 16), r // 2), :] = piece[r : r + r // 2, w:]
        at = r + r // 2
        wo_ref[pl.ds(pl.multiple_of(q * o, 16), o), :] = piece[at : at + o, :]
    at += o
    qb_ref[...] = pieces[0][at : at + 2, :w]


def unpack_ffn_kernel(at_ref, *refs):
    ups, downs, (wu_ref, wd_ref, ub_ref) = refs[:4], refs[4:8], refs[8:]
    r, c, d = wu_ref.shape[0] // 4, wu_ref.shape[1] // 2, wd_ref.shape[0] // 4
    for i in range(4):
        rows = pl.ds(pl.multiple_of(at_ref[i] * r, 16), r)
        wu_ref[rows, :c] = ups[i][:r, :]
        wu_ref[rows, c:] = ups[i][r : 2 * r, :]
        wd_ref[pl.ds(pl.multiple_of(at_ref[9 + i] * d, 16), d), :] = downs[i][...]
    ub_ref[...] = ups[0][2 * r : 2 * r + 2, :]


def unpack(kernel, at, pieces, like):
    whole = pl.BlockSpec(memory_space=pltpu.VMEM)
    return pl.pallas_call(
        kernel,
        in_specs=[pl.BlockSpec(memory_space=pltpu.SMEM)] + [whole] * len(pieces),
        out_specs=[whole] * len(like),
        out_shape=[jax.ShapeDtypeStruct(a.shape, BF16) for a in like],
        compiler_params=pltpu.CompilerParams(vmem_limit_bytes=32 * 2**20),
        cost_estimate=cost(0, 5 * 2**20),
        name=kernel.__name__,
    )(at, *pieces)


def over_mp(x):
    n = lax.axis_size("mp")
    return lax.ppermute(x, "mp", [(i, i ^ 1) for i in range(n)])


def over_dp(x, bit):
    n = lax.axis_size("dp")
    return lax.ppermute(x, "dp", [(i, i ^ bit) for i in range(n)])


def gather_pieces(rows, at_ref, refs, store):
    k = 0
    for ref in refs:
        for i in range(ref.shape[0] // rows):
            spot = pl.ds(pl.multiple_of(at_ref[k] * rows, 16), rows)
            store(spot, ref[i * rows : (i + 1) * rows, :].astype(F32))
            k += 1


def place_kernel(rows, at_ref, *refs):
    out_ref = refs[-1]

    def store(spot, value):
        out_ref[spot, :] = value

    gather_pieces(rows, at_ref, refs[:-1], store)


def place_up_kernel(rows, at_ref, *refs):
    out_ref = refs[-1]
    height, width = out_ref.shape[0], out_ref.shape[1] // 2
    k = 0
    for ref in refs[:-1]:
        for i in range(ref.shape[0] // rows):
            place, count = at_ref[k], height // rows
            spot = pl.ds(pl.multiple_of(place % count * rows, 16), rows)
            columns = pl.ds(pl.multiple_of(place // count * width, 128), width)
            out_ref[spot, columns] = ref[i * rows : (i + 1) * rows, :].astype(F32)
            k += 1


def place_attn_kernel(rows, at_ref, *refs):
    qkv_ref, out_ref, held_ref = refs[-3:]

    def store(spot, value):
        held_ref[spot, :] = value

    gather_pieces(rows, at_ref, refs[:-3], store)
    width = qkv_ref.shape[2]
    for c in range(3):
        for e in range(0, width, PAIR):
            qkv_ref[c, :, e : e + PAIR] = held_ref[c * width + e : c * width + e + PAIR, :].T
    out_ref[...] = held_ref[3 * width :, :]


def place(kernel, pieces, at, *shapes):
    total, cols = sum(piece.shape[0] for piece in pieces), pieces[0].shape[1]
    whole = pl.BlockSpec(memory_space=pltpu.VMEM)
    return pl.pallas_call(
        functools.partial(kernel, total // at.shape[0]),
        in_specs=[pl.BlockSpec(memory_space=pltpu.SMEM)] + [whole] * len(pieces),
        out_specs=[whole] * len(shapes),
        out_shape=[jax.ShapeDtypeStruct(s, F32) for s in shapes],
        scratch_shapes=[] if len(shapes) == 1 else [pltpu.VMEM((total, cols), F32)],
        compiler_params=pltpu.CompilerParams(vmem_limit_bytes=32 * 2**20),
        cost_estimate=cost(0, 6 * total * cols),
        name=kernel.__name__,
    )(at, *pieces)


def tie(x, *after):
    return lax.optimization_barrier((x,) + after)[0]


def land(info, x, got, own=None, step=None):
    n = got.shape[0]
    if own is not None:
        x = lax.dynamic_slice_in_dim(x, info[own] * n, n, 0)
    total = (x.astype(F32) + got.astype(F32)).astype(BF16)
    if step is None:
        return total
    return total, lax.dynamic_slice_in_dim(total, (1 - info[step]) * (n // 2), n // 2, 0)


def arrive(after, *flights):
    held = [c.crossed if part == "x" else c.got[part] for c, part in flights]
    held = lax.optimization_barrier((*held, after))
    for (c, part), got in zip(flights, held):
        if part == "x":
            c.crossed = got
        else:
            c.got[part] = got


class Chain:
    def __init__(self, info, bits):
        self.info, self.bits = info, bits
        self.dp_bits = [b for b in bits if b != "x"]
        self.order = [0]
        for b in reversed(self.dp_bits):
            self.order += [o ^ b for o in self.order]
        self.x, self.got, self.own, self.at = {}, {}, {}, {}
        self.held, self.back = None, list(reversed(self.dp_bits))

    def send(self, part, own, away):
        self.got[part] = over_dp(away, self.bits[0])
        self.x[part], self.own[part], self.at[part] = own, None, 0

    def hop(self, part="m", *after):
        if self.held is not None:
            return self.double(*after)
        x, at = tie(self.x[part], *after), self.at[part]
        got = self.crossed if self.bits[at] == "x" else self.got[part]
        bit = self.bits[at + 1] if at + 1 < len(self.bits) else None
        self.at[part] = at + 1
        if bit is None or bit == "x":
            x = land(self.info, x, got, self.own[part])
            self.x[part], self.own[part] = x, None
            if bit is None:
                bit = 2 * max(self.dp_bits)
                while bit < lax.axis_size("dp"):
                    x = land(self.info, x, over_dp(x, bit))
                    bit *= 2
                self.held = [x]
                self.double()
            elif part == "o":
                self.crossed = over_mp(x)
            return x
        x, away = land(self.info, x, got, self.own[part], SLOT[bit])
        self.x[part], self.own[part], self.got[part] = x, SLOT[bit], over_dp(away, bit)
        return x

    def double(self, *after):
        full = jnp.concatenate(self.held, axis=0) if len(self.held) > 1 else self.held[0]
        full = tie(full, *after)
        self.held.append(over_dp(full, self.back.pop(0)))
        return full

    def spots(self, me):
        who = me ^ jnp.array(self.order, jnp.int32)
        spot = jnp.zeros_like(who)
        for b in self.dp_bits:
            spot = 2 * spot + (who & b) // b
        return spot


def pack_small_kernel(sums_ref, um_ref, uo_ref, qm_ref, qo_ref, keep_ref, send_ref):
    n, c, w = sums_ref.shape[0], sums_ref.shape[1], qm_ref.shape[1]
    for out_ref, u_ref, q_ref in ((keep_ref, um_ref, qm_ref), (send_ref, uo_ref, qo_ref)):
        out_ref[...] = jnp.zeros(out_ref.shape, F32)
        out_ref[:n, :] = sums_ref[...]
        for i in range(u_ref.shape[1] // c):
            out_ref[n + i : n + i + 1, :] = u_ref[:, i * c : (i + 1) * c]
        at = n + u_ref.shape[1] // c
        for i in range(2):
            out_ref[at : at + 1, i * w : (i + 1) * w] = q_ref[i : i + 1, :]


def pack_small(sums, up_sums, qv_sums):
    shape = jax.ShapeDtypeStruct((16, sums.shape[1]), F32)
    return pl.pallas_call(
        pack_small_kernel, out_shape=[shape, shape], cost_estimate=cost(0, 2**18), name="pack_small"
    )(sums, *up_sums, *qv_sums)


def shards(
    tokens_in,
    seg_lengths,
    pad_counts,
    w_qkv,
    qv_bias,
    w_out,
    out_bias,
    norm1_gain,
    norm1_bias,
    w_up,
    up_bias,
    w_down,
    down_bias,
    norm2_gain,
    norm2_bias,
    cotangent,
):
    tokens, width = tokens_in.shape
    local = w_qkv.shape[2]
    me = lax.axis_index("dp")
    rows_here = tokens // SEQ
    slot = jnp.arange(13, dtype=jnp.int32)
    start = lax.axis_index("mp") * rows_here
    quarters = jnp.array([0, 2, 1, 3, 0, 0, 0, 0, 0, 0, 2, 1, 3], jnp.int32)
    quarters = quarters ^ jnp.where(slot < 4, me & 3, (me & CORE) | ((me & Z1) // 2))
    bits = jnp.where(slot == 4, start, (me >> jnp.clip(slot - 5, 0, 3)) & 1)
    info = jnp.where((slot < 4) | (slot > 8), quarters, bits)
    vectors = jnp.stack([out_bias, norm1_gain, norm1_bias, down_bias, norm2_gain, norm2_bias])
    up_bias = up_bias.reshape(-1, width)

    attn_w = pack_attn(info, w_qkv, w_out, qv_bias)
    up_w, down_w, q_aug, k_aug = pack_ffn(
        info, rows_here, seg_lengths, w_up, w_down, tie(up_bias, attn_w)
    )
    attn_w, up_w, down_w = over_mp(attn_w), over_mp(up_w), over_mp(down_w)
    early = local // PAIR - 1
    attn_args = (info, pad_counts, q_aug, k_aug)
    fwd_m = attn_fwd(tokens_in, w_qkv, qv_bias, *attn_args, span=(0, early))
    attn_w = tie(attn_w, fwd_m[1])
    attn_y, attn_core = over_dp(attn_w, Y), over_dp(attn_w, CORE)
    bias_m = tie(qv_bias, attn_w)
    fwd_m = attn_fwd(
        tokens_in, w_qkv, bias_m, *attn_args, span=(early, local // PAIR), into=fwd_m
    )
    up_w = tie(up_w, fwd_m[1])
    up_y = over_dp(up_w, Y)
    attn_core = tie(attn_core, up_w)
    attn_y = tie(attn_y, attn_core)
    w_qkv_o, w_out_o, qv_bias_o = unpack(
        unpack_attn_kernel,
        info,
        (attn_w, attn_y, attn_core, over_dp(attn_y, CORE)),
        (w_qkv, w_out, qv_bias),
    )
    w_qkvs, w_outs = (w_qkv, w_qkv_o), (w_out, w_out_o)
    fwd_o = attn_fwd(tokens_in, w_qkv_o, qv_bias_o, *attn_args)
    qkv, ctx, probs, rinv = zip(fwd_m, fwd_o)
    down_w, up_y, up_w = lax.optimization_barrier((down_w, up_y, up_w, ctx[1]))[:3]
    down_z = over_dp(down_w, Z1)
    up_core, up_both, down_core = over_dp(up_w, CORE), over_dp(up_y, CORE), over_dp(down_w, CORE)
    mid, xhat, rstd, part, act_m, slope_m = ffn_front(
        info, (ctx[0], tie(ctx[1], down_w)), tokens_in, w_outs, vectors, w_up, up_bias, w_down
    )
    down_z, up_core, up_both, down_core = lax.optimization_barrier(
        (down_z, up_core, up_both, down_core, mid)
    )[:4]
    w_up_o, w_down_o, up_bias_o = unpack(
        unpack_ffn_kernel,
        info,
        (up_w, up_y, up_core, up_both, down_w, down_z, down_core, over_dp(down_z, CORE)),
        (w_up, w_down, up_bias),
    )
    (
        tokens_out, pooled, act_o, grad_branch, upper_m, upper_o, grad_resid, grad_attended,
        sums, up_sum_m, up_sum_o,
    ) = ffn_back(
        info, pad_counts, mid, xhat, rstd, part, slope_m, cotangent, (w_up, w_up_o),
        (w_down, w_down_o), up_bias_o, vectors,
    )

    down = Chain(info, [CORE, "x", Z1, Y, Z2])
    up = Chain(info, [CORE, "x", Z1, Y, Z2])
    attn = Chain(info, [CORE, Y, "x", Z1, Z2])

    def attn_back(h, *after):
        g_att = tie(grad_attended, *after)
        dx, own, away, qv = attn_bwd(
            info, tokens_in, g_att, w_outs[h], qkv[h], ctx[h], probs[h], rinv[h]
        )
        return dx, own.reshape(-1, width), away.reshape(-1, width), qv

    def weight_grad(a, b, *after):
        return dot(tie(a, *after), b, TN).astype(BF16)

    def input_grad(h, grad_act, *after):
        return jnp.einsum(
            "cte,cde->td", tie(grad_act, *after), w_qkvs[h], preferred_element_type=F32
        )

    away = weight_grad(act_o[1], grad_branch)
    own = weight_grad(act_o[0], grad_branch, away)
    down.send("o", own, away)
    away = weight_grad(act_m[1], grad_branch, own)
    last = down.hop("o", away)
    own = weight_grad(act_m[0], grad_branch, last)
    down.send("m", own, away)
    away = weight_grad(mid, upper_o[1], own)
    own = weight_grad(mid, upper_o[0], away)
    up.send("o", own, away)
    last = down.hop("m", own)
    away = weight_grad(mid, upper_m[1], last)
    last = up.hop("o", away)
    own = weight_grad(mid, upper_m[0], last)
    up.send("m", own, away)
    dx_o, own, away, qv_o = attn_back(1, own)
    attn.send("o", own, away)
    last = up.hop("m", own)
    last = down.hop("m", last)
    last = attn.hop("o", last)
    dx_m, own, away, qv_m = attn_back(0, last)
    attn.send("m", own, away)
    small, small_send = pack_small(sums, (up_sum_m, up_sum_o), (qv_m, qv_o))
    last = down.hop("m", small)
    last = attn.hop("o", last)
    last = up.hop("m", last)
    last = attn.hop("m", last)
    small_got = over_mp(tie(small_send, last))
    count, bit = lax.axis_size("dp"), 1
    for what in "dsuadaudsaudasudsaugapsua":
        if what == "s":
            last = small = tie(small, last) + small_got
            if bit < count:
                small_got = over_dp(small, bit)
                bit *= 2
        elif what == "g":
            total = input_grad(1, dx_o, last) + grad_resid
            total = total + input_grad(0, dx_m, last)
            grad_input = last = total.astype(BF16)
        elif what == "p":
            down.held[0] = tie(down.held[0], last)
            (grad_down,) = place(place_kernel, down.held, down.spots(me), w_down.shape)
            last = grad_down
            up.held[-1] = tie(up.held[-1], last)
            attn.held[-1] = tie(attn.held[-1], last)
        else:
            last = {"d": down, "u": up, "a": attn}[what].hop("m", last)
    if bit > 16:
        small = small + small_got
    while bit < count:
        small = small + over_dp(small, bit)
        bit *= 2
    (grad_up,) = place(place_up_kernel, up.held, up.spots(me), w_up.shape)
    grad_qkv, grad_out = place(
        place_attn_kernel, attn.held, attn.spots(me), w_qkv.shape, w_out.shape
    )
    vectors = [small[i] for i in (5, 3, 4, 2, 0, 1)]
    grad_up_bias = small[6:8].reshape(-1)
    grad_qv_bias = small[8].reshape(2, local)
    return (
        tokens_out,
        pooled,
        grad_input,
        grad_qkv,
        grad_qv_bias,
        grad_out,
        vectors[0],
        vectors[1],
        vectors[2],
        grad_up,
        grad_up_bias,
        grad_down,
        vectors[3],
        vectors[4],
        vectors[5],
    )


def solution(mesh):
    token = P(("dp", "mp"), None)
    in_specs = (
        token,
        P("dp", None),
        P("dp"),
        P(None, None, "mp"),
        P(None, "mp"),
        P("mp", None),
        P(),
        P(),
        P(),
        P(None, "mp"),
        P("mp"),
        P("mp", None),
        P(),
        P(),
        P(),
        token,
    )
    out_specs = (
        token,
        token,
        token,
        P(None, None, "mp"),
        P(None, "mp"),
        P("mp", None),
        P(),
        P(),
        P(),
        P(None, "mp"),
        P("mp"),
        P("mp", None),
        P(),
        P(),
        P(),
    )
    return jax.shard_map(shards, mesh=mesh, in_specs=in_specs, out_specs=out_specs, check_vma=False)
```
